32 devices in a mesh: dp: 8 (over z, core), seq: 4 (over y, x).
Axes of the slice: x: 2, y: 2, z: 4, core: 2. Of those that a mesh axis runs over, the one named last changes fastest.
Arguments:
- inputs: float32 [2, 8, 1024, 960], P(None, 'dp', 'seq'), may hold values from -6 to 6
- cotangent: float32 [2, 8, 1024, 960], P(None, 'dp', 'seq'), may hold values from -6 to 6
- segments: int32 [2, 8, 1024], P(None, 'dp', 'seq'), may hold values from 0 to 2, as said below
- depths: int32 [2, 8, 1024], P(None, 'dp', 'seq'), may hold values from 1 to 3
- query_weight: bfloat16 [960, 960], P('dp', 'seq'), may hold values from -0.1875 to 0.1875
- key_weight: bfloat16 [960, 320], P('dp', 'seq'), may hold values from -0.1875 to 0.1875
- value_weight: bfloat16 [960, 320], P('dp', 'seq'), may hold values from -0.1875 to 0.1875
- out_weight: bfloat16 [960, 960], P('dp', 'seq'), may hold values from -0.75 to 0.75
- gate_weight: bfloat16 [960, 2560], P('dp', 'seq'), may hold values from -0.1875 to 0.1875
- up_weight: bfloat16 [960, 2560], P('dp', 'seq'), may hold values from -0.1875 to 0.1875
- down_weight: bfloat16 [2560, 960], P('dp', 'seq'), may hold values from -0.125 to 0.125
- attn_gain: bfloat16 [960], P('dp'), may hold values from 0.25 to 1.75
- ffn_gain: bfloat16 [960], P('dp'), may hold values from 0.25 to 1.75
- router_weight: bfloat16 [960, 3], P('dp'), may hold values from -0.1875 to 0.1875
Outputs:
- outputs: float32 [2, 8, 1024, 960], P(None, 'dp', 'seq')
- input_grad: float32 [2, 8, 1024, 960], P(None, 'dp', 'seq')
- query_grad: float32 [960, 960], P('dp', 'seq')
- key_grad: float32 [960, 320], P('dp', 'seq')
- value_grad: float32 [960, 320], P('dp', 'seq')
- out_grad: float32 [960, 960], P('dp', 'seq')
- gate_grad: float32 [960, 2560], P('dp', 'seq')
- up_grad: float32 [960, 2560], P('dp', 'seq')
- down_grad: float32 [2560, 960], P('dp', 'seq')
- attn_gain_grad: float32 [960], P('dp')
- ffn_gain_grad: float32 [960], P('dp')
- router_grad: float32 [960, 3], P('dp')
The draws below stay inside these ranges and needn't reach their ends.
Inputs may be any that keep to these rules, and one draw needn't show every extreme that they name: `segments`: segment numbers never fall along a pack.
All inputs are finite; a program needn't handle non-finite values.
Results may differ from the reference program's by a relative error of at most 0.028.
Values may be sent and summed in bfloat16 or wider, within the bound.
A program may use at most 384 MiB of HBM per device.

```python
import jax
import jax.numpy as jnp
from jax import lax

D = 960
FF = 2560
HEADS = 15
KV_HEADS = 5
HEAD_DIM = 64
QW = 960
KW = 320
RECUR = 3
MICRO = 2
LEN = 1024
TOK = 256
PACKS = 8


def draw_segments(key, part):
    key = jax.random.fold_in(key, 7)
    start_key, end_key = jax.random.split(key)
    starts = jax.random.randint(start_key, (MICRO, PACKS, 1), 1, TOK)
    endings = jax.random.randint(end_key, (MICRO, PACKS, 1), LEN - TOK + 1, LEN)
    places = jnp.arange(LEN, dtype=jnp.int32)[None, None, :]
    return (places >= starts).astype(jnp.int32) + (places >= endings).astype(jnp.int32)


def set_ends(entries, own_key, low, high):
    extent = entries.shape
    spot = [jax.random.randint(jax.random.fold_in(own_key, axis), (), 0, extent[axis]) for axis in range(len(extent))]
    entries = entries.at[tuple(spot)].set(low)
    longest = extent.index(max(extent))
    spot[longest] = (spot[longest] + 1) % extent[longest]
    return entries.at[tuple(spot)].set(high)


def levels(key, extent, cuts, smallest, top_value):
    factor_of = 1.0
    for position, shards_of in cuts:
        steps = jax.random.uniform(jax.random.fold_in(jax.random.fold_in(key, 6), position), (shards_of,), jnp.float32, smallest / len(cuts), top_value / len(cuts))
        factor_of = factor_of * jnp.repeat(jnp.exp(steps), extent[position] // shards_of).reshape((-1,) + (1,) * (len(extent) - 1 - position))
    return factor_of


def bell_draw(rng, extent, spread, bound, cuts=(), held_as=jnp.bfloat16):
    factor_of = levels(rng, extent, cuts, -0.22, 0.18) if cuts else 1.0
    array = jax.random.normal(rng, extent, jnp.float32) * spread * factor_of
    return jnp.minimum(jnp.maximum(array, -bound), bound).astype(held_as)


def setup_inputs(seed: int = 0) -> dict:
    splits = jax.random.split(jax.random.key(seed), 15)
    return {
        "inputs": bell_draw(splits[0], (MICRO, PACKS, LEN, D), 1.0, 6.0, ((1, 8), (2, 4)), jnp.float32),
        "cotangent": bell_draw(splits[1], (MICRO, PACKS, LEN, D), 1.0, 6.0, ((1, 8), (2, 4)), jnp.float32),
        "segments": draw_segments(jax.random.fold_in(splits[14], 71), 0),
        "depths": set_ends(jax.random.randint(splits[3], (MICRO, PACKS, LEN), 1, RECUR + 1), jax.random.fold_in(splits[3], 1), 1, RECUR).astype(jnp.int32),
        "query_weight": bell_draw(splits[4], (D, QW), D ** -0.5, 0.1875, ((0, 8), (1, 4))),
        "key_weight": bell_draw(splits[5], (D, KW), D ** -0.5, 0.1875, ((0, 8), (1, 4))),
        "value_weight": bell_draw(splits[6], (D, KW), D ** -0.5, 0.1875, ((0, 8), (1, 4))),
        "out_weight": bell_draw(splits[7], (QW, D), (QW // 16) ** -0.5, 0.75, ((0, 8), (1, 4))),
        "gate_weight": bell_draw(splits[8], (D, FF), D ** -0.5, 0.1875, ((0, 8), (1, 4))),
        "up_weight": bell_draw(splits[9], (D, FF), D ** -0.5, 0.1875, ((0, 8), (1, 4))),
        "down_weight": bell_draw(splits[10], (FF, D), FF ** -0.5, 0.125, ((0, 8), (1, 4))),
        "attn_gain": jnp.clip(1.0 + 0.15 * jax.random.normal(splits[11], (D,), jnp.float32), 0.25, 1.75).astype(jnp.bfloat16),
        "ffn_gain": jnp.clip(1.0 + 0.15 * jax.random.normal(splits[12], (D,), jnp.float32), 0.25, 1.75).astype(jnp.bfloat16),
        "router_weight": bell_draw(splits[13], (D, RECUR), D ** -0.5, 0.1875, ((0, 8),)),
    }


epsilon = 1e-05
rope_base = 10000.0

@jax.custom_vjp
def low(v):
    return lax.optimization_barrier(v.astype(jnp.bfloat16)).astype(jnp.float32)

@jax.custom_vjp
def low_back(v):
    return v

def low_keep(v):
    return (low(v), None)

def low_pass(kept, grad):
    return (grad,)

def back_keep(v):
    return (v, None)

def back_low(kept, grad):
    return (low(grad),)
low.defvjp(low_keep, low_pass)
low_back.defvjp(back_keep, back_low)

def product(left_side, right_side):
    return jnp.dot(left_side, right_side, precision=lax.Precision.HIGHEST)

def root_norm(values_in, gain_vec):
    inverse = lax.rsqrt(lax.optimization_barrier(jnp.mean(values_in * values_in, axis=-1, keepdims=True)) + epsilon)
    return values_in * inverse * gain_vec

def rotate(values_in, positions, turn_sign):
    row_count = values_in.shape[0]
    head_count = values_in.shape[1] // HEAD_DIM
    half_dim = HEAD_DIM // 2
    frequency = rope_base ** (-(jnp.arange(half_dim, dtype=jnp.float32) * 2.0 / HEAD_DIM))
    angles = positions.astype(jnp.float32)[:, None] * frequency[None, :]
    cosine = jnp.cos(angles)[:, None, :]
    sine_part = turn_sign * jnp.sin(angles)[:, None, :]
    pieces = values_in.reshape(row_count, head_count, HEAD_DIM)
    first_half = pieces[:, :, :half_dim]
    second = pieces[:, :, half_dim:]
    turned = jnp.concatenate([first_half * cosine - second * sine_part, second * cosine + first_half * sine_part], axis=-1)
    return turned.reshape(row_count, head_count * HEAD_DIM)

def attention(queries, keys, values, segment_ids, active, positions):
    length = queries.shape[0]
    block_rows = min(512, length)
    groups = HEADS // KV_HEADS
    key_heads = keys.reshape(length, KV_HEADS, HEAD_DIM)
    value_heads = values.reshape(length, KV_HEADS, HEAD_DIM)

    def one_block(pieces):
        query_block, query_pos, query_seg = pieces
        query_heads = query_block.reshape(block_rows, KV_HEADS, groups, HEAD_DIM)
        scaled = jnp.einsum('qkgd,tkd->kgqt', query_heads, key_heads, precision=lax.Precision.HIGHEST) * HEAD_DIM ** (-0.5)
        scores = low_back(scaled)
        visible = (segment_ids[None, :] == query_seg[:, None]) & (positions[None, :] <= query_pos[:, None]) & (active[None, :] | (positions[None, :] == query_pos[:, None]))
        probs = low(jax.nn.softmax(jnp.where(visible[None, None], scores, -1e+30), axis=-1))
        mixed = jnp.einsum('kgqt,tkd->qkgd', probs, value_heads, precision=lax.Precision.HIGHEST)
        return mixed.reshape(block_rows, HEADS * HEAD_DIM)
    blocks = lax.map(jax.checkpoint(one_block), (queries.reshape(length // block_rows, block_rows, HEADS * HEAD_DIM), positions.reshape(length // block_rows, block_rows), segment_ids.reshape(length // block_rows, block_rows)))
    return blocks.reshape(length, HEADS * HEAD_DIM)

def forward(params, state_in, segment_ids, depth_ids):
    query_w, key_w, value_w, out_w, gate_w, up_w, down_w, attn_g, ffn_g, router_w = params
    length = state_in.shape[0]
    positions = jnp.arange(length, dtype=jnp.int32)
    state = state_in
    for recursion in range(RECUR):
        active = depth_ids > recursion
        active_f = active.astype(jnp.float32)
        attn_input = low(root_norm(state, attn_g))
        queries = low(rotate(low_back(product(attn_input, query_w)), positions, 1.0))
        keys = low(rotate(low_back(product(attn_input, key_w)), positions, 1.0))
        values = low(low_back(product(attn_input, value_w)))
        attended = low_back(low(attention(queries, keys, values, segment_ids, active, positions)))
        attn_branch = low_back(product(attended, out_w))
        midway = state + attn_branch
        ffn_input = low(root_norm(midway, ffn_g))
        gate_pre = low_back(product(ffn_input, gate_w))
        up_pre = low_back(product(ffn_input, up_w))
        hidden = low(jax.nn.silu(gate_pre) * up_pre)
        ffn_branch = low_back(product(hidden, down_w))
        router_gate = jax.nn.sigmoid(product(state, router_w[:, recursion]))
        state = state + (active_f * router_gate)[:, None] * (attn_branch + ffn_branch)
    return state

def reference(inputs, cotangent, segments, depths, query_weight, key_weight, value_weight, out_weight, gate_weight, up_weight, down_weight, attn_gain, ffn_gain, router_weight):
    params = tuple((weight.astype(jnp.float32) for weight in (query_weight, key_weight, value_weight, out_weight, gate_weight, up_weight, down_weight, attn_gain, ffn_gain, router_weight)))
    pack_total = MICRO * PACKS
    flat_inputs = inputs.reshape(pack_total, LEN, D)
    flat_cot = cotangent.reshape(pack_total, LEN, D)
    flat_seg = segments.reshape(pack_total, LEN)
    flat_depth = depths.reshape(pack_total, LEN)

    def one_pack(carry, pieces):
        pack_in, pack_cot, pack_seg, pack_depth = pieces
        pack_out, pull = jax.vjp(lambda weights, state_in: forward(weights, state_in, pack_seg, pack_depth), params, pack_in)
        weight_grads, input_grads = pull(pack_cot)
        return (tuple((earlier + latest for earlier, latest in zip(carry, weight_grads))), (pack_out, input_grads))
    starting = tuple((jnp.zeros(weight.shape, jnp.float32) for weight in params))
    summed, (outs_all, grads_all) = lax.scan(one_pack, starting, (flat_inputs, flat_cot, flat_seg, flat_depth))
    return (outs_all.reshape(MICRO, PACKS, LEN, D), grads_all.reshape(MICRO, PACKS, LEN, D), summed[0], summed[1], summed[2], summed[3], summed[4], summed[5], summed[6], summed[7], summed[8], summed[9])
```

```python
import functools

import jax
import jax.numpy as jnp
from jax import lax
from jax.experimental import pallas as pl
from jax.experimental.pallas import tpu as pltpu
from jax.sharding import PartitionSpec as P

HEADS = 15
KV_HEADS = 5
HEAD_DIM = 64
RECUR = 3
GROUP = HEADS // KV_HEADS
KW = KV_HEADS * HEAD_DIM
QW = HEADS * HEAD_DIM
LANE = 128
MIB = 2**20

epsilon = 1e-05
rope_base = 10000.0

NN = (((1,), (0,)), ((), ()))
NT = (((1,), (1,)), ((), ()))
BF = jnp.bfloat16
F32 = jnp.float32

vmem = pl.BlockSpec(memory_space=pltpu.VMEM)


def dot(left, right, dims=NN):
    return lax.dot_general(left, right, dims, preferred_element_type=F32)


def ceil_to(size, unit):
    return -(-size // unit) * unit


def shape(dims, dtype):
    return jax.ShapeDtypeStruct(dims, dtype)


def params(limit):
    return pltpu.CompilerParams(vmem_limit_bytes=limit * MIB)


def turn(block, cosine, sine):
    lanes = lax.broadcasted_iota(jnp.int32, block.shape, 1) % HEAD_DIM
    partner = jnp.where(
        lanes < HEAD_DIM // 2,
        pltpu.roll(block, LANE - HEAD_DIM // 2, 1),
        pltpu.roll(block, HEAD_DIM // 2, 1),
    )
    return block * cosine + partner * sine


def norm_back(grad_out, values_in, gain):
    inverse = lax.rsqrt(jnp.mean(values_in * values_in, axis=-1, keepdims=True) + epsilon)
    weighted = grad_out * gain
    inner = jnp.mean(weighted * values_in, axis=-1, keepdims=True)
    grad_gain = jnp.sum(grad_out * values_in * inverse, axis=0, keepdims=True)
    return weighted * inverse - values_in * (inverse * inverse * inverse * inner), grad_gain


def pre_kernel(cols, state, gain, weight, cosine, sine, normed, queries, pair, qbuf, kbuf):
    qc, kc = cols
    values_in = state[...]
    inverse = lax.rsqrt(jnp.mean(values_in * values_in, axis=-1, keepdims=True) + epsilon)
    low = (values_in * inverse * gain[...]).astype(BF)
    normed[...] = low
    for piece in range(weight.shape[0]):
        made = dot(low, weight[piece])
        qbuf[:, piece * qc : (piece + 1) * qc] = made[:, :qc]
        kbuf[:, piece * kc : (piece + 1) * kc] = made[:, qc : qc + kc]
        pair[:, KW + piece * kc : KW + (piece + 1) * kc] = made[:, qc + kc : qc + 2 * kc].astype(BF)
    for buf, out, width, scale in ((qbuf, queries, QW, HEAD_DIM**-0.5), (kbuf, pair, KW, 1.0)):
        for start in range(0, width, LANE):
            stop = min(start + LANE, width)
            turned = turn(buf[:, start : start + LANE], cosine[...], sine[...]) * scale
            out[:, start:stop] = turned[:, : stop - start].astype(BF)


def pre_part(state, gain, weight, cosine, sine, cols):
    tokens, width = state.shape
    return pl.pallas_call(
        functools.partial(pre_kernel, cols),
        out_shape=(
            shape((tokens, width), BF),
            shape((tokens, QW), BF),
            shape((tokens, 2 * KW), BF),
        ),
        in_specs=[vmem] * 5,
        out_specs=(vmem,) * 3,
        scratch_shapes=[
            pltpu.VMEM((tokens, ceil_to(QW, LANE)), F32),
            pltpu.VMEM((tokens, ceil_to(KW, LANE)), F32),
        ],
        compiler_params=params(40),
        name="pre",
    )(state, gain, weight, cosine, sine)


def fill_bias(info, bias, recursion):
    keys, tokens = bias.shape
    columns = info[...].T
    place = lax.broadcasted_iota(jnp.int32, (keys, tokens), 0)
    query = lax.broadcasted_iota(jnp.int32, (keys, tokens), 1)
    apart = place % tokens - place // tokens * tokens - query
    same = columns[:, 0:1] == info[0:1, 0:tokens]
    live = columns[:, 1:2] > recursion
    seen = same & (((apart < 0) & live) | (apart == 0))
    bias[...] = jnp.where(seen, 0.0, -1e30)


def head_cols(head):
    return slice(head * HEAD_DIM, (head + 1) * HEAD_DIM)


def stack_heads(ref, group):
    heads = range(group * GROUP, (group + 1) * GROUP)
    return jnp.concatenate([ref[:, head_cols(head)] for head in heads], axis=0)


def attend_kernel(blocks, recursion, *refs):
    queries, pairs = refs[0], refs[1 : 1 + blocks]
    info, attended, logs, bias = refs[1 + blocks :]
    tokens = queries.shape[0]
    keys = blocks * tokens
    fill_bias(info, bias, recursion)
    logs[...] = jnp.zeros(logs.shape, F32)
    for group in range(KV_HEADS):
        key = jnp.concatenate([ref[:, head_cols(group)] for ref in pairs], axis=0)
        value = jnp.concatenate([ref[:, head_cols(KV_HEADS + group)] for ref in pairs], axis=0)
        value_t = jnp.concatenate([value.T, jnp.ones((16, keys), BF)], axis=0)
        query = stack_heads(queries, group)
        scores = dot(key, query, NT) + jnp.concatenate([bias[...]] * GROUP, axis=1)
        top = jnp.max(scores, axis=0, keepdims=True)
        weights = jnp.exp(scores - top).astype(BF)
        mixed = dot(value_t, weights)
        total = mixed[HEAD_DIM : HEAD_DIM + 1]
        mixed = mixed[:HEAD_DIM] * (1.0 / total)
        log_total = top + jnp.log(total)
        for offset in range(GROUP):
            head = group * GROUP + offset
            span = slice(offset * tokens, (offset + 1) * tokens)
            attended[:, head_cols(head)] = mixed[:, span].T.astype(BF)
            logs[head : head + 1, :] = log_total[:, span]


def attend(queries, pairs, info, recursion):
    tokens = queries.shape[0]
    blocks = len(pairs)
    return pl.pallas_call(
        functools.partial(attend_kernel, blocks, recursion),
        out_shape=(shape((tokens, QW), BF), shape((ceil_to(HEADS, 8), tokens), F32)),
        in_specs=[vmem] * (2 + blocks),
        out_specs=(vmem, vmem),
        scratch_shapes=[pltpu.VMEM((blocks * tokens, tokens), F32)],
        compiler_params=params(40),
        name="attend",
    )(queries, *pairs, info)


def attend_back_kernel(blocks, recursion, *refs):
    queries, pairs = refs[0], refs[1 : 1 + blocks]
    info, attended, logs, grad, grad_queries = refs[1 + blocks : 6 + blocks]
    grad_pairs, bias = refs[6 + blocks : 6 + 2 * blocks], refs[6 + 2 * blocks]
    tokens = queries.shape[0]
    fill_bias(info, bias, recursion)
    product = (attended[...].astype(F32) * grad[...].astype(F32)).T
    for group in range(KV_HEADS):
        key = jnp.concatenate([ref[:, head_cols(group)] for ref in pairs], axis=0)
        value = jnp.concatenate([ref[:, head_cols(KV_HEADS + group)] for ref in pairs], axis=0)
        key_t = key.T
        query = stack_heads(queries, group)
        grad_mixed = stack_heads(grad, group)
        heads = range(group * GROUP, (group + 1) * GROUP)
        delta = jnp.concatenate(
            [jnp.sum(product[head_cols(head)], axis=0, keepdims=True) for head in heads], axis=1
        )
        log_total = jnp.concatenate([logs[head : head + 1, :] for head in heads], axis=1)
        scores = dot(key, query, NT) + jnp.concatenate([bias[...]] * GROUP, axis=1)
        probs = jnp.exp(scores - log_total)
        grad_probs = dot(value, grad_mixed, NT)
        grad_scores = (probs * (grad_probs - delta)).astype(BF)
        grad_value = dot(probs.astype(BF), grad_mixed)
        grad_key = dot(grad_scores, query)
        grad_query = dot(key_t, grad_scores) * HEAD_DIM**-0.5
        for offset, head in enumerate(heads):
            span = slice(offset * tokens, (offset + 1) * tokens)
            grad_queries[:, head_cols(head)] = grad_query[:, span].T
        for block, ref in enumerate(grad_pairs):
            rows = slice(block * tokens, (block + 1) * tokens)
            ref[:, head_cols(group)] = grad_key[rows].astype(ref.dtype)
            ref[:, head_cols(KV_HEADS + group)] = grad_value[rows].astype(ref.dtype)


def attend_back(queries, pairs, info, attended, logs, grad, recursion):
    tokens = queries.shape[0]
    blocks = len(pairs)
    return pl.pallas_call(
        functools.partial(attend_back_kernel, blocks, recursion),
        out_shape=(shape((tokens, QW), F32), shape((tokens, 2 * KW), F32))
        + (shape((tokens, 2 * KW), BF),) * (blocks - 1),
        in_specs=[vmem] * (5 + blocks),
        out_specs=(vmem,) * (1 + blocks),
        scratch_shapes=[pltpu.VMEM((blocks * tokens, tokens), F32)],
        compiler_params=params(48),
        name="attend_back",
    )(queries, *pairs, info, attended, logs, grad)


def post_kernel(
    shift, state, attended, out_w, gain, router, active, gate_w, up_w, down_w,
    state_out, normed, gate_out, up_out, hidden_out, midway_out, update_out, routed,
    branch, total,
):
    pieces, cols = down_w.shape[0], down_w.shape[2]
    step = pl.program_id(0)

    @pl.when(step == 0)
    def _():
        for piece in range(pieces):
            made = dot(attended[...], out_w[piece])
            branch[:, piece * cols : (piece + 1) * cols] = made[:, shift : shift + cols]
        midway = state[...] + branch[...]
        midway_out[...] = midway
        inverse = lax.rsqrt(jnp.mean(midway * midway, axis=-1, keepdims=True) + epsilon)
        normed[...] = (midway * inverse * gain[...]).astype(BF)
        total[...] = jnp.zeros(total.shape, F32)

    low = normed[...]
    gate = dot(low, gate_w[0])
    up = dot(low, up_w[0])
    gate_out[0] = gate.astype(BF)
    up_out[0] = up.astype(BF)
    hidden = (gate / (1.0 + jnp.exp(-gate)) * up).astype(BF)
    hidden_out[0] = hidden
    for piece in range(pieces):
        total[piece] += dot(hidden, down_w[piece])

    @pl.when(step == pl.num_programs(0) - 1)
    def _():
        for piece in range(pieces):
            span = slice(piece * cols, (piece + 1) * cols)
            branch[:, span] = branch[:, span] + total[piece]
        update = branch[...]
        update_out[...] = update
        before = state[...]
        chance = 1.0 / (1.0 + jnp.exp(-jnp.sum(before * router[...], axis=-1, keepdims=True)))
        routed[...] = jnp.broadcast_to(chance, routed.shape)
        state_out[...] = before + (active[:, 0:1] * chance) * update


def post_part(state, attended, out_w, gain, router, active, gate_w, up_w, down_w, shift):
    tokens, width = state.shape
    pieces, _, part = gate_w.shape
    cols = down_w.shape[2]

    def whole(*dims):
        return pl.BlockSpec(dims, lambda f: (0,) * len(dims))

    chunk = pl.BlockSpec((1, tokens, part), lambda f: (f, 0, 0))
    weight = pl.BlockSpec((1, width, part), lambda f: (f, 0, 0))
    row = whole(tokens, width)
    return pl.pallas_call(
        functools.partial(post_kernel, shift),
        grid=(pieces,),
        out_shape=(
            shape((tokens, width), F32),
            shape((tokens, width), BF),
            shape((pieces, tokens, part), BF),
            shape((pieces, tokens, part), BF),
            shape((pieces, tokens, part), BF),
            shape((tokens, width), F32),
            shape((tokens, width), F32),
            shape((tokens, LANE), F32),
        ),
        in_specs=[
            row, whole(tokens, QW), whole(*out_w.shape), whole(1, width), whole(1, width),
            whole(tokens, LANE), weight, weight,
            pl.BlockSpec((pieces, part, cols), lambda f: (0, f, 0)),
        ],
        out_specs=(row, row, chunk, chunk, chunk, row, row, whole(tokens, LANE)),
        scratch_shapes=[pltpu.VMEM((tokens, width), F32), pltpu.VMEM((pieces, tokens, cols), F32)],
        compiler_params=params(48),
        name="post",
    )(state, attended, out_w, gain, router, active, gate_w, up_w, down_w)


def post_back_kernel(
    shift, grad_state, update, routed, active, state, midway, gain, router, out_w, gate_pre, up_pre,
    gate_w, up_w, down_w,
    grad_ffn, grad_gate_out, grad_up_out, grad_branch, grad_attended, partial, gain_grad, router_grad,
    total, scaled, logit,
):
    pieces, cols = down_w.shape[0], down_w.shape[2]
    step = pl.program_id(0)

    @pl.when(step == 0)
    def _():
        chance = routed[:, 0:1]
        weight = active[:, 0:1] * chance
        grad = grad_state[...]
        change = grad * weight
        scaled[...] = change
        slope = jnp.sum(grad * update[...], axis=-1, keepdims=True) * weight * (1.0 - chance)
        logit[...] = jnp.broadcast_to(slope, logit.shape)
        router_grad[...] = jnp.sum(state[...] * slope, axis=0, keepdims=True)
        low = change.astype(BF)
        for piece in range(pieces):
            grad_ffn[piece] = low[:, piece * cols : (piece + 1) * cols]
        total[...] = jnp.zeros(total.shape, F32)

    grad_hidden = dot(grad_ffn[0], down_w[0], NT)
    for piece in range(1, pieces):
        grad_hidden += dot(grad_ffn[piece], down_w[piece], NT)
    gate = gate_pre[0].astype(F32)
    chance = 1.0 / (1.0 + jnp.exp(-gate))
    smooth = gate * chance
    grad_gate = (grad_hidden * up_pre[0].astype(F32) * (chance + smooth * (1.0 - chance))).astype(BF)
    grad_up = (grad_hidden * smooth).astype(BF)
    grad_gate_out[0] = grad_gate
    grad_up_out[0] = grad_up
    total[...] += dot(grad_gate, gate_w[0], NT) + dot(grad_up, up_w[0], NT)

    @pl.when(step == pl.num_programs(0) - 1)
    def _():
        grad_midway, grad_gain = norm_back(total[...], midway[...], gain[...])
        gain_grad[...] = grad_gain
        partial[...] = grad_state[...] + logit[:, 0:1] * router[...] + grad_midway
        low = (scaled[...] + grad_midway).astype(BF)
        grad = None
        for piece in range(pieces):
            if grad_branch.shape[2] > cols:
                grad_branch[piece] = jnp.zeros(grad_branch.shape[1:], BF)
            grad_branch[piece, :, shift : shift + cols] = low[:, piece * cols : (piece + 1) * cols]
            made = dot(grad_branch[piece], out_w[piece], NT)
            grad = made if grad is None else grad + made
        grad_attended[...] = grad.astype(BF)


def post_back(
    grad_state, update, routed, active, state, midway, gain, router, out_w, gate_pre, up_pre,
    gate_w, up_w, down_w, shift,
):
    tokens, width = state.shape
    pieces, _, part = gate_w.shape
    cols = down_w.shape[2]

    def whole(*dims):
        return pl.BlockSpec(dims, lambda f: (0,) * len(dims))

    chunk = pl.BlockSpec((1, tokens, part), lambda f: (f, 0, 0))
    weight = pl.BlockSpec((1, width, part), lambda f: (f, 0, 0))
    row, thin, line = whole(tokens, width), whole(tokens, LANE), whole(1, width)
    branch_dims = (pieces, tokens, out_w.shape[2])
    return pl.pallas_call(
        functools.partial(post_back_kernel, shift),
        grid=(pieces,),
        out_shape=(
            shape((pieces, tokens, cols), BF),
            shape((pieces, tokens, part), BF),
            shape((pieces, tokens, part), BF),
            shape(branch_dims, BF),
            shape((tokens, QW), BF),
            shape((tokens, width), F32),
            shape((1, width), F32),
            shape((1, width), F32),
        ),
        in_specs=[
            row, row, thin, thin, row, row, line, line, whole(*out_w.shape), chunk, chunk,
            weight, weight, pl.BlockSpec((pieces, part, cols), lambda f: (0, f, 0)),
        ],
        out_specs=(
            whole(pieces, tokens, cols), chunk, chunk, whole(*branch_dims), whole(tokens, QW),
            row, line, line,
        ),
        scratch_shapes=[
            pltpu.VMEM((tokens, width), F32),
            pltpu.VMEM((tokens, width), F32),
            pltpu.VMEM((tokens, LANE), F32),
        ],
        compiler_params=params(48),
        name="post_back",
    )(grad_state, update, routed, active, state, midway, gain, router, out_w, gate_pre, up_pre,
      gate_w, up_w, down_w)


def pre_back_kernel(cols, blocks, *refs):
    qc, kc = cols
    grad_queries, own, others = refs[0], refs[1], refs[2 : 1 + blocks]
    partial, state, gain, weight, cosine, sine = refs[1 + blocks : 7 + blocks]
    packed, grad_state, gain_grad, qbuf, kbuf = refs[7 + blocks :]
    summed = own[...]
    for ref in others:
        summed = summed + ref[...].astype(F32)
    kbuf[:, :KW] = summed[:, :KW]
    qbuf[:, :QW] = grad_queries[...]
    for buf in (qbuf, kbuf):
        for start in range(0, buf.shape[1], LANE):
            span = slice(start, start + LANE)
            buf[:, span] = turn(buf[:, span], cosine[...], -sine[...])
    low_q = qbuf[...].astype(BF)
    low_k = kbuf[...].astype(BF)
    low_v = summed[:, KW:].astype(BF)
    total = None
    for piece in range(weight.shape[0]):
        packed[piece] = jnp.zeros(packed.shape[1:], BF)
        packed[piece, :, :qc] = low_q[:, piece * qc : (piece + 1) * qc]
        packed[piece, :, qc : qc + kc] = low_k[:, piece * kc : (piece + 1) * kc]
        packed[piece, :, qc + kc : qc + 2 * kc] = low_v[:, piece * kc : (piece + 1) * kc]
        made = dot(packed[piece], weight[piece], NT)
        total = made if total is None else total + made
    grad_in, grad_gain = norm_back(total, state[...], gain[...])
    gain_grad[...] = grad_gain
    grad_state[...] = partial[...] + grad_in


def pre_back(grad_queries, grad_pairs, partial, state, gain, weight, cosine, sine, cols):
    tokens, width = state.shape
    return pl.pallas_call(
        functools.partial(pre_back_kernel, cols, len(grad_pairs)),
        out_shape=(
            shape((weight.shape[0], tokens, weight.shape[2]), BF),
            shape((tokens, width), F32),
            shape((1, width), F32),
        ),
        in_specs=[vmem] * (7 + len(grad_pairs)),
        out_specs=(vmem,) * 3,
        scratch_shapes=[
            pltpu.VMEM((tokens, ceil_to(QW, LANE)), F32),
            pltpu.VMEM((tokens, ceil_to(KW, LANE)), F32),
        ],
        compiler_params=params(40),
        name="pre_back",
    )(grad_queries, *grad_pairs, partial, state, gain, weight, cosine, sine)


def attn_sums_kernel(count, low_col, *refs):
    normed, packed = refs[:count], refs[count : 2 * count]
    attended, branch = refs[2 * count : 3 * count], refs[3 * count : 4 * count]
    out, left, right = refs[4 * count :]

    @pl.when(pl.program_id(0) == 0)
    def _():
        left[...] = jnp.concatenate([ref[...].T for ref in normed], axis=1)
        right[...] = jnp.concatenate([ref[...].T for ref in attended], axis=1)

    first = dot(left[...], jnp.concatenate([ref[0] for ref in packed], axis=0))
    second = dot(right[...], jnp.concatenate([ref[0] for ref in branch], axis=0))
    high_col = first.shape[1]
    if low_col:
        out[0, :, :low_col] = first[:, :low_col].astype(BF)
    out[0, :, low_col:high_col] = (first[:, low_col:] + second[:, : high_col - low_col]).astype(BF)
    if high_col < out.shape[2]:
        out[0, :, high_col:] = second[:, high_col - low_col :].astype(BF)


def attn_sums(normed, packed, attended, branch, low_col, total_cols):
    count = len(normed)
    tokens, width = normed[0].shape
    pieces = packed[0].shape[0]
    row = pl.BlockSpec((tokens, width), lambda s: (0, 0))
    part = pl.BlockSpec((1, tokens, packed[0].shape[2]), lambda s: (s, 0, 0))
    thin = pl.BlockSpec((1, tokens, branch[0].shape[2]), lambda s: (s, 0, 0))
    return pl.pallas_call(
        functools.partial(attn_sums_kernel, count, low_col),
        grid=(pieces,),
        out_shape=shape((pieces, width, total_cols), BF),
        in_specs=[row] * count + [part] * count + [row] * count + [thin] * count,
        out_specs=pl.BlockSpec((1, width, total_cols), lambda s: (s, 0, 0)),
        scratch_shapes=[pltpu.VMEM((width, count * tokens), BF)] * 2,
        compiler_params=params(56),
        name="attn_sums",
    )(*normed, *packed, *attended, *branch)


def pair_sums_kernel(count, *refs):
    normed, first, second = refs[:count], refs[count : 2 * count], refs[2 * count : 3 * count]
    first_out, second_out, left = refs[3 * count :]

    @pl.when(pl.program_id(0) == 0)
    def _():
        left[...] = jnp.concatenate([ref[...].T for ref in normed], axis=1)

    for source, out in ((first, first_out), (second, second_out)):
        out[0] = dot(left[...], jnp.concatenate([ref[0] for ref in source], axis=0)).astype(BF)


def pair_sums(normed, first, second):
    count = len(normed)
    tokens, width = normed[0].shape
    pieces, _, part = first[0].shape
    row = pl.BlockSpec((tokens, width), lambda s: (0, 0))
    chunk = pl.BlockSpec((1, tokens, part), lambda s: (s, 0, 0))
    result = pl.BlockSpec((1, width, part), lambda s: (s, 0, 0))
    return pl.pallas_call(
        functools.partial(pair_sums_kernel, count),
        grid=(pieces,),
        out_shape=(shape((pieces, width, part), BF),) * 2,
        in_specs=[row] * count + [chunk] * (2 * count),
        out_specs=(result, result),
        scratch_shapes=[pltpu.VMEM((width, count * tokens), BF)],
        compiler_params=params(56),
        name="pair_sums",
    )(*normed, *first, *second)


def down_sums_kernel(count, *refs):
    hidden, grads, out, right = refs[:count], refs[count : 2 * count], refs[-2], refs[-1]

    @pl.when(pl.program_id(0) == 0)
    def _():
        for piece in range(out.shape[0]):
            right[piece] = jnp.concatenate([ref[piece] for ref in grads], axis=0)

    left = jnp.concatenate([ref[0].T for ref in hidden], axis=1)
    for piece in range(out.shape[0]):
        out[piece] = dot(left, right[piece]).astype(BF)


def down_sums(hidden, grads):
    count = len(hidden)
    pieces, tokens, part = hidden[0].shape
    cols = grads[0].shape[2]
    return pl.pallas_call(
        functools.partial(down_sums_kernel, count),
        grid=(pieces,),
        out_shape=shape((pieces, pieces * part, cols), BF),
        in_specs=[pl.BlockSpec((1, tokens, part), lambda f: (f, 0, 0))] * count
        + [pl.BlockSpec((pieces, tokens, cols), lambda f: (0, 0, 0))] * count,
        out_specs=pl.BlockSpec((pieces, part, cols), lambda f: (0, f, 0)),
        scratch_shapes=[pltpu.VMEM((pieces, count * tokens, cols), BF)],
        compiler_params=params(56),
        name="down_sums",
    )(*hidden, *grads)


def rope_tables(tokens):
    half = HEAD_DIM // 2
    frequency = rope_base ** (-(jnp.arange(half, dtype=F32) * 2.0 / HEAD_DIM))
    positions = lax.axis_index("seq") * tokens + jnp.arange(tokens, dtype=jnp.int32)
    angles = positions.astype(F32)[:, None] * frequency[None, :]
    cosine, sine = jnp.cos(angles), jnp.sin(angles)
    repeat = LANE // HEAD_DIM
    return (
        jnp.concatenate([cosine, cosine] * repeat, axis=1),
        jnp.concatenate([-sine, sine] * repeat, axis=1),
    )


def pass_on(array, step, count):
    return lax.ppermute(array, "seq", [(i, i + step) for i in range(count - step)])


def pass_back(array, step, count):
    return lax.ppermute(array, "seq", [(i + step, i) for i in range(count - step)])


def local(
    inputs, cotangent, segments, depths, query_weight, key_weight, value_weight, out_weight,
    gate_weight, up_weight, down_weight, attn_gain, ffn_gain, router_weight,
):
    micros, _, tokens, width = inputs.shape
    seq = lax.axis_size("seq")
    mine = lax.axis_index("seq")
    rows = query_weight.shape[0]
    qc, kc = query_weight.shape[1], key_weight.shape[1]
    cols = (qc, kc)

    attn_local = jnp.concatenate([query_weight, key_weight, value_weight, out_weight], axis=1)
    both = ("seq", "dp")

    def gather(local_part):
        full = lax.all_gather(local_part, both, axis=0, tiled=False)
        return full.reshape(seq, -1, full.shape[-1])

    attn_w = gather(attn_local)
    gate_w, up_w, down_w = gather(gate_weight), gather(up_weight), gather(down_weight)
    small = jnp.concatenate([attn_gain[:, None], ffn_gain[:, None], router_weight], axis=1)
    small = lax.all_gather(small, "dp", axis=0, tiled=True).astype(F32).T
    attn_g, ffn_g = small[0:1], small[1:2]
    routers = [small[2 + r : 3 + r] for r in range(RECUR)]
    used = qc + 2 * kc
    total_cols = attn_w.shape[2]
    high_col = min(ceil_to(used, LANE), total_cols)
    low_col = used // LANE * LANE
    shift = used - low_col
    qkv_w, out_w = attn_w[:, :, :high_col], attn_w[:, :, low_col:]

    marks = jnp.stack([segments[:, 0], depths[:, 0]], axis=1)
    marks = lax.all_gather(marks, "seq", axis=0, tiled=False).astype(F32)
    order = mine - jnp.arange(seq)
    marks = jnp.where((order >= 0)[:, None, None, None], marks[order % seq], -1.0)
    marks = marks.transpose(1, 2, 0, 3).reshape(micros, 2, seq * tokens)
    infos = [jnp.pad(marks[m], ((0, 6), (0, 0))) for m in range(micros)]
    cosine, sine = rope_tables(tokens)

    states = [inputs[m, 0] for m in range(micros)]
    actives = [
        [
            jnp.broadcast_to((depths[m, 0] > r).astype(F32)[:, None], (tokens, LANE))
            for r in range(RECUR)
        ]
        for m in range(micros)
    ]
    saved = [[None] * RECUR for _ in range(micros)]
    for r in range(RECUR):
        made = []
        for m in range(micros):
            normed, queries, pair = pre_part(states[m], attn_g, qkv_w, cosine, sine, cols)
            pairs = [pair] + [pass_on(pair, step, seq) for step in range(1, seq)]
            made.append((normed, queries, pairs))
        for m in range(micros):
            normed, queries, pairs = made[m]
            attended, logs = attend(queries, pairs, infos[m], r)
            state_out, ffn_in, gate, up, hidden, midway, update, routed = post_part(
                states[m], attended, out_w, ffn_g, routers[r], actives[m][r], gate_w, up_w, down_w, shift
            )
            saved[m][r] = dict(
                state=states[m], normed=normed, queries=queries, pairs=pairs, attended=attended,
                logs=logs, ffn_in=ffn_in, gate=gate, up=up, hidden=hidden, midway=midway,
                update=update, routed=routed,
            )
            states[m] = state_out

    grads = [cotangent[m, 0] for m in range(micros)]
    attn_gain_sum, ffn_gain_sum, router_sums = 0.0, 0.0, [0.0] * RECUR
    for r in reversed(range(RECUR)):
        partials = []
        for m in range(micros):
            s = saved[m][r]
            grad_ffn, grad_gate, grad_up, grad_branch, grad_attended, partial, gain_grad, router_grad = (
                post_back(
                    grads[m], s["update"], s["routed"], actives[m][r], s["state"], s["midway"], ffn_g,
                    routers[r], out_w, s["gate"], s["up"], gate_w, up_w, down_w, shift,
                )
            )
            ffn_gain_sum = ffn_gain_sum + gain_grad
            router_sums[r] = router_sums[r] + router_grad
            s.update(grad_ffn=grad_ffn, grad_gate=grad_gate, grad_up=grad_up, grad_branch=grad_branch)
            grad_queries, *grad_pairs = attend_back(
                s["queries"], s["pairs"], infos[m], s["attended"], s["logs"], grad_attended, r
            )
            grad_pairs = [grad_pairs[0]] + [
                pass_back(grad_pairs[step], step, seq) for step in range(1, seq)
            ]
            partials.append((partial, grad_queries, grad_pairs))
        for m in range(micros):
            s = saved[m][r]
            partial, grad_queries, grad_pairs = partials[m]
            packed, grads[m], gain_grad = pre_back(
                grad_queries, grad_pairs, partial, s["state"], attn_g, qkv_w, cosine, sine, cols
            )
            attn_gain_sum = attn_gain_sum + gain_grad
            s.update(packed=packed)

    flat = [saved[m][r] for r in reversed(range(RECUR)) for m in range(micros)]

    def every(name):
        return [s[name] for s in flat]

    down_sum = down_sums(every("hidden"), every("grad_ffn"))
    gate_sum, up_sum = pair_sums(every("ffn_in"), every("grad_gate"), every("grad_up"))
    attn_sum = attn_sums(
        every("normed"), every("packed"), every("attended"), every("grad_branch"), low_col, total_cols
    )

    def reduce(partial):
        partial = partial.reshape(seq, lax.axis_size("dp"), -1, partial.shape[-1])
        part = lax.psum_scatter(partial, "seq", scatter_dimension=0, tiled=False)
        return lax.psum_scatter(part, "dp", scatter_dimension=0, tiled=False).astype(F32)

    down_grad, gate_grad, up_grad, attn_grad = (
        reduce(partial) for partial in (down_sum, gate_sum, up_sum, attn_sum)
    )
    small_sum = jnp.concatenate([attn_gain_sum, ffn_gain_sum, *router_sums], axis=0)
    small_sum = lax.psum(small_sum, both)
    small_own = lax.dynamic_slice_in_dim(small_sum, lax.axis_index("dp") * rows, rows, axis=1)

    outputs = jnp.stack(states, axis=0)[:, None]
    input_grad = jnp.stack(grads, axis=0)[:, None]
    return (
        outputs,
        input_grad,
        attn_grad[:, :qc],
        attn_grad[:, qc : qc + kc],
        attn_grad[:, qc + kc : used],
        attn_grad[:, used:],
        gate_grad,
        up_grad,
        down_grad,
        small_own[0],
        small_own[1],
        small_own[2:].T,
    )


def solution(mesh):
    data = P(None, "dp", "seq", None)
    marks = P(None, "dp", "seq")
    weight = P("dp", "seq")
    in_specs = (data, data, marks, marks) + (weight,) * 7 + (P("dp"), P("dp"), P("dp", None))
    out_specs = (data, data) + (weight,) * 7 + (P("dp"), P("dp"), P("dp", None))
    return jax.shard_map(local, mesh=mesh, in_specs=in_specs, out_specs=out_specs, check_vma=False)
```

```python
import functools

import jax
import jax.numpy as jnp
from jax import lax
from jax.experimental import pallas as pl
from jax.experimental.pallas import tpu as pltpu
from jax.sharding import PartitionSpec as P

HEADS = 15
KV_HEADS = 5
HEAD_DIM = 64
RECUR = 3
GROUP = HEADS // KV_HEADS
KW = KV_HEADS * HEAD_DIM
QW = HEADS * HEAD_DIM
LANE = 128
MIB = 2**20

epsilon = 1e-05
rope_base = 10000.0

NN = (((1,), (0,)), ((), ()))
NT = (((1,), (1,)), ((), ()))
BF = jnp.bfloat16
F32 = jnp.float32

vmem = pl.BlockSpec(memory_space=pltpu.VMEM)


def dot(left, right, dims=NN):
    return lax.dot_general(left, right, dims, preferred_element_type=F32)


def ceil_to(size, unit):
    return -(-size // unit) * unit


def shape(dims, dtype):
    return jax.ShapeDtypeStruct(dims, dtype)


def params(limit):
    return pltpu.CompilerParams(vmem_limit_bytes=limit * MIB)


def turn(block, cosine, sine):
    lanes = lax.broadcasted_iota(jnp.int32, block.shape, 1) % HEAD_DIM
    partner = jnp.where(
        lanes < HEAD_DIM // 2,
        pltpu.roll(block, LANE - HEAD_DIM // 2, 1),
        pltpu.roll(block, HEAD_DIM // 2, 1),
    )
    return block * cosine + partner * sine


def norm_back(grad_out, values_in, gain):
    inverse = lax.rsqrt(jnp.mean(values_in * values_in, axis=-1, keepdims=True) + epsilon)
    weighted = grad_out * gain
    inner = jnp.mean(weighted * values_in, axis=-1, keepdims=True)
    grad_gain = jnp.sum(grad_out * values_in * inverse, axis=0, keepdims=True)
    return weighted * inverse - values_in * (inverse * inverse * inverse * inner), grad_gain


def pre_kernel(cols, state, gain, weight, cosine, sine, normed, queries, pair, qbuf, kbuf):
    qc, kc = cols
    values_in = state[...]
    inverse = lax.rsqrt(jnp.mean(values_in * values_in, axis=-1, keepdims=True) + epsilon)
    low = (values_in * inverse * gain[...]).astype(BF)
    normed[...] = low
    for piece in range(weight.shape[0]):
        made = dot(low, weight[piece])
        qbuf[:, piece * qc : (piece + 1) * qc] = made[:, :qc]
        kbuf[:, piece * kc : (piece + 1) * kc] = made[:, qc : qc + kc]
        pair[:, KW + piece * kc : KW + (piece + 1) * kc] = made[:, qc + kc : qc + 2 * kc].astype(BF)
    for buf, out, width, scale in ((qbuf, queries, QW, HEAD_DIM**-0.5), (kbuf, pair, KW, 1.0)):
        for start in range(0, width, LANE):
            stop = min(start + LANE, width)
            turned = turn(buf[:, start : start + LANE], cosine[...], sine[...]) * scale
            out[:, start:stop] = turned[:, : stop - start].astype(BF)


def pre_part(state, gain, weight, cosine, sine, cols):
    tokens, width = state.shape
    return pl.pallas_call(
        functools.partial(pre_kernel, cols),
        out_shape=(
            shape((tokens, width), BF),
            shape((tokens, QW), BF),
            shape((tokens, 2 * KW), BF),
        ),
        in_specs=[vmem] * 5,
        out_specs=(vmem,) * 3,
        scratch_shapes=[
            pltpu.VMEM((tokens, ceil_to(QW, LANE)), F32),
            pltpu.VMEM((tokens, ceil_to(KW, LANE)), F32),
        ],
        compiler_params=params(40),
        name="pre",
    )(state, gain, weight, cosine, sine)


def fill_bias(info, bias, recursion):
    keys, tokens = bias.shape
    columns = info[...].T
    place = lax.broadcasted_iota(jnp.int32, (keys, tokens), 0)
    query = lax.broadcasted_iota(jnp.int32, (keys, tokens), 1)
    apart = place % tokens - place // tokens * tokens - query
    same = columns[:, 0:1] == info[0:1, 0:tokens]
    live = columns[:, 1:2] > recursion
    seen = same & (((apart < 0) & live) | (apart == 0))
    bias[...] = jnp.where(seen, 0.0, -1e30)


def head_cols(head):
    return slice(head * HEAD_DIM, (head + 1) * HEAD_DIM)


def stack_heads(ref, group):
    heads = range(group * GROUP, (group + 1) * GROUP)
    return jnp.concatenate([ref[:, head_cols(head)] for head in heads], axis=0)


def attend_kernel(blocks, recursion, *refs):
    queries, pairs = refs[0], refs[1 : 1 + blocks]
    info, attended, logs, bias = refs[1 + blocks :]
    tokens = queries.shape[0]
    keys = blocks * tokens
    fill_bias(info, bias, recursion)
    logs[...] = jnp.zeros(logs.shape, F32)
    for group in range(KV_HEADS):
        key = jnp.concatenate([ref[:, head_cols(group)] for ref in pairs], axis=0)
        value = jnp.concatenate([ref[:, head_cols(KV_HEADS + group)] for ref in pairs], axis=0)
        value_t = jnp.concatenate([value.T, jnp.ones((16, keys), BF)], axis=0)
        query = stack_heads(queries, group)
        scores = dot(key, query, NT) + jnp.concatenate([bias[...]] * GROUP, axis=1)
        top = jnp.max(scores, axis=0, keepdims=True)
        weights = jnp.exp(scores - top).astype(BF)
        mixed = dot(value_t, weights)
        total = mixed[HEAD_DIM : HEAD_DIM + 1]
        mixed = mixed[:HEAD_DIM] * (1.0 / total)
        log_total = top + jnp.log(total)
        for offset in range(GROUP):
            head = group * GROUP + offset
            span = slice(offset * tokens, (offset + 1) * tokens)
            attended[:, head_cols(head)] = mixed[:, span].T.astype(BF)
            logs[head : head + 1, :] = log_total[:, span]


def attend(queries, pairs, info, recursion):
    tokens = queries.shape[0]
    blocks = len(pairs)
    return pl.pallas_call(
        functools.partial(attend_kernel, blocks, recursion),
        out_shape=(shape((tokens, QW), BF), shape((ceil_to(HEADS, 8), tokens), F32)),
        in_specs=[vmem] * (2 + blocks),
        out_specs=(vmem, vmem),
        scratch_shapes=[pltpu.VMEM((blocks * tokens, tokens), F32)],
        compiler_params=params(40),
        name="attend",
    )(queries, *pairs, info)


def attend_back_kernel(blocks, recursion, *refs):
    queries, pairs = refs[0], refs[1 : 1 + blocks]
    info, attended, logs, grad, grad_queries = refs[1 + blocks : 6 + blocks]
    grad_pairs, bias = refs[6 + blocks : 6 + 2 * blocks], refs[6 + 2 * blocks]
    tokens = queries.shape[0]
    fill_bias(info, bias, recursion)
    product = (attended[...].astype(F32) * grad[...].astype(F32)).T
    for group in range(KV_HEADS):
        key = jnp.concatenate([ref[:, head_cols(group)] for ref in pairs], axis=0)
        value = jnp.concatenate([ref[:, head_cols(KV_HEADS + group)] for ref in pairs], axis=0)
        key_t = key.T
        query = stack_heads(queries, group)
        grad_mixed = stack_heads(grad, group)
        heads = range(group * GROUP, (group + 1) * GROUP)
        delta = jnp.concatenate(
            [jnp.sum(product[head_cols(head)], axis=0, keepdims=True) for head in heads], axis=1
        )
        log_total = jnp.concatenate([logs[head : head + 1, :] for head in heads], axis=1)
        scores = dot(key, query, NT) + jnp.concatenate([bias[...]] * GROUP, axis=1)
        probs = jnp.exp(scores - log_total)
        grad_probs = dot(value, grad_mixed, NT)
        grad_scores = (probs * (grad_probs - delta)).astype(BF)
        grad_value = dot(probs.astype(BF), grad_mixed)
        grad_key = dot(grad_scores, query)
        grad_query = dot(key_t, grad_scores) * HEAD_DIM**-0.5
        for offset, head in enumerate(heads):
            span = slice(offset * tokens, (offset + 1) * tokens)
            grad_queries[:, head_cols(head)] = grad_query[:, span].T
        for block, ref in enumerate(grad_pairs):
            rows = slice(block * tokens, (block + 1) * tokens)
            ref[:, head_cols(group)] = grad_key[rows].astype(ref.dtype)
            ref[:, head_cols(KV_HEADS + group)] = grad_value[rows].astype(ref.dtype)


def attend_back(queries, pairs, info, attended, logs, grad, recursion):
    tokens = queries.shape[0]
    blocks = len(pairs)
    return pl.pallas_call(
        functools.partial(attend_back_kernel, blocks, recursion),
        out_shape=(shape((tokens, QW), F32), shape((tokens, 2 * KW), F32))
        + (shape((tokens, 2 * KW), BF),) * (blocks - 1),
        in_specs=[vmem] * (5 + blocks),
        out_specs=(vmem,) * (1 + blocks),
        scratch_shapes=[pltpu.VMEM((blocks * tokens, tokens), F32)],
        compiler_params=params(48),
        name="attend_back",
    )(queries, *pairs, info, attended, logs, grad)


def post_kernel(
    shift, state, attended, out_w, gain, router, active, gate_w, up_w, down_w,
    state_out, normed, gate_out, up_out, hidden_out, midway_out, update_out, routed,
    branch, total,
):
    pieces, cols = down_w.shape[0], down_w.shape[2]
    step = pl.program_id(0)

    @pl.when(step == 0)
    def _():
        for piece in range(pieces):
            made = dot(attended[...], out_w[piece])
            branch[:, piece * cols : (piece + 1) * cols] = made[:, shift : shift + cols]
        midway = state[...] + branch[...]
        midway_out[...] = midway
        inverse = lax.rsqrt(jnp.mean(midway * midway, axis=-1, keepdims=True) + epsilon)
        normed[...] = (midway * inverse * gain[...]).astype(BF)
        total[...] = jnp.zeros(total.shape, F32)

    low = normed[...]
    gate = dot(low, gate_w[0])
    up = dot(low, up_w[0])
    gate_out[0] = gate.astype(BF)
    up_out[0] = up.astype(BF)
    hidden = (gate / (1.0 + jnp.exp(-gate)) * up).astype(BF)
    hidden_out[0] = hidden
    for piece in range(pieces):
        total[piece] += dot(hidden, down_w[piece])

    @pl.when(step == pl.num_programs(0) - 1)
    def _():
        for piece in range(pieces):
            span = slice(piece * cols, (piece + 1) * cols)
            branch[:, span] = branch[:, span] + total[piece]
        update = branch[...]
        update_out[...] = update
        before = state[...]
        chance = 1.0 / (1.0 + jnp.exp(-jnp.sum(before * router[...], axis=-1, keepdims=True)))
        routed[...] = jnp.broadcast_to(chance, routed.shape)
        state_out[...] = before + (active[:, 0:1] * chance) * update


def post_part(state, attended, out_w, gain, router, active, gate_w, up_w, down_w, shift):
    tokens, width = state.shape
    pieces, _, part = gate_w.shape
    cols = down_w.shape[2]

    def whole(*dims):
        return pl.BlockSpec(dims, lambda f: (0,) * len(dims))

    chunk = pl.BlockSpec((1, tokens, part), lambda f: (f, 0, 0))
    weight = pl.BlockSpec((1, width, part), lambda f: (f, 0, 0))
    row = whole(tokens, width)
    return pl.pallas_call(
        functools.partial(post_kernel, shift),
        grid=(pieces,),
        out_shape=(
            shape((tokens, width), F32),
            shape((tokens, width), BF),
            shape((pieces, tokens, part), BF),
            shape((pieces, tokens, part), BF),
            shape((pieces, tokens, part), BF),
            shape((tokens, width), F32),
            shape((tokens, width), F32),
            shape((tokens, LANE), F32),
        ),
        in_specs=[
            row, whole(tokens, QW), whole(*out_w.shape), whole(1, width), whole(1, width),
            whole(tokens, LANE), weight, weight,
            pl.BlockSpec((pieces, part, cols), lambda f: (0, f, 0)),
        ],
        out_specs=(row, row, chunk, chunk, chunk, row, row, whole(tokens, LANE)),
        scratch_shapes=[pltpu.VMEM((tokens, width), F32), pltpu.VMEM((pieces, tokens, cols), F32)],
        compiler_params=params(48),
        name="post",
    )(state, attended, out_w, gain, router, active, gate_w, up_w, down_w)


def post_back_kernel(
    shift, grad_state, update, routed, active, state, midway, gain, router, out_w, gate_pre, up_pre,
    gate_w, up_w, down_w,
    grad_ffn, grad_gate_out, grad_up_out, grad_branch, grad_attended, partial, gain_grad, router_grad,
    total, scaled, logit,
):
    pieces, cols = down_w.shape[0], down_w.shape[2]
    step = pl.program_id(0)

    @pl.when(step == 0)
    def _():
        chance = routed[:, 0:1]
        weight = active[:, 0:1] * chance
        grad = grad_state[...]
        change = grad * weight
        scaled[...] = change
        slope = jnp.sum(grad * update[...], axis=-1, keepdims=True) * weight * (1.0 - chance)
        logit[...] = jnp.broadcast_to(slope, logit.shape)
        router_grad[...] = jnp.sum(state[...] * slope, axis=0, keepdims=True)
        low = change.astype(BF)
        for piece in range(pieces):
            grad_ffn[piece] = low[:, piece * cols : (piece + 1) * cols]
        total[...] = jnp.zeros(total.shape, F32)

    grad_hidden = dot(grad_ffn[0], down_w[0], NT)
    for piece in range(1, pieces):
        grad_hidden += dot(grad_ffn[piece], down_w[piece], NT)
    gate = gate_pre[0].astype(F32)
    chance = 1.0 / (1.0 + jnp.exp(-gate))
    smooth = gate * chance
    grad_gate = (grad_hidden * up_pre[0].astype(F32) * (chance + smooth * (1.0 - chance))).astype(BF)
    grad_up = (grad_hidden * smooth).astype(BF)
    grad_gate_out[0] = grad_gate
    grad_up_out[0] = grad_up
    total[...] += dot(grad_gate, gate_w[0], NT) + dot(grad_up, up_w[0], NT)

    @pl.when(step == pl.num_programs(0) - 1)
    def _():
        grad_midway, grad_gain = norm_back(total[...], midway[...], gain[...])
        gain_grad[...] = grad_gain
        partial[...] = grad_state[...] + logit[:, 0:1] * router[...] + grad_midway
        low = (scaled[...] + grad_midway).astype(BF)
        grad = None
        for piece in range(pieces):
            if grad_branch.shape[2] > cols:
                grad_branch[piece] = jnp.zeros(grad_branch.shape[1:], BF)
            grad_branch[piece, :, shift : shift + cols] = low[:, piece * cols : (piece + 1) * cols]
            made = dot(grad_branch[piece], out_w[piece], NT)
            grad = made if grad is None else grad + made
        grad_attended[...] = grad.astype(BF)


def post_back(
    grad_state, update, routed, active, state, midway, gain, router, out_w, gate_pre, up_pre,
    gate_w, up_w, down_w, shift,
):
    tokens, width = state.shape
    pieces, _, part = gate_w.shape
    cols = down_w.shape[2]

    def whole(*dims):
        return pl.BlockSpec(dims, lambda f: (0,) * len(dims))

    chunk = pl.BlockSpec((1, tokens, part), lambda f: (f, 0, 0))
    weight = pl.BlockSpec((1, width, part), lambda f: (f, 0, 0))
    row, thin, line = whole(tokens, width), whole(tokens, LANE), whole(1, width)
    branch_dims = (pieces, tokens, out_w.shape[2])
    return pl.pallas_call(
        functools.partial(post_back_kernel, shift),
        grid=(pieces,),
        out_shape=(
            shape((pieces, tokens, cols), BF),
            shape((pieces, tokens, part), BF),
            shape((pieces, tokens, part), BF),
            shape(branch_dims, BF),
            shape((tokens, QW), BF),
            shape((tokens, width), F32),
            shape((1, width), F32),
            shape((1, width), F32),
        ),
        in_specs=[
            row, row, thin, thin, row, row, line, line, whole(*out_w.shape), chunk, chunk,
            weight, weight, pl.BlockSpec((pieces, part, cols), lambda f: (0, f, 0)),
        ],
        out_specs=(
            whole(pieces, tokens, cols), chunk, chunk, whole(*branch_dims), whole(tokens, QW),
            row, line, line,
        ),
        scratch_shapes=[
            pltpu.VMEM((tokens, width), F32),
            pltpu.VMEM((tokens, width), F32),
            pltpu.VMEM((tokens, LANE), F32),
        ],
        compiler_params=params(48),
        name="post_back",
    )(grad_state, update, routed, active, state, midway, gain, router, out_w, gate_pre, up_pre,
      gate_w, up_w, down_w)


def pre_back_kernel(cols, blocks, *refs):
    qc, kc = cols
    grad_queries, own, others = refs[0], refs[1], refs[2 : 1 + blocks]
    partial, state, gain, weight, cosine, sine = refs[1 + blocks : 7 + blocks]
    packed, grad_state, gain_grad, qbuf, kbuf = refs[7 + blocks :]
    summed = own[...]
    for ref in others:
        summed = summed + ref[...].astype(F32)
    kbuf[:, :KW] = summed[:, :KW]
    qbuf[:, :QW] = grad_queries[...]
    for buf in (qbuf, kbuf):
        for start in range(0, buf.shape[1], LANE):
            span = slice(start, start + LANE)
            buf[:, span] = turn(buf[:, span], cosine[...], -sine[...])
    low_q = qbuf[...].astype(BF)
    low_k = kbuf[...].astype(BF)
    low_v = summed[:, KW:].astype(BF)
    total = None
    for piece in range(weight.shape[0]):
        packed[piece] = jnp.zeros(packed.shape[1:], BF)
        packed[piece, :, :qc] = low_q[:, piece * qc : (piece + 1) * qc]
        packed[piece, :, qc : qc + kc] = low_k[:, piece * kc : (piece + 1) * kc]
        packed[piece, :, qc + kc : qc + 2 * kc] = low_v[:, piece * kc : (piece + 1) * kc]
        made = dot(packed[piece], weight[piece], NT)
        total = made if total is None else total + made
    grad_in, grad_gain = norm_back(total, state[...], gain[...])
    gain_grad[...] = grad_gain
    grad_state[...] = partial[...] + grad_in


def pre_back(grad_queries, grad_pairs, partial, state, gain, weight, cosine, sine, cols):
    tokens, width = state.shape
    return pl.pallas_call(
        functools.partial(pre_back_kernel, cols, len(grad_pairs)),
        out_shape=(
            shape((weight.shape[0], tokens, weight.shape[2]), BF),
            shape((tokens, width), F32),
            shape((1, width), F32),
        ),
        in_specs=[vmem] * (7 + len(grad_pairs)),
        out_specs=(vmem,) * 3,
        scratch_shapes=[
            pltpu.VMEM((tokens, ceil_to(QW, LANE)), F32),
            pltpu.VMEM((tokens, ceil_to(KW, LANE)), F32),
        ],
        compiler_params=params(40),
        name="pre_back",
    )(grad_queries, *grad_pairs, partial, state, gain, weight, cosine, sine)


def attn_sums_kernel(count, low_col, *refs):
    normed, packed = refs[:count], refs[count : 2 * count]
    attended, branch = refs[2 * count : 3 * count], refs[3 * count : 4 * count]
    out, left, right = refs[4 * count :]

    @pl.when(pl.program_id(0) == 0)
    def _():
        left[...] = jnp.concatenate([ref[...].T for ref in normed], axis=1)
        right[...] = jnp.concatenate([ref[...].T for ref in attended], axis=1)

    first = dot(left[...], jnp.concatenate([ref[0] for ref in packed], axis=0))
    second = dot(right[...], jnp.concatenate([ref[0] for ref in branch], axis=0))
    high_col = first.shape[1]
    if low_col:
        out[0, :, :low_col] = first[:, :low_col].astype(BF)
    out[0, :, low_col:high_col] = (first[:, low_col:] + second[:, : high_col - low_col]).astype(BF)
    if high_col < out.shape[2]:
        out[0, :, high_col:] = second[:, high_col - low_col :].astype(BF)


def attn_sums(normed, packed, attended, branch, low_col, total_cols):
    count = len(normed)
    tokens, width = normed[0].shape
    pieces = packed[0].shape[0]
    row = pl.BlockSpec((tokens, width), lambda s: (0, 0))
    part = pl.BlockSpec((1, tokens, packed[0].shape[2]), lambda s: (s, 0, 0))
    thin = pl.BlockSpec((1, tokens, branch[0].shape[2]), lambda s: (s, 0, 0))
    return pl.pallas_call(
        functools.partial(attn_sums_kernel, count, low_col),
        grid=(pieces,),
        out_shape=shape((pieces, width, total_cols), BF),
        in_specs=[row] * count + [part] * count + [row] * count + [thin] * count,
        out_specs=pl.BlockSpec((1, width, total_cols), lambda s: (s, 0, 0)),
        scratch_shapes=[pltpu.VMEM((width, count * tokens), BF)] * 2,
        compiler_params=params(56),
        name="attn_sums",
    )(*normed, *packed, *attended, *branch)


def pair_sums_kernel(count, *refs):
    normed, first, second = refs[:count], refs[count : 2 * count], refs[2 * count : 3 * count]
    first_out, second_out, left = refs[3 * count :]

    @pl.when(pl.program_id(0) == 0)
    def _():
        left[...] = jnp.concatenate([ref[...].T for ref in normed], axis=1)

    for source, out in ((first, first_out), (second, second_out)):
        out[0] = dot(left[...], jnp.concatenate([ref[0] for ref in source], axis=0)).astype(BF)


def pair_sums(normed, first, second):
    count = len(normed)
    tokens, width = normed[0].shape
    pieces, _, part = first[0].shape
    row = pl.BlockSpec((tokens, width), lambda s: (0, 0))
    chunk = pl.BlockSpec((1, tokens, part), lambda s: (s, 0, 0))
    result = pl.BlockSpec((1, width, part), lambda s: (s, 0, 0))
    return pl.pallas_call(
        functools.partial(pair_sums_kernel, count),
        grid=(pieces,),
        out_shape=(shape((pieces, width, part), BF),) * 2,
        in_specs=[row] * count + [chunk] * (2 * count),
        out_specs=(result, result),
        scratch_shapes=[pltpu.VMEM((width, count * tokens), BF)],
        compiler_params=params(56),
        name="pair_sums",
    )(*normed, *first, *second)


def down_sums_kernel(count, *refs):
    hidden, grads, out, right = refs[:count], refs[count : 2 * count], refs[-2], refs[-1]

    @pl.when(pl.program_id(0) == 0)
    def _():
        for piece in range(out.shape[0]):
            right[piece] = jnp.concatenate([ref[piece] for ref in grads], axis=0)

    left = jnp.concatenate([ref[0].T for ref in hidden], axis=1)
    for piece in range(out.shape[0]):
        out[piece] = dot(left, right[piece]).astype(BF)


def down_sums(hidden, grads):
    count = len(hidden)
    pieces, tokens, part = hidden[0].shape
    cols = grads[0].shape[2]
    return pl.pallas_call(
        functools.partial(down_sums_kernel, count),
        grid=(pieces,),
        out_shape=shape((pieces, pieces * part, cols), BF),
        in_specs=[pl.BlockSpec((1, tokens, part), lambda f: (f, 0, 0))] * count
        + [pl.BlockSpec((pieces, tokens, cols), lambda f: (0, 0, 0))] * count,
        out_specs=pl.BlockSpec((pieces, part, cols), lambda f: (0, f, 0)),
        scratch_shapes=[pltpu.VMEM((pieces, count * tokens, cols), BF)],
        compiler_params=params(56),
        name="down_sums",
    )(*hidden, *grads)


MESH = pl.DeviceIdType.MESH


class Place:
    def __init__(self, layers):
        dp, seq = lax.axis_index("dp"), lax.axis_index("seq")
        self.layers = layers
        self.z, self.core = lax.div(dp, 2), lax.rem(dp, 2)
        self.y, self.x = lax.div(seq, 2), lax.rem(seq, 2)
        self.sibling = (self.z * 2 + 1 - self.core, seq)
        self.over_x = (dp, self.y * 2 + 1 - self.x)
        self.over_y = (dp, (1 - self.y) * 2 + self.x)
        self.up = [(lax.rem(self.z + k, layers) * 2 + self.core, seq) for k in range(layers)]
        self.down = [
            (lax.rem(self.z + layers - k, layers) * 2 + self.core, seq) for k in range(layers)
        ]
        self.peers = [self.sibling, self.over_x, self.over_y] + self.up[1:]

    def greet(self):
        barrier = pltpu.get_barrier_semaphore()
        for peer in self.peers:
            pl.semaphore_signal(barrier, inc=1, device_id=peer, device_id_type=MESH)
        pl.semaphore_wait(barrier, len(self.peers))


def remote(source, target, sems, peer):
    return pltpu.make_async_remote_copy(
        src_ref=source, dst_ref=target, send_sem=sems[0], recv_sem=sems[1],
        device_id=peer, device_id_type=MESH,
    )


def gather_kernel(count, layers, *refs):
    ins, outs = refs[:count], refs[count : 2 * count]
    send, recv, keep = refs[2 * count :]
    here = Place(layers)
    here.greet()
    y, x, z, core = here.y, here.x, here.z, here.core
    sent = []

    def slot(a, index):
        return send.at[a, index], recv.at[a, index]

    def start(a, index, source, target, peer):
        copy = remote(source, target, slot(a, index), peer)
        copy.start()
        sent.append(copy)

    def arrive(a, index, landing):
        remote(landing, landing, slot(a, index), here.sibling).wait_recv()

    def layer(k):
        return lax.rem(z + layers - k, layers)

    def sides(a):
        if a % 2 == 0:
            return here.over_x, here.over_y, (y, 1 - x), ((1 - y, x), (1 - y, 1 - x))
        return here.over_y, here.over_x, (1 - y, x), ((y, 1 - x), (1 - y, 1 - x))

    own = [pltpu.make_async_copy(ins[a], outs[a].at[y, x, z, core], keep.at[a]) for a in range(count)]
    for copy in own:
        copy.start()

    def first(k):
        for a in range(count):
            spot = outs[a].at[y, x, layer(k), core]
            source = ins[a] if k == 0 else spot
            if k:
                arrive(a, k, spot)
            start(a, layers + k, source, spot, sides(a)[0])
            start(a, 2 * layers + k, source, spot, sides(a)[1])

    def second(k):
        for a in range(count):
            side = sides(a)[2]
            spot = outs[a].at[side[0], side[1], layer(k), core]
            arrive(a, layers + k, spot)
            start(a, 3 * layers + k, spot, spot, sides(a)[1])

    def third(k):
        for a in range(count):
            for turn_of, side in enumerate(sides(a)[3]):
                arrive(a, (2 + turn_of) * layers + k, outs[a].at[side[0], side[1], layer(k), core])
            if k == 0:
                own[a].wait()
            spot = outs[a].at[:, :, layer(k), core]
            start(a, 4 * layers + k, spot, spot, here.sibling)

    def z_sends(k):
        for a in range(count):
            start(a, k, ins[a], outs[a].at[y, x, z, core], here.up[k])

    for a in range(count):
        for k in range(1, layers):
            start(a, k, ins[a], outs[a].at[y, x, z, core], here.up[k])
    for k in range(layers + 2):
        if k < layers:
            first(k)
        if 1 <= k <= layers:
            second(k - 1)
        if k >= 2:
            third(k - 2)
    for k in range(layers):
        for a in range(count):
            arrive(a, 4 * layers + k, outs[a].at[:, :, layer(k), 1 - core])
    for copy in sent:
        copy.wait_send()


def gather_all(parts, layers):
    count = len(parts)
    anywhere = pl.BlockSpec(memory_space=pl.ANY)
    return pl.pallas_call(
        functools.partial(gather_kernel, count, layers),
        out_shape=tuple(shape((2, 2, layers, 2) + part.shape, part.dtype) for part in parts),
        in_specs=[anywhere] * count,
        out_specs=(anywhere,) * count,
        scratch_shapes=[
            pltpu.SemaphoreType.DMA((count, 5 * layers)),
            pltpu.SemaphoreType.DMA((count, 5 * layers)),
            pltpu.SemaphoreType.DMA((count,)),
        ],
        compiler_params=pltpu.CompilerParams(collective_id=0, has_side_effects=True),
        name="gather_all",
    )(*parts)


def reduce_kernel(count, layers, *refs):
    ins, outs = refs[:count], refs[count : 2 * count]
    held, core_in, first_in, second_in, done, z_in = (
        refs[(2 + i) * count : (3 + i) * count] for i in range(6)
    )
    send, recv, keep = refs[8 * count :]
    here = Place(layers)
    here.greet()
    y, x, z, core = here.y, here.x, here.z, here.core
    sent = []

    def slot(a, index):
        return send.at[a, index], recv.at[a, index]

    def start(a, index, source, target, peer):
        copy = remote(source, target, slot(a, index), peer)
        copy.start()
        sent.append(copy)

    def arrive(a, index, landing):
        remote(landing, landing, slot(a, index), here.sibling).wait_recv()

    def layer(k):
        return lax.rem(z + k + 1, layers)

    def added(ref, one, two):
        return (one.astype(F32) + two.astype(F32)).astype(ref.dtype)

    loads = [[None] * layers for _ in range(count)]
    for k in range(layers):
        for a in range(count):
            start(a, k, ins[a].at[:, :, layer(k), 1 - core], core_in[a].at[k], here.sibling)
            loads[a][k] = pltpu.make_async_copy(
                ins[a].at[:, :, layer(k), core], held[a].at[k], keep.at[a, k]
            )
            loads[a][k].start()

    def first(k):
        for a in range(count):
            loads[a][k].wait()
            arrive(a, k, core_in[a].at[k])
            held[a][k] = added(held[a], held[a][k], core_in[a][k])
            if a % 2 == 0:
                start(a, layers + k, held[a].at[k, :, 1 - x], first_in[a].at[k], here.over_x)
            else:
                start(a, layers + k, held[a].at[k, 1 - y], first_in[a].at[k], here.over_y)

    def second(k):
        for a in range(count):
            arrive(a, layers + k, first_in[a].at[k])
            for i in range(2):
                if a % 2 == 0:
                    held[a][k, i, x] = added(held[a], held[a][k, i, x], first_in[a][k, i])
                else:
                    held[a][k, y, i] = added(held[a], held[a][k, y, i], first_in[a][k, i])
            if a % 2 == 0:
                start(a, 2 * layers + k, held[a].at[k, 1 - y, x], second_in[a].at[k], here.over_y)
            else:
                start(a, 2 * layers + k, held[a].at[k, y, 1 - x], second_in[a].at[k], here.over_x)

    def third(k):
        for a in range(count):
            arrive(a, 2 * layers + k, second_in[a].at[k])
            done[a][k] = added(held[a], held[a][k, y, x], second_in[a][k])
            if k < layers - 1:
                start(a, 3 * layers + k, done[a].at[k], z_in[a].at[k], here.up[k + 1])

    for k in range(layers + 2):
        if k < layers:
            first(k)
        if 1 <= k <= layers:
            second(k - 1)
        if k >= 2:
            third(k - 2)
    for a in range(count):
        total = done[a][layers - 1].astype(F32)
        for k in range(layers - 1):
            arrive(a, 3 * layers + k, z_in[a].at[k])
            total = total + z_in[a][k].astype(F32)
        outs[a][...] = total
    for copy in sent:
        copy.wait_send()


def reduce_all(parts):
    count = len(parts)
    layers = parts[0].shape[2]
    anywhere = pl.BlockSpec(memory_space=pl.ANY)

    def buffers(*lead):
        return [pltpu.VMEM(lead + part.shape[4:], part.dtype) for part in parts]

    return pl.pallas_call(
        functools.partial(reduce_kernel, count, layers),
        out_shape=tuple(shape(part.shape[4:], F32) for part in parts),
        in_specs=[anywhere] * count,
        out_specs=(vmem,) * count,
        scratch_shapes=[
            *buffers(layers, 2, 2),
            *buffers(layers, 2, 2),
            *buffers(layers, 2),
            *buffers(layers),
            *buffers(layers),
            *buffers(layers - 1),
            pltpu.SemaphoreType.DMA((count, 4 * layers)),
            pltpu.SemaphoreType.DMA((count, 4 * layers)),
            pltpu.SemaphoreType.DMA((count, layers)),
        ],
        compiler_params=pltpu.CompilerParams(
            collective_id=1, has_side_effects=True, vmem_limit_bytes=56 * MIB
        ),
        name="reduce_all",
    )(*parts)


def rope_tables(tokens):
    half = HEAD_DIM // 2
    frequency = rope_base ** (-(jnp.arange(half, dtype=F32) * 2.0 / HEAD_DIM))
    positions = lax.axis_index("seq") * tokens + jnp.arange(tokens, dtype=jnp.int32)
    angles = positions.astype(F32)[:, None] * frequency[None, :]
    cosine, sine = jnp.cos(angles), jnp.sin(angles)
    repeat = LANE // HEAD_DIM
    return (
        jnp.concatenate([cosine, cosine] * repeat, axis=1),
        jnp.concatenate([-sine, sine] * repeat, axis=1),
    )


def pass_on(array, step, count):
    return lax.ppermute(array, "seq", [(i, i + step) for i in range(count - step)])


def pass_back(array, step, count):
    return lax.ppermute(array, "seq", [(i + step, i) for i in range(count - step)])


def local(
    inputs, cotangent, segments, depths, query_weight, key_weight, value_weight, out_weight,
    gate_weight, up_weight, down_weight, attn_gain, ffn_gain, router_weight,
):
    micros, _, tokens, width = inputs.shape
    seq, ranks = lax.axis_size("seq"), lax.axis_size("dp")
    mine = lax.axis_index("seq")
    rows = query_weight.shape[0]
    qc, kc = query_weight.shape[1], key_weight.shape[1]
    cols = (qc, kc)

    attn_local = jnp.concatenate([query_weight, key_weight, value_weight, out_weight], axis=1)
    both = ("seq", "dp")

    span = ceil_to(max(rows, tokens), LANE)
    small = jnp.concatenate([attn_gain[None], ffn_gain[None], router_weight.T], axis=0).astype(F32)
    marks = jnp.concatenate([segments[:, 0], depths[:, 0]], axis=0).astype(F32)
    small = jnp.concatenate(
        [
            jnp.pad(small, ((0, 8 - small.shape[0]), (0, span - rows))),
            jnp.pad(marks, ((0, ceil_to(2 * micros, 8) - 2 * micros), (0, span - tokens))),
        ],
        axis=0,
    )
    parts = (attn_local, gate_weight, up_weight, down_weight, small)
    direct = seq == 4 and ranks % 2 == 0
    if direct:
        gathered = gather_all(parts, ranks // 2)
    else:
        gathered = [lax.all_gather(part, both, axis=0, tiled=False) for part in parts]
    attn_w, gate_w, up_w, down_w = (
        full.reshape(seq, -1, full.shape[-1]) for full in gathered[:4]
    )
    small = gathered[4].reshape(seq, ranks, *small.shape)
    marks = lax.dynamic_index_in_dim(small, lax.axis_index("dp"), 1, keepdims=False)
    marks = marks[:, 8 : 8 + 2 * micros, :tokens].reshape(seq, 2, micros, tokens)
    small = small[0, :, : 2 + RECUR, :rows].transpose(1, 0, 2).reshape(2 + RECUR, width)
    attn_g, ffn_g = small[0:1], small[1:2]
    routers = [small[2 + r : 3 + r] for r in range(RECUR)]
    used = qc + 2 * kc
    total_cols = attn_w.shape[2]
    high_col = min(ceil_to(used, LANE), total_cols)
    low_col = used // LANE * LANE
    shift = used - low_col
    qkv_w, out_w = attn_w[:, :, :high_col], attn_w[:, :, low_col:]

    order = mine - jnp.arange(seq)
    marks = jnp.where((order >= 0)[:, None, None, None], marks[order % seq], -1.0)
    marks = marks.transpose(2, 1, 0, 3).reshape(micros, 2, seq * tokens)
    infos = [jnp.pad(marks[m], ((0, 6), (0, 0))) for m in range(micros)]
    cosine, sine = rope_tables(tokens)

    states = [inputs[m, 0] for m in range(micros)]
    actives = [
        [
            jnp.broadcast_to((depths[m, 0] > r).astype(F32)[:, None], (tokens, LANE))
            for r in range(RECUR)
        ]
        for m in range(micros)
    ]
    saved = [[None] * RECUR for _ in range(micros)]
    for r in range(RECUR):
        made = []
        for m in range(micros):
            normed, queries, pair = pre_part(states[m], attn_g, qkv_w, cosine, sine, cols)
            pairs = [pair] + [pass_on(pair, step, seq) for step in range(1, seq)]
            made.append((normed, queries, pairs))
        for m in range(micros):
            normed, queries, pairs = made[m]
            attended, logs = attend(queries, pairs, infos[m], r)
            state_out, ffn_in, gate, up, hidden, midway, update, routed = post_part(
                states[m], attended, out_w, ffn_g, routers[r], actives[m][r], gate_w, up_w, down_w, shift
            )
            saved[m][r] = dict(
                state=states[m], normed=normed, queries=queries, pairs=pairs, attended=attended,
                logs=logs, ffn_in=ffn_in, gate=gate, up=up, hidden=hidden, midway=midway,
                update=update, routed=routed,
            )
            states[m] = state_out

    grads = [cotangent[m, 0] for m in range(micros)]
    attn_gain_sum, ffn_gain_sum, router_sums = 0.0, 0.0, [0.0] * RECUR
    for r in reversed(range(RECUR)):
        partials = []
        for m in range(micros):
            s = saved[m][r]
            grad_ffn, grad_gate, grad_up, grad_branch, grad_attended, partial, gain_grad, router_grad = (
                post_back(
                    grads[m], s["update"], s["routed"], actives[m][r], s["state"], s["midway"], ffn_g,
                    routers[r], out_w, s["gate"], s["up"], gate_w, up_w, down_w, shift,
                )
            )
            ffn_gain_sum = ffn_gain_sum + gain_grad
            router_sums[r] = router_sums[r] + router_grad
            s.update(grad_ffn=grad_ffn, grad_gate=grad_gate, grad_up=grad_up, grad_branch=grad_branch)
            grad_queries, *grad_pairs = attend_back(
                s["queries"], s["pairs"], infos[m], s["attended"], s["logs"], grad_attended, r
            )
            grad_pairs = [grad_pairs[0]] + [
                pass_back(grad_pairs[step], step, seq) for step in range(1, seq)
            ]
            partials.append((partial, grad_queries, grad_pairs))
        for m in range(micros):
            s = saved[m][r]
            partial, grad_queries, grad_pairs = partials[m]
            packed, grads[m], gain_grad = pre_back(
                grad_queries, grad_pairs, partial, s["state"], attn_g, qkv_w, cosine, sine, cols
            )
            attn_gain_sum = attn_gain_sum + gain_grad
            s.update(packed=packed)

    flat = [saved[m][r] for r in reversed(range(RECUR)) for m in range(micros)]

    def every(name):
        return [s[name] for s in flat]

    down_sum = down_sums(every("hidden"), every("grad_ffn"))
    gate_sum, up_sum = pair_sums(every("ffn_in"), every("grad_gate"), every("grad_up"))
    attn_sum = attn_sums(
        every("normed"), every("packed"), every("attended"), every("grad_branch"), low_col, total_cols
    )

    small_sum = jnp.concatenate([attn_gain_sum, ffn_gain_sum, *router_sums], axis=0)
    small_sum = small_sum.reshape(2 + RECUR, ranks, rows).transpose(1, 0, 2)
    small_sum = jnp.pad(
        small_sum, ((0, 0), (0, 8 - small_sum.shape[1]), (0, ceil_to(rows, LANE) - rows))
    )
    small_sum = jnp.broadcast_to(small_sum[None], (seq,) + small_sum.shape)
    sums = [
        part.reshape(seq, ranks, -1, part.shape[-1])
        for part in (attn_sum, gate_sum, up_sum, down_sum, small_sum)
    ]
    if direct:
        sums = reduce_all([part.reshape(2, 2, ranks // 2, 2, *part.shape[2:]) for part in sums])
    else:
        sums = [lax.psum_scatter(part, "seq", scatter_dimension=0) for part in sums]
        sums = [lax.psum_scatter(part, "dp", scatter_dimension=0).astype(F32) for part in sums]
    attn_grad, gate_grad, up_grad, down_grad, small_own = sums
    small_own = small_own[: 2 + RECUR, :rows]

    outputs = jnp.stack(states, axis=0)[:, None]
    input_grad = jnp.stack(grads, axis=0)[:, None]
    return (
        outputs,
        input_grad,
        attn_grad[:, :qc],
        attn_grad[:, qc : qc + kc],
        attn_grad[:, qc + kc : used],
        attn_grad[:, used:],
        gate_grad,
        up_grad,
        down_grad,
        small_own[0],
        small_own[1],
        small_own[2:].T,
    )


def solution(mesh):
    data = P(None, "dp", "seq", None)
    marks = P(None, "dp", "seq")
    weight = P("dp", "seq")
    in_specs = (data, data, marks, marks) + (weight,) * 7 + (P("dp"), P("dp"), P("dp", None))
    out_specs = (data, data) + (weight,) * 7 + (P("dp"), P("dp"), P("dp", None))
    return jax.shard_map(local, mesh=mesh, in_specs=in_specs, out_specs=out_specs, check_vma=False)
```

```python
import functools

import jax
import jax.numpy as jnp
from jax import lax
from jax.experimental import pallas as pl
from jax.experimental.pallas import tpu as pltpu
from jax.sharding import PartitionSpec as P

HEADS = 15
KV_HEADS = 5
HEAD_DIM = 64
RECUR = 3
GROUP = HEADS // KV_HEADS
KW = KV_HEADS * HEAD_DIM
QW = HEADS * HEAD_DIM
LANE = 128
MIB = 2**20

epsilon = 1e-05
rope_base = 10000.0

NN = (((1,), (0,)), ((), ()))
NT = (((1,), (1,)), ((), ()))
BF = jnp.bfloat16
F32 = jnp.float32

vmem = pl.BlockSpec(memory_space=pltpu.VMEM)


def dot(left, right, dims=NN):
    return lax.dot_general(left, right, dims, preferred_element_type=F32)


def ceil_to(size, unit):
    return -(-size // unit) * unit


def shape(dims, dtype):
    return jax.ShapeDtypeStruct(dims, dtype)


def params(limit):
    return pltpu.CompilerParams(vmem_limit_bytes=limit * MIB)


def turn(block, cosine, sine):
    lanes = lax.broadcasted_iota(jnp.int32, block.shape, 1) % HEAD_DIM
    partner = jnp.where(
        lanes < HEAD_DIM // 2,
        pltpu.roll(block, LANE - HEAD_DIM // 2, 1),
        pltpu.roll(block, HEAD_DIM // 2, 1),
    )
    return block * cosine + partner * sine


def norm_back(grad_out, values_in, gain):
    inverse = lax.rsqrt(jnp.mean(values_in * values_in, axis=-1, keepdims=True) + epsilon)
    weighted = grad_out * gain
    inner = jnp.mean(weighted * values_in, axis=-1, keepdims=True)
    grad_gain = jnp.sum(grad_out * values_in * inverse, axis=0, keepdims=True)
    return weighted * inverse - values_in * (inverse * inverse * inverse * inner), grad_gain


def pre_kernel(cols, state, gain, weight, cosine, sine, normed, queries, pair, qbuf, kbuf):
    qc, kc = cols
    values_in = state[...]
    inverse = lax.rsqrt(jnp.mean(values_in * values_in, axis=-1, keepdims=True) + epsilon)
    low = (values_in * inverse * gain[...]).astype(BF)
    normed[...] = low
    for piece in range(weight.shape[0]):
        made = dot(low, weight[piece])
        qbuf[:, piece * qc : (piece + 1) * qc] = made[:, :qc]
        kbuf[:, piece * kc : (piece + 1) * kc] = made[:, qc : qc + kc]
        pair[:, KW + piece * kc : KW + (piece + 1) * kc] = made[:, qc + kc : qc + 2 * kc].astype(BF)
    for buf, out, width, scale in ((qbuf, queries, QW, HEAD_DIM**-0.5), (kbuf, pair, KW, 1.0)):
        for start in range(0, width, LANE):
            stop = min(start + LANE, width)
            turned = turn(buf[:, start : start + LANE], cosine[...], sine[...]) * scale
            out[:, start:stop] = turned[:, : stop - start].astype(BF)


def pre_part(state, gain, weight, cosine, sine, cols):
    tokens, width = state.shape
    return pl.pallas_call(
        functools.partial(pre_kernel, cols),
        out_shape=(
            shape((tokens, width), BF),
            shape((tokens, QW), BF),
            shape((tokens, 2 * KW), BF),
        ),
        in_specs=[vmem] * 5,
        out_specs=(vmem,) * 3,
        scratch_shapes=[
            pltpu.VMEM((tokens, ceil_to(QW, LANE)), F32),
            pltpu.VMEM((tokens, ceil_to(KW, LANE)), F32),
        ],
        compiler_params=params(40),
        name="pre",
    )(state, gain, weight, cosine, sine)


def fill_bias(info, bias, recursion):
    keys, tokens = bias.shape
    columns = info[...].T
    place = lax.broadcasted_iota(jnp.int32, (keys, tokens), 0)
    query = lax.broadcasted_iota(jnp.int32, (keys, tokens), 1)
    apart = place % tokens - place // tokens * tokens - query
    same = columns[:, 0:1] == info[0:1, 0:tokens]
    live = columns[:, 1:2] > recursion
    seen = same & (((apart < 0) & live) | (apart == 0))
    bias[...] = jnp.where(seen, 0.0, -1e30)


def head_cols(head):
    return slice(head * HEAD_DIM, (head + 1) * HEAD_DIM)


def stack_heads(ref, group):
    heads = range(group * GROUP, (group + 1) * GROUP)
    return jnp.concatenate([ref[:, head_cols(head)] for head in heads], axis=0)


def attend_kernel(blocks, recursion, *refs):
    queries, pairs = refs[0], refs[1 : 1 + blocks]
    info, attended, logs, bias = refs[1 + blocks :]
    tokens = queries.shape[0]
    keys = blocks * tokens
    fill_bias(info, bias, recursion)
    logs[...] = jnp.zeros(logs.shape, F32)
    for group in range(KV_HEADS):
        key = jnp.concatenate([ref[:, head_cols(group)] for ref in pairs], axis=0)
        value = jnp.concatenate([ref[:, head_cols(KV_HEADS + group)] for ref in pairs], axis=0)
        value_t = jnp.concatenate([value.T, jnp.ones((16, keys), BF)], axis=0)
        query = stack_heads(queries, group)
        scores = dot(key, query, NT) + jnp.concatenate([bias[...]] * GROUP, axis=1)
        top = jnp.max(scores, axis=0, keepdims=True)
        weights = jnp.exp(scores - top).astype(BF)
        mixed = dot(value_t, weights)
        total = mixed[HEAD_DIM : HEAD_DIM + 1]
        mixed = mixed[:HEAD_DIM] * (1.0 / total)
        log_total = top + jnp.log(total)
        for offset in range(GROUP):
            head = group * GROUP + offset
            span = slice(offset * tokens, (offset + 1) * tokens)
            attended[:, head_cols(head)] = mixed[:, span].T.astype(BF)
            logs[head : head + 1, :] = log_total[:, span]


def attend(queries, pairs, info, recursion):
    tokens = queries.shape[0]
    blocks = len(pairs)
    return pl.pallas_call(
        functools.partial(attend_kernel, blocks, recursion),
        out_shape=(shape((tokens, QW), BF), shape((ceil_to(HEADS, 8), tokens), F32)),
        in_specs=[vmem] * (2 + blocks),
        out_specs=(vmem, vmem),
        scratch_shapes=[pltpu.VMEM((blocks * tokens, tokens), F32)],
        compiler_params=params(40),
        name="attend",
    )(queries, *pairs, info)


def attend_back_kernel(blocks, recursion, *refs):
    queries, pairs = refs[0], refs[1 : 1 + blocks]
    info, attended, logs, grad, grad_queries = refs[1 + blocks : 6 + blocks]
    grad_pairs, bias = refs[6 + blocks : 6 + 2 * blocks], refs[6 + 2 * blocks]
    tokens = queries.shape[0]
    fill_bias(info, bias, recursion)
    product = (attended[...].astype(F32) * grad[...].astype(F32)).T
    for group in range(KV_HEADS):
        key = jnp.concatenate([ref[:, head_cols(group)] for ref in pairs], axis=0)
        value = jnp.concatenate([ref[:, head_cols(KV_HEADS + group)] for ref in pairs], axis=0)
        key_t = key.T
        query = stack_heads(queries, group)
        grad_mixed = stack_heads(grad, group)
        heads = range(group * GROUP, (group + 1) * GROUP)
        delta = jnp.concatenate(
            [jnp.sum(product[head_cols(head)], axis=0, keepdims=True) for head in heads], axis=1
        )
        log_total = jnp.concatenate([logs[head : head + 1, :] for head in heads], axis=1)
        scores = dot(key, query, NT) + jnp.concatenate([bias[...]] * GROUP, axis=1)
        probs = jnp.exp(scores - log_total)
        grad_probs = dot(value, grad_mixed, NT)
        grad_scores = (probs * (grad_probs - delta)).astype(BF)
        grad_value = dot(probs.astype(BF), grad_mixed)
        grad_key = dot(grad_scores, query)
        grad_query = dot(key_t, grad_scores) * HEAD_DIM**-0.5
        for offset, head in enumerate(heads):
            span = slice(offset * tokens, (offset + 1) * tokens)
            grad_queries[:, head_cols(head)] = grad_query[:, span].T
        for block, ref in enumerate(grad_pairs):
            rows = slice(block * tokens, (block + 1) * tokens)
            ref[:, head_cols(group)] = grad_key[rows].astype(ref.dtype)
            ref[:, head_cols(KV_HEADS + group)] = grad_value[rows].astype(ref.dtype)


def attend_back(queries, pairs, info, attended, logs, grad, recursion):
    tokens = queries.shape[0]
    blocks = len(pairs)
    return pl.pallas_call(
        functools.partial(attend_back_kernel, blocks, recursion),
        out_shape=(shape((tokens, QW), F32), shape((tokens, 2 * KW), F32))
        + (shape((tokens, 2 * KW), BF),) * (blocks - 1),
        in_specs=[vmem] * (5 + blocks),
        out_specs=(vmem,) * (1 + blocks),
        scratch_shapes=[pltpu.VMEM((blocks * tokens, tokens), F32)],
        compiler_params=params(48),
        name="attend_back",
    )(queries, *pairs, info, attended, logs, grad)


def is_outer():
    place = lax.axis_index("seq")
    return (place == 0) | (place == 3)


def block_bias(info, bias, index, key_block, query_block, recursion, columns, diagonal):
    block = bias.shape[1]

    def span(which):
        return pl.ds(pl.multiple_of(which * block, block), block)

    same = columns[span(key_block), 0:1] == info[0:1, span(query_block)]
    seen = columns[span(key_block), 1:2] > recursion
    if diagonal:
        key = lax.broadcasted_iota(jnp.int32, (block, block), 0)
        query = lax.broadcasted_iota(jnp.int32, (block, block), 1)
        seen = ((key < query) & seen) | (key == query)
    bias[index] = jnp.where(same & seen, 0.0, -1e30)


def tall_heads(ref, rows, group):
    heads = range(group * GROUP, (group + 1) * GROUP)
    return jnp.concatenate([ref[rows, head_cols(head)] for head in heads], axis=0)


def thrice(bias):
    return jnp.concatenate([bias] * GROUP, axis=1)


def with_ones(value):
    return jnp.concatenate([value.T, jnp.ones((16, value.shape[0]), BF)], axis=0)


def own_kernel(recursion, queries, pair, info, part, columns, bias):
    block = queries.shape[0] // 2
    wide = GROUP * block
    columns[...] = info[...].T
    block_bias(info, bias, 0, 0, 0, recursion, columns, True)
    block_bias(info, bias, 1, 0, 1, recursion, columns, False)
    block_bias(info, bias, 2, 1, 1, recursion, columns, True)
    low, high = slice(0, block), slice(block, 2 * block)
    for group in range(KV_HEADS):
        kc, vc = head_cols(group), head_cols(KV_HEADS + group)
        query_low, query_high = tall_heads(queries, low, group), tall_heads(queries, high, group)
        first = dot(pair[low, kc], query_low, NT) + thrice(bias[0])
        second = dot(pair[low, kc], query_high, NT) + thrice(bias[1])
        third = dot(pair[high, kc], query_high, NT) + thrice(bias[2])
        value_low, value_high = with_ones(pair[low, vc]), with_ones(pair[high, vc])
        top = jnp.max(first, axis=0, keepdims=True)
        mixed = dot(value_low, jnp.exp(first - top).astype(BF))
        part[group, : HEAD_DIM + 8, :wide] = mixed[: HEAD_DIM + 8]
        part[group, HEAD_DIM + 8 :, :wide] = jnp.broadcast_to(top, (8, wide))
        top = jnp.maximum(
            jnp.max(second, axis=0, keepdims=True), jnp.max(third, axis=0, keepdims=True)
        )
        mixed = dot(value_low, jnp.exp(second - top).astype(BF))
        mixed += dot(value_high, jnp.exp(third - top).astype(BF))
        part[group, : HEAD_DIM + 8, wide:] = mixed[: HEAD_DIM + 8]
        part[group, HEAD_DIM + 8 :, wide:] = jnp.broadcast_to(top, (8, wide))


def attend_own(queries, pair, info, recursion):
    tokens = queries.shape[0]
    block = tokens // 2
    return pl.pallas_call(
        functools.partial(own_kernel, recursion),
        out_shape=shape((KV_HEADS, HEAD_DIM + 16, GROUP * tokens), F32),
        in_specs=[vmem] * 3,
        out_specs=vmem,
        scratch_shapes=[
            pltpu.VMEM(info.shape[::-1], F32),
            pltpu.VMEM((3, block, block), F32),
        ],
        compiler_params=params(40),
        name="attend_own",
    )(queries, pair, info)


def rest_rows(block):
    outer = is_outer()
    shift = pl.multiple_of(jnp.where(outer, block, 0), block)
    return outer, pl.ds(shift, block)


def rest_kernel(recursion, queries, pair, info, part, attended, logs, columns, bias):
    block = queries.shape[0] // 2
    wide = GROUP * block
    columns[...] = info[...].T
    outer, rows = rest_rows(block)
    fifth = jnp.where(outer, 1, 0)
    block_bias(info, bias, 0, 2, 1, recursion, columns, False)
    block_bias(info, bias, 1, 2 + fifth, fifth, recursion, columns, False)
    low, high = slice(0, block), slice(block, 2 * block)
    logs[...] = jnp.zeros(logs.shape, F32)
    for group in range(KV_HEADS):
        kc, vc = head_cols(group), head_cols(KV_HEADS + group)
        fourth = dot(pair[low, kc], tall_heads(queries, high, group), NT) + thrice(bias[0])
        fifth = dot(pair[rows, kc], tall_heads(queries, rows, group), NT) + thrice(bias[1])
        own_low, own_high = part[group, :, :wide], part[group, :, wide:]
        top_low, top_high = own_low[HEAD_DIM + 8 : HEAD_DIM + 9], own_high[HEAD_DIM + 8 : HEAD_DIM + 9]
        fifth_top = jnp.max(fifth, axis=0, keepdims=True)
        new_low = jnp.where(outer, top_low, jnp.maximum(top_low, fifth_top))
        new_high = jnp.maximum(top_high, jnp.max(fourth, axis=0, keepdims=True))
        new_high = jnp.where(outer, jnp.maximum(new_high, fifth_top), new_high)
        fourth = jnp.exp(fourth - new_high).astype(BF)
        fifth = jnp.exp(fifth - jnp.where(outer, new_high, new_low)).astype(BF)
        added_high = dot(with_ones(pair[low, vc]), fourth)[: HEAD_DIM + 8]
        added = dot(with_ones(pair[rows, vc]), fifth)[: HEAD_DIM + 8]
        mixed_low = own_low[: HEAD_DIM + 8] * jnp.exp(top_low - new_low)
        mixed_low += jnp.where(outer, 0.0, added)
        mixed_high = own_high[: HEAD_DIM + 8] * jnp.exp(top_high - new_high)
        mixed_high += added_high + jnp.where(outer, added, 0.0)
        for start, mixed, top in ((0, mixed_low, new_low), (block, mixed_high, new_high)):
            total = mixed[HEAD_DIM : HEAD_DIM + 1]
            final = mixed[:HEAD_DIM] * (1.0 / total)
            log_total = top + jnp.log(total)
            for offset in range(GROUP):
                head = group * GROUP + offset
                span = slice(offset * block, (offset + 1) * block)
                attended[start : start + block, head_cols(head)] = final[:, span].T.astype(BF)
                logs[head : head + 1, start : start + block] = log_total[:, span]


def attend_rest(queries, pair, info, part, recursion):
    tokens = queries.shape[0]
    block = tokens // 2
    return pl.pallas_call(
        functools.partial(rest_kernel, recursion),
        out_shape=(shape((tokens, QW), BF), shape((ceil_to(HEADS, 8), tokens), F32)),
        in_specs=[vmem] * 4,
        out_specs=(vmem, vmem),
        scratch_shapes=[
            pltpu.VMEM(info.shape[::-1], F32),
            pltpu.VMEM((2, block, block), F32),
        ],
        compiler_params=params(40),
        name="attend_rest",
    )(queries, pair, info, part)


def flat_row(ref, cols, group):
    heads = range(group * GROUP, (group + 1) * GROUP)
    return jnp.concatenate([ref[head : head + 1, cols] for head in heads], axis=1)


def block_back(key, value, query, grad_mixed, bias, log_total, delta):
    probs = jnp.exp(dot(key, query, NT) + thrice(bias) - log_total)
    grad_scores = (probs * (dot(value, grad_mixed, NT) - delta)).astype(BF)
    grad_value = dot(probs.astype(BF), grad_mixed)
    grad_key = dot(grad_scores, query)
    return dot(key.T, grad_scores), grad_key, grad_value


def rest_back_kernel(
    recursion, queries, pair, info, attended, logs, grad, grad_pair, part, deltas, columns, bias
):
    block = queries.shape[0] // 2
    wide = GROUP * block
    columns[...] = info[...].T
    outer, rows = rest_rows(block)
    fifth = jnp.where(outer, 1, 0)
    block_bias(info, bias, 0, 2, 1, recursion, columns, False)
    block_bias(info, bias, 1, 2 + fifth, fifth, recursion, columns, False)
    low, high = slice(0, block), slice(block, 2 * block)
    product = (attended[...].astype(F32) * grad[...].astype(F32)).T
    deltas[...] = jnp.zeros(deltas.shape, F32)
    for head in range(HEADS):
        deltas[head : head + 1, :] = jnp.sum(product[head_cols(head)], axis=0, keepdims=True)
    for group in range(KV_HEADS):
        kc, vc = head_cols(group), head_cols(KV_HEADS + group)
        query_high, key_high, value_high = block_back(
            pair[low, kc], pair[low, vc], tall_heads(queries, high, group),
            tall_heads(grad, high, group), bias[0], flat_row(logs, high, group),
            flat_row(deltas, high, group),
        )
        query, key, value = block_back(
            pair[rows, kc], pair[rows, vc], tall_heads(queries, rows, group),
            tall_heads(grad, rows, group), bias[1], flat_row(logs, rows, group),
            flat_row(deltas, rows, group),
        )
        part[group, :, :wide] = jnp.where(outer, 0.0, query)
        part[group, :, wide:] = query_high + jnp.where(outer, query, 0.0)
        grad_pair[low, kc] = (key_high + jnp.where(outer, 0.0, key)).astype(BF)
        grad_pair[low, vc] = (value_high + jnp.where(outer, 0.0, value)).astype(BF)
        grad_pair[high, kc] = jnp.where(outer, key, 0.0).astype(BF)
        grad_pair[high, vc] = jnp.where(outer, value, 0.0).astype(BF)


def attend_rest_back(queries, pair, info, attended, logs, grad, recursion):
    tokens = queries.shape[0]
    block = tokens // 2
    return pl.pallas_call(
        functools.partial(rest_back_kernel, recursion),
        out_shape=(
            shape((tokens, 2 * KW), BF),
            shape((KV_HEADS, HEAD_DIM, GROUP * tokens), F32),
            shape(logs.shape, F32),
        ),
        in_specs=[vmem] * 6,
        out_specs=(vmem,) * 3,
        scratch_shapes=[
            pltpu.VMEM(info.shape[::-1], F32),
            pltpu.VMEM((2, block, block), F32),
        ],
        compiler_params=params(48),
        name="attend_rest_back",
    )(queries, pair, info, attended, logs, grad)


def own_back_kernel(
    recursion, queries, pair, info, logs, deltas, grad, part, grad_queries, grad_pair, columns, bias
):
    block = queries.shape[0] // 2
    wide = GROUP * block
    columns[...] = info[...].T
    block_bias(info, bias, 0, 0, 0, recursion, columns, True)
    block_bias(info, bias, 1, 0, 1, recursion, columns, False)
    block_bias(info, bias, 2, 1, 1, recursion, columns, True)
    low, high = slice(0, block), slice(block, 2 * block)
    for group in range(KV_HEADS):
        kc, vc = head_cols(group), head_cols(KV_HEADS + group)
        made = []
        for index, keys, side in ((0, low, low), (1, low, high), (2, high, high)):
            made.append(
                block_back(
                    pair[keys, kc], pair[keys, vc], tall_heads(queries, side, group),
                    tall_heads(grad, side, group), bias[index], flat_row(logs, side, group),
                    flat_row(deltas, side, group),
                )
            )
        first, second, third = made
        grad_pair[low, kc] = first[1] + second[1]
        grad_pair[low, vc] = first[2] + second[2]
        grad_pair[high, kc] = third[1]
        grad_pair[high, vc] = third[2]
        query_low = (part[group, :, :wide] + first[0]) * HEAD_DIM**-0.5
        query_high = (part[group, :, wide:] + second[0] + third[0]) * HEAD_DIM**-0.5
        for start, made_query in ((0, query_low), (block, query_high)):
            for offset in range(GROUP):
                head = group * GROUP + offset
                span = slice(offset * block, (offset + 1) * block)
                grad_queries[start : start + block, head_cols(head)] = made_query[:, span].T


def attend_own_back(queries, pair, info, logs, deltas, grad, part, recursion):
    tokens = queries.shape[0]
    block = tokens // 2
    return pl.pallas_call(
        functools.partial(own_back_kernel, recursion),
        out_shape=(shape((tokens, QW), F32), shape((tokens, 2 * KW), F32)),
        in_specs=[vmem] * 7,
        out_specs=(vmem,) * 2,
        scratch_shapes=[
            pltpu.VMEM(info.shape[::-1], F32),
            pltpu.VMEM((3, block, block), F32),
        ],
        compiler_params=params(48),
        name="attend_own_back",
    )(queries, pair, info, logs, deltas, grad, part)


def post_kernel(
    shift, state, attended, out_w, gain, router, active, gate_w, up_w, down_w,
    state_out, normed, gate_out, up_out, hidden_out, midway_out, update_out, routed,
    branch, total,
):
    pieces, cols = down_w.shape[0], down_w.shape[2]
    step = pl.program_id(0)

    @pl.when(step == 0)
    def _():
        for piece in range(pieces):
            made = dot(attended[...], out_w[piece])
            branch[:, piece * cols : (piece + 1) * cols] = made[:, shift : shift + cols]
        midway = state[...] + branch[...]
        midway_out[...] = midway
        inverse = lax.rsqrt(jnp.mean(midway * midway, axis=-1, keepdims=True) + epsilon)
        normed[...] = (midway * inverse * gain[...]).astype(BF)
        total[...] = jnp.zeros(total.shape, F32)

    low = normed[...]
    gate = dot(low, gate_w[0])
    up = dot(low, up_w[0])
    gate_out[0] = gate.astype(BF)
    up_out[0] = up.astype(BF)
    hidden = (gate / (1.0 + jnp.exp(-gate)) * up).astype(BF)
    hidden_out[0] = hidden
    for piece in range(pieces):
        total[piece] += dot(hidden, down_w[piece])

    @pl.when(step == pl.num_programs(0) - 1)
    def _():
        for piece in range(pieces):
            span = slice(piece * cols, (piece + 1) * cols)
            branch[:, span] = branch[:, span] + total[piece]
        update = branch[...]
        update_out[...] = update
        before = state[...]
        chance = 1.0 / (1.0 + jnp.exp(-jnp.sum(before * router[...], axis=-1, keepdims=True)))
        routed[...] = jnp.broadcast_to(chance, routed.shape)
        state_out[...] = before + (active[:, 0:1] * chance) * update


def post_part(state, attended, out_w, gain, router, active, gate_w, up_w, down_w, shift):
    tokens, width = state.shape
    pieces, _, part = gate_w.shape
    cols = down_w.shape[2]

    def whole(*dims):
        return pl.BlockSpec(dims, lambda f: (0,) * len(dims))

    chunk = pl.BlockSpec((1, tokens, part), lambda f: (f, 0, 0))
    weight = pl.BlockSpec((1, width, part), lambda f: (f, 0, 0))
    row = whole(tokens, width)
    made = pl.pallas_call(
        functools.partial(post_kernel, shift),
        grid=(pieces,),
        out_shape=(
            shape((tokens, width), F32),
            shape((tokens, width), BF),
            shape((pieces, tokens, part), BF),
            shape((pieces, tokens, part), BF),
            shape((pieces, tokens, part), BF),
            shape((tokens, width), F32),
            shape((tokens, width), F32),
            shape((tokens, LANE), F32),
        ),
        in_specs=[
            row, whole(tokens, QW), whole(*out_w.shape), whole(1, width), whole(1, width),
            whole(tokens, LANE), weight, weight,
            pl.BlockSpec((pieces, part, cols), lambda f: (0, f, 0)),
        ],
        out_specs=(row, row, chunk, chunk, chunk, row, row, whole(tokens, LANE)),
        scratch_shapes=[pltpu.VMEM((tokens, width), F32), pltpu.VMEM((pieces, tokens, cols), F32)],
        compiler_params=params(48),
        name="post",
    )(state, attended, out_w, gain, router, active, gate_w, up_w, down_w)
    names = ("state_out", "ffn_in", "gate", "up", "hidden", "midway", "update", "routed")
    return dict(zip(names, made))


def post_back_kernel(
    shift, grad_state, update, routed, active, state, midway, gain, router, out_w, gate_pre, up_pre,
    gate_w, up_w, down_w,
    grad_ffn, grad_gate_out, grad_up_out, grad_branch, grad_attended, partial, gain_grad, router_grad,
    total, scaled, logit,
):
    pieces, cols = down_w.shape[0], down_w.shape[2]
    step = pl.program_id(0)

    @pl.when(step == 0)
    def _():
        chance = routed[:, 0:1]
        weight = active[:, 0:1] * chance
        grad = grad_state[...]
        change = grad * weight
        scaled[...] = change
        slope = jnp.sum(grad * update[...], axis=-1, keepdims=True) * weight * (1.0 - chance)
        logit[...] = jnp.broadcast_to(slope, logit.shape)
        router_grad[...] = jnp.sum(state[...] * slope, axis=0, keepdims=True)
        low = change.astype(BF)
        for piece in range(pieces):
            grad_ffn[piece] = low[:, piece * cols : (piece + 1) * cols]
        total[...] = jnp.zeros(total.shape, F32)

    grad_hidden = dot(grad_ffn[0], down_w[0], NT)
    for piece in range(1, pieces):
        grad_hidden += dot(grad_ffn[piece], down_w[piece], NT)
    gate = gate_pre[0].astype(F32)
    chance = 1.0 / (1.0 + jnp.exp(-gate))
    smooth = gate * chance
    grad_gate = (grad_hidden * up_pre[0].astype(F32) * (chance + smooth * (1.0 - chance))).astype(BF)
    grad_up = (grad_hidden * smooth).astype(BF)
    grad_gate_out[0] = grad_gate
    grad_up_out[0] = grad_up
    total[...] += dot(grad_gate, gate_w[0], NT) + dot(grad_up, up_w[0], NT)

    @pl.when(step == pl.num_programs(0) - 1)
    def _():
        grad_midway, grad_gain = norm_back(total[...], midway[...], gain[...])
        gain_grad[...] = grad_gain
        partial[...] = grad_state[...] + logit[:, 0:1] * router[...] + grad_midway
        low = (scaled[...] + grad_midway).astype(BF)
        grad = None
        for piece in range(pieces):
            if grad_branch.shape[2] > cols:
                grad_branch[piece] = jnp.zeros(grad_branch.shape[1:], BF)
            grad_branch[piece, :, shift : shift + cols] = low[:, piece * cols : (piece + 1) * cols]
            made = dot(grad_branch[piece], out_w[piece], NT)
            grad = made if grad is None else grad + made
        grad_attended[...] = grad.astype(BF)


def post_back(grad_state, s, gain, router, out_w, gate_w, up_w, down_w, shift):
    state = s["state"]
    tokens, width = state.shape
    pieces, _, part = gate_w.shape
    cols = down_w.shape[2]

    def whole(*dims):
        return pl.BlockSpec(dims, lambda f: (0,) * len(dims))

    chunk = pl.BlockSpec((1, tokens, part), lambda f: (f, 0, 0))
    weight = pl.BlockSpec((1, width, part), lambda f: (f, 0, 0))
    row, thin, line = whole(tokens, width), whole(tokens, LANE), whole(1, width)
    branch_dims = (pieces, tokens, out_w.shape[2])
    made = pl.pallas_call(
        functools.partial(post_back_kernel, shift),
        grid=(pieces,),
        out_shape=(
            shape((pieces, tokens, cols), BF),
            shape((pieces, tokens, part), BF),
            shape((pieces, tokens, part), BF),
            shape(branch_dims, BF),
            shape((tokens, QW), BF),
            shape((tokens, width), F32),
            shape((1, width), F32),
            shape((1, width), F32),
        ),
        in_specs=[
            row, row, thin, thin, row, row, line, line, whole(*out_w.shape), chunk, chunk,
            weight, weight, pl.BlockSpec((pieces, part, cols), lambda f: (0, f, 0)),
        ],
        out_specs=(
            whole(pieces, tokens, cols), chunk, chunk, whole(*branch_dims), whole(tokens, QW),
            row, line, line,
        ),
        scratch_shapes=[
            pltpu.VMEM((tokens, width), F32),
            pltpu.VMEM((tokens, width), F32),
            pltpu.VMEM((tokens, LANE), F32),
        ],
        compiler_params=params(48),
        name="post_back",
    )(grad_state, s["update"], s["routed"], s["active"], state, s["midway"], gain, router, out_w,
      s["gate"], s["up"], gate_w, up_w, down_w)
    names = (
        "grad_ffn", "grad_gate", "grad_up", "grad_branch", "grad_attended", "partial",
        "ffn_gain_grad", "router_grad",
    )
    return dict(zip(names, made))


def pre_back_kernel(cols, blocks, *refs):
    qc, kc = cols
    grad_queries, own, others = refs[0], refs[1], refs[2 : 1 + blocks]
    partial, state, gain, weight, cosine, sine = refs[1 + blocks : 7 + blocks]
    packed, grad_state, gain_grad, qbuf, kbuf = refs[7 + blocks :]
    summed = own[...]
    for ref in others:
        summed = summed + ref[...].astype(F32)
    kbuf[:, :KW] = summed[:, :KW]
    qbuf[:, :QW] = grad_queries[...]
    for buf in (qbuf, kbuf):
        for start in range(0, buf.shape[1], LANE):
            span = slice(start, start + LANE)
            buf[:, span] = turn(buf[:, span], cosine[...], -sine[...])
    low_q = qbuf[...].astype(BF)
    low_k = kbuf[...].astype(BF)
    low_v = summed[:, KW:].astype(BF)
    total = None
    for piece in range(weight.shape[0]):
        packed[piece] = jnp.zeros(packed.shape[1:], BF)
        packed[piece, :, :qc] = low_q[:, piece * qc : (piece + 1) * qc]
        packed[piece, :, qc : qc + kc] = low_k[:, piece * kc : (piece + 1) * kc]
        packed[piece, :, qc + kc : qc + 2 * kc] = low_v[:, piece * kc : (piece + 1) * kc]
        made = dot(packed[piece], weight[piece], NT)
        total = made if total is None else total + made
    grad_in, grad_gain = norm_back(total, state[...], gain[...])
    gain_grad[...] = grad_gain
    grad_state[...] = partial[...] + grad_in


def pre_back(grad_queries, grad_pairs, partial, state, gain, weight, cosine, sine, cols):
    tokens, width = state.shape
    return pl.pallas_call(
        functools.partial(pre_back_kernel, cols, len(grad_pairs)),
        out_shape=(
            shape((weight.shape[0], tokens, weight.shape[2]), BF),
            shape((tokens, width), F32),
            shape((1, width), F32),
        ),
        in_specs=[vmem] * (7 + len(grad_pairs)),
        out_specs=(vmem,) * 3,
        scratch_shapes=[
            pltpu.VMEM((tokens, ceil_to(QW, LANE)), F32),
            pltpu.VMEM((tokens, ceil_to(KW, LANE)), F32),
        ],
        compiler_params=params(40),
        name="pre_back",
    )(grad_queries, *grad_pairs, partial, state, gain, weight, cosine, sine)


def attn_sums_kernel(count, low_col, *refs):
    normed, packed = refs[:count], refs[count : 2 * count]
    attended, branch = refs[2 * count : 3 * count], refs[3 * count : 4 * count]
    out, left, right = refs[4 * count :]

    @pl.when(pl.program_id(0) == 0)
    def _():
        left[...] = jnp.concatenate([ref[...].T for ref in normed], axis=1)
        right[...] = jnp.concatenate([ref[...].T for ref in attended], axis=1)

    first = dot(left[...], jnp.concatenate([ref[0] for ref in packed], axis=0))
    second = dot(right[...], jnp.concatenate([ref[0] for ref in branch], axis=0))
    high_col = first.shape[1]
    if low_col:
        out[0, :, :low_col] = first[:, :low_col].astype(BF)
    out[0, :, low_col:high_col] = (first[:, low_col:] + second[:, : high_col - low_col]).astype(BF)
    if high_col < out.shape[2]:
        out[0, :, high_col:] = second[:, high_col - low_col :].astype(BF)


def attn_sums(normed, packed, attended, branch, low_col, total_cols):
    count = len(normed)
    tokens, width = normed[0].shape
    pieces = packed[0].shape[0]
    row = pl.BlockSpec((tokens, width), lambda s: (0, 0))
    part = pl.BlockSpec((1, tokens, packed[0].shape[2]), lambda s: (s, 0, 0))
    thin = pl.BlockSpec((1, tokens, branch[0].shape[2]), lambda s: (s, 0, 0))
    return pl.pallas_call(
        functools.partial(attn_sums_kernel, count, low_col),
        grid=(pieces,),
        out_shape=shape((pieces, width, total_cols), BF),
        in_specs=[row] * count + [part] * count + [row] * count + [thin] * count,
        out_specs=pl.BlockSpec((1, width, total_cols), lambda s: (s, 0, 0)),
        scratch_shapes=[pltpu.VMEM((width, count * tokens), BF)] * 2,
        compiler_params=params(56),
        name="attn_sums",
    )(*normed, *packed, *attended, *branch)


def pair_sums_kernel(count, *refs):
    normed, first, second = refs[:count], refs[count : 2 * count], refs[2 * count : 3 * count]
    first_out, second_out, left = refs[3 * count :]

    @pl.when(pl.program_id(0) == 0)
    def _():
        left[...] = jnp.concatenate([ref[...].T for ref in normed], axis=1)

    for source, out in ((first, first_out), (second, second_out)):
        out[0] = dot(left[...], jnp.concatenate([ref[0] for ref in source], axis=0)).astype(BF)


def pair_sums(normed, first, second):
    count = len(normed)
    tokens, width = normed[0].shape
    pieces, _, part = first[0].shape
    row = pl.BlockSpec((tokens, width), lambda s: (0, 0))
    chunk = pl.BlockSpec((1, tokens, part), lambda s: (s, 0, 0))
    result = pl.BlockSpec((1, width, part), lambda s: (s, 0, 0))
    return pl.pallas_call(
        functools.partial(pair_sums_kernel, count),
        grid=(pieces,),
        out_shape=(shape((pieces, width, part), BF),) * 2,
        in_specs=[row] * count + [chunk] * (2 * count),
        out_specs=(result, result),
        scratch_shapes=[pltpu.VMEM((width, count * tokens), BF)],
        compiler_params=params(56),
        name="pair_sums",
    )(*normed, *first, *second)


def down_sums_kernel(count, *refs):
    hidden, grads, out, right = refs[:count], refs[count : 2 * count], refs[-2], refs[-1]

    @pl.when(pl.program_id(0) == 0)
    def _():
        for piece in range(out.shape[0]):
            right[piece] = jnp.concatenate([ref[piece] for ref in grads], axis=0)

    left = jnp.concatenate([ref[0].T for ref in hidden], axis=1)
    for piece in range(out.shape[0]):
        out[piece] = dot(left, right[piece]).astype(BF)


def down_sums(hidden, grads):
    count = len(hidden)
    pieces, tokens, part = hidden[0].shape
    cols = grads[0].shape[2]
    return pl.pallas_call(
        functools.partial(down_sums_kernel, count),
        grid=(pieces,),
        out_shape=shape((pieces, pieces * part, cols), BF),
        in_specs=[pl.BlockSpec((1, tokens, part), lambda f: (f, 0, 0))] * count
        + [pl.BlockSpec((pieces, tokens, cols), lambda f: (0, 0, 0))] * count,
        out_specs=pl.BlockSpec((pieces, part, cols), lambda f: (0, f, 0)),
        scratch_shapes=[pltpu.VMEM((pieces, count * tokens, cols), BF)],
        compiler_params=params(56),
        name="down_sums",
    )(*hidden, *grads)


MESH = pl.DeviceIdType.MESH


class Place:
    def __init__(self, layers):
        dp, seq = lax.axis_index("dp"), lax.axis_index("seq")
        self.layers = layers
        self.z, self.core = lax.div(dp, 2), lax.rem(dp, 2)
        self.y, self.x = lax.div(seq, 2), lax.rem(seq, 2)
        self.sibling = (self.z * 2 + 1 - self.core, seq)
        self.over_x = (dp, self.y * 2 + 1 - self.x)
        self.over_y = (dp, (1 - self.y) * 2 + self.x)
        self.up = [(lax.rem(self.z + k, layers) * 2 + self.core, seq) for k in range(layers)]
        self.down = [
            (lax.rem(self.z + layers - k, layers) * 2 + self.core, seq) for k in range(layers)
        ]
        self.peers = [self.sibling, self.over_x, self.over_y] + self.up[1:]

    def greet(self):
        barrier = pltpu.get_barrier_semaphore()
        for peer in self.peers:
            pl.semaphore_signal(barrier, inc=1, device_id=peer, device_id_type=MESH)
        pl.semaphore_wait(barrier, len(self.peers))


def remote(source, target, sems, peer):
    return pltpu.make_async_remote_copy(
        src_ref=source, dst_ref=target, send_sem=sems[0], recv_sem=sems[1],
        device_id=peer, device_id_type=MESH,
    )


def gather_kernel(count, layers, *refs):
    ins, outs = refs[:count], refs[count : 2 * count]
    send, recv, keep = refs[2 * count :]
    here = Place(layers)
    here.greet()
    y, x, z, core = here.y, here.x, here.z, here.core
    sent = []

    def slot(a, index):
        return send.at[a, index], recv.at[a, index]

    def start(a, index, source, target, peer):
        copy = remote(source, target, slot(a, index), peer)
        copy.start()
        sent.append(copy)

    def arrive(a, index, landing):
        remote(landing, landing, slot(a, index), here.sibling).wait_recv()

    def layer(k):
        return lax.rem(z + layers - k, layers)

    def sides(a):
        if a % 2 == 0:
            return here.over_x, here.over_y, (y, 1 - x), ((1 - y, x), (1 - y, 1 - x))
        return here.over_y, here.over_x, (1 - y, x), ((y, 1 - x), (1 - y, 1 - x))

    own = [pltpu.make_async_copy(ins[a], outs[a].at[y, x, z, core], keep.at[a]) for a in range(count)]
    for copy in own:
        copy.start()

    def first(k):
        for a in range(count):
            spot = outs[a].at[y, x, layer(k), core]
            source = ins[a] if k == 0 else spot
            if k:
                arrive(a, k, spot)
            start(a, layers + k, source, spot, sides(a)[0])
            start(a, 2 * layers + k, source, spot, sides(a)[1])

    def second(k):
        for a in range(count):
            side = sides(a)[2]
            spot = outs[a].at[side[0], side[1], layer(k), core]
            arrive(a, layers + k, spot)
            start(a, 3 * layers + k, spot, spot, sides(a)[1])

    def third(k):
        for a in range(count):
            for turn_of, side in enumerate(sides(a)[3]):
                arrive(a, (2 + turn_of) * layers + k, outs[a].at[side[0], side[1], layer(k), core])
            if k == 0:
                own[a].wait()
            spot = outs[a].at[:, :, layer(k), core]
            start(a, 4 * layers + k, spot, spot, here.sibling)

    def z_sends(k):
        for a in range(count):
            start(a, k, ins[a], outs[a].at[y, x, z, core], here.up[k])

    for a in range(count):
        for k in range(1, layers):
            start(a, k, ins[a], outs[a].at[y, x, z, core], here.up[k])
    for k in range(layers + 2):
        if k < layers:
            first(k)
        if 1 <= k <= layers:
            second(k - 1)
        if k >= 2:
            third(k - 2)
    for k in range(layers):
        for a in range(count):
            arrive(a, 4 * layers + k, outs[a].at[:, :, layer(k), 1 - core])
    for copy in sent:
        copy.wait_send()


def gather_all(parts, layers):
    count = len(parts)
    anywhere = pl.BlockSpec(memory_space=pl.ANY)
    return pl.pallas_call(
        functools.partial(gather_kernel, count, layers),
        out_shape=tuple(shape((2, 2, layers, 2) + part.shape, part.dtype) for part in parts),
        in_specs=[anywhere] * count,
        out_specs=(anywhere,) * count,
        scratch_shapes=[
            pltpu.SemaphoreType.DMA((count, 5 * layers)),
            pltpu.SemaphoreType.DMA((count, 5 * layers)),
            pltpu.SemaphoreType.DMA((count,)),
        ],
        compiler_params=pltpu.CompilerParams(collective_id=0, has_side_effects=True),
        name="gather_all",
    )(*parts)


def finish_kernel(layers, count, low_col, *refs):
    refs = list(refs)

    def pop(size):
        taken = refs[:size]
        del refs[:size]
        return taken

    normed, packed, attended, branch, ffn_in, grad_gate, grad_up, hidden, grad_ffn = (
        pop(count) for _ in range(9)
    )
    (small,) = pop(1)
    outs = pop(5)
    held, core_in, first_in, second_in, done, z_in = (pop(5) for _ in range(6))
    raw, left, right, ffn_right, stage, down_stage = pop(6)
    send, recv, keep, load = refs
    here = Place(layers)
    here.greet()
    y, x, z, core = here.y, here.x, here.z, here.core
    tokens = raw.shape[0] // count
    sent = []

    def slot(a, index):
        return send.at[a, index], recv.at[a, index]

    def start(a, index, source, target, peer):
        copy = remote(source, target, slot(a, index), peer)
        copy.start()
        sent.append(copy)

    def arrive(a, index, landing):
        remote(landing, landing, slot(a, index), here.sibling).wait_recv()

    def layer(k):
        return lax.rem(z + k + 1, layers)

    def added(ref, one, two):
        return (one.astype(F32) + two.astype(F32)).astype(ref.dtype)

    def load_left(index, sources):
        return [
            pltpu.make_async_copy(ref, raw.at[pl.ds(i * tokens, tokens)], load.at[index, i])
            for i, ref in enumerate(sources)
        ]

    def load_right(index, spot, sources, piece, start_col):
        width = sources[0].shape[2]
        return [
            pltpu.make_async_copy(
                ref.at[piece],
                right.at[spot, pl.ds(i * tokens, tokens), pl.ds(start_col, width)],
                load.at[index + spot, i],
            )
            for i, ref in enumerate(sources)
        ]

    def go(copies):
        for copy in copies:
            copy.start()

    def hold(copies):
        for copy in copies:
            copy.wait()

    def turn_left(spot):
        for i in range(count):
            rows = slice(i * tokens, (i + 1) * tokens)
            left[spot, :, rows] = raw[rows].T

    def sends(a, piece, source):
        if a == 3:
            theirs = source.at[:, :, 1 - core]
            ours = source.at[:, :, core]
            spot = (piece,)
        else:
            theirs = source.at[:, 1 - core]
            ours = source.at[:, core]
            spot = (slice(None), lax.div(piece, 2), lax.rem(piece, 2))
        return (
            remote(
                theirs, core_in[a].at[spot], (send.at[a, piece], recv.at[a, piece]), here.sibling
            ),
            pltpu.make_async_copy(ours, held[a].at[spot], keep.at[a, piece]),
        )

    def products(a, fetch, multiply, stages):
        go(fetch(0, 0))

        def step(piece, carry):
            spot = lax.rem(piece, 2)
            hold(fetch(piece, spot))

            @pl.when(piece < 3)
            def _():
                go(fetch(piece + 1, 1 - spot))

            @pl.when(piece >= 2)
            def _():
                out, own = sends(a, piece - 2, stages.at[spot])
                out.wait_send()
                own.wait()

            multiply(piece, spot)
            for copy in sends(a, piece, stages.at[spot]):
                copy.start()
            return carry

        lax.fori_loop(0, 4, step, 0)
        for piece in (2, 3):
            out, own = sends(a, piece, stages.at[piece % 2])
            out.wait_send()
            own.wait()

    def store(spot, result):
        rows = stage.shape[3]
        for index in range(2 * layers):
            stage[spot, index // 2, index % 2] = result[index * rows : (index + 1) * rows].astype(BF)

    def ffn_product(which):
        def multiply(piece, spot):
            width = which[0].shape[2]
            store(spot, dot(left[0], right[spot, :, :width]))

        return multiply

    high_col = packed[0].shape[2]
    far_col = branch[0].shape[2]

    def attn_product(piece, spot):
        first = dot(left[1], right[spot, :, :high_col])
        second = dot(left[0], right[spot, :, high_col : high_col + far_col])
        cut = high_col - low_col
        store(
            spot,
            jnp.concatenate(
                [first[:, :low_col], first[:, low_col:] + second[:, :cut], second[:, cut:]], axis=1
            ),
        )

    def down_product(piece, spot):
        part = hidden[0].shape[2]
        turned = jnp.concatenate(
            [right[spot, i * tokens : (i + 1) * tokens, :part].T for i in range(count)], axis=1
        )
        rows = part // 2
        for column in range(4):
            result = dot(turned, ffn_right[column]).astype(BF)
            for index in range(2):
                down_stage[spot, column // 2, column % 2, index] = result[
                    index * rows : (index + 1) * rows
                ]

    def first(a):
        if a < 4:
            for piece in range(4):
                spot = (piece,) if a == 3 else (slice(None), piece // 2, piece % 2)
                arrive(a, piece, core_in[a].at[spot])
        else:
            arrive(a, 0, core_in[a])
        for k in range(layers):
            held[a][k] = added(held[a], held[a][k], core_in[a][k])
        for k in range(layers):
            if k % 2 == 0:
                start(a, 4 + k, held[a].at[layer(k), :, 1 - x], first_in[a].at[k], here.over_x)
            else:
                start(a, 4 + k, held[a].at[layer(k), 1 - y], first_in[a].at[k], here.over_y)

    def second(a):
        for k in range(layers):
            at = layer(k)
            arrive(a, 4 + k, first_in[a].at[k])
            for i in range(2):
                if k % 2 == 0:
                    held[a][at, i, x] = added(held[a], held[a][at, i, x], first_in[a][k, i])
                else:
                    held[a][at, y, i] = added(held[a], held[a][at, y, i], first_in[a][k, i])
            index = 4 + layers + k
            if k % 2 == 0:
                start(a, index, held[a].at[at, 1 - y, x], second_in[a].at[k], here.over_y)
            else:
                start(a, index, held[a].at[at, y, 1 - x], second_in[a].at[k], here.over_x)

    def third(a):
        for k in range(layers):
            arrive(a, 4 + layers + k, second_in[a].at[k])
            done[a][k] = added(held[a], held[a][layer(k), y, x], second_in[a][k])
            if k < layers - 1:
                index = 4 + 2 * layers + k
                start(a, index, done[a].at[k], z_in[a].at[k], here.up[k + 1])

    def fourth(a):
        total = done[a][layers - 1].astype(F32)
        for k in range(layers - 1):
            arrive(a, 4 + 2 * layers + k, z_in[a].at[k])
            total = total + z_in[a][k].astype(F32)
        outs[a][...] = total

    start(4, 0, small.at[:, 1 - core], core_in[4], here.sibling)
    small_own = pltpu.make_async_copy(small.at[:, core], held[4], keep.at[4, 0])
    small_own.start()
    ffn_left = load_left(0, ffn_in)
    go(ffn_left)
    down_right = [
        pltpu.make_async_copy(
            ref.at[column],
            ffn_right.at[column, pl.ds(i * tokens, tokens)],
            load.at[6 + column, i],
        )
        for i, ref in enumerate(grad_ffn)
        for column in range(4)
    ]

    def fetch_of(index, sources):
        return lambda piece, spot: load_right(index, spot, sources, piece, 0)

    def fetch_attn(piece, spot):
        return load_right(2, spot, packed, piece, 0) + load_right(4, spot, branch, piece, high_col)

    hold(ffn_left)
    turn_left(0)
    normed_left = load_left(1, normed)
    go(normed_left)
    go(down_right)
    products(0, fetch_of(2, grad_gate), ffn_product(grad_gate), stage)
    first(0)
    hold(normed_left)
    turn_left(1)
    attended_left = load_left(0, attended)
    go(attended_left)
    products(1, fetch_of(2, grad_up), ffn_product(grad_up), stage)
    first(1)
    second(0)
    hold(attended_left)
    turn_left(0)
    products(2, fetch_attn, attn_product, stage)
    first(2)
    second(1)
    third(0)
    hold(down_right)
    products(3, fetch_of(2, hidden), down_product, down_stage)
    first(3)
    small_own.wait()
    first(4)
    second(2)
    third(1)
    second(3)
    second(4)
    third(2)
    third(3)
    third(4)
    for a in range(5):
        fourth(a)
    for copy in sent:
        copy.wait_send()


def finish(normed, packed, attended, branch, ffn_in, grad_gate, grad_up, hidden, grad_ffn, small, low_col):
    count = len(normed)
    tokens, width = normed[0].shape
    pieces, _, part = hidden[0].shape
    cols = grad_ffn[0].shape[2]
    layers = small.shape[0]
    ranks = 2 * layers
    anywhere = pl.BlockSpec(memory_space=pl.ANY)
    rows, down_rows = width // ranks, pieces * part // ranks
    wide = packed[0].shape[2] + branch[0].shape[2]
    ends = [(rows, part), (rows, part), (rows, part), (down_rows, cols), small.shape[4:]]
    types = [BF] * 4 + [F32]

    def buffers(*lead):
        return [pltpu.VMEM(lead + end, dtype) for end, dtype in zip(ends, types)]

    operands = (
        *normed, *packed, *attended, *branch, *ffn_in, *grad_gate, *grad_up, *hidden, *grad_ffn, small,
    )
    return pl.pallas_call(
        functools.partial(finish_kernel, layers, count, low_col),
        out_shape=tuple(shape(end, F32) for end in ends),
        in_specs=[anywhere] * len(operands),
        out_specs=(vmem,) * 5,
        scratch_shapes=[
            *buffers(layers, 2, 2),
            *buffers(layers, 2, 2),
            *buffers(layers, 2),
            *buffers(layers),
            *buffers(layers),
            *buffers(layers - 1),
            pltpu.VMEM((count * tokens, width), BF),
            pltpu.VMEM((2, width, count * tokens), BF),
            pltpu.VMEM((2, count * tokens, max(wide, part)), BF),
            pltpu.VMEM((pieces, count * tokens, cols), BF),
            pltpu.VMEM((2, layers, 2, rows, part), BF),
            pltpu.VMEM((2, 2, 2, 2, down_rows, cols), BF),
            pltpu.SemaphoreType.DMA((5, 4 + 3 * layers)),
            pltpu.SemaphoreType.DMA((5, 4 + 3 * layers)),
            pltpu.SemaphoreType.DMA((5, 4)),
            pltpu.SemaphoreType.DMA((10, count)),
        ],
        compiler_params=pltpu.CompilerParams(
            collective_id=1, has_side_effects=True, vmem_limit_bytes=61 * MIB
        ),
        name="finish",
    )(*operands)


def rope_tables(positions):
    half = HEAD_DIM // 2
    frequency = rope_base ** (-(jnp.arange(half, dtype=F32) * 2.0 / HEAD_DIM))
    angles = positions.astype(F32)[:, None] * frequency[None, :]
    cosine, sine = jnp.cos(angles), jnp.sin(angles)
    repeat = LANE // HEAD_DIM
    return (
        jnp.concatenate([cosine, cosine] * repeat, axis=1),
        jnp.concatenate([-sine, sine] * repeat, axis=1),
    )


def pass_on(array, step, count):
    return lax.ppermute(array, "seq", [(i, i + step) for i in range(count - step)])


def pass_back(array, step, count):
    return lax.ppermute(array, "seq", [(i + step, i) for i in range(count - step)])


def row_plan(inputs, cotangent, depths, marks, block_params):
    micros, _, tokens, _ = inputs.shape
    seq, mine = lax.axis_size("seq"), lax.axis_index("seq")
    attn_g, ffn_g, routers, qkv_w, out_w, gate_w, up_w, down_w, cols, shift = block_params
    order = mine - jnp.arange(seq)
    marks = jnp.where((order >= 0)[:, None, None, None], marks[order % seq], -1.0)
    marks = marks.transpose(2, 1, 0, 3).reshape(micros, 2, seq * tokens)
    infos = [jnp.pad(marks[m], ((0, 6), (0, 0))) for m in range(micros)]
    cosine, sine = rope_tables(mine * tokens + jnp.arange(tokens, dtype=jnp.int32))
    states = [inputs[m, 0] for m in range(micros)]
    actives = [
        [
            jnp.broadcast_to((depths[m, 0] > r).astype(F32)[:, None], (tokens, LANE))
            for r in range(RECUR)
        ]
        for m in range(micros)
    ]
    saved = [[None] * RECUR for _ in range(micros)]
    for r in range(RECUR):
        made = []
        for m in range(micros):
            normed, queries, pair = pre_part(states[m], attn_g, qkv_w, cosine, sine, cols)
            pairs = [pair] + [pass_on(pair, step, seq) for step in range(1, seq)]
            made.append((normed, queries, pairs))
        for m in range(micros):
            normed, queries, pairs = made[m]
            attended, logs = attend(queries, pairs, infos[m], r)
            after = post_part(
                states[m], attended, out_w, ffn_g, routers[r], actives[m][r], gate_w, up_w, down_w, shift
            )
            saved[m][r] = dict(
                after, state=states[m], normed=normed, queries=queries, pairs=pairs,
                attended=attended, logs=logs, active=actives[m][r],
            )
            states[m] = after["state_out"]
    grads = [cotangent[m, 0] for m in range(micros)]
    for r in reversed(range(RECUR)):
        partials = []
        for m in range(micros):
            s = saved[m][r]
            s.update(post_back(grads[m], s, ffn_g, routers[r], out_w, gate_w, up_w, down_w, shift))
            grad_queries, *grad_pairs = attend_back(
                s["queries"], s["pairs"], infos[m], s["attended"], s["logs"], s["grad_attended"], r
            )
            grad_pairs = [grad_pairs[0]] + [
                pass_back(grad_pairs[step], step, seq) for step in range(1, seq)
            ]
            partials.append((grad_queries, grad_pairs))
        for m in range(micros):
            s = saved[m][r]
            s["packed"], grads[m], s["attn_gain_grad"] = pre_back(
                *partials[m], s["partial"], s["state"], attn_g, qkv_w, cosine, sine, cols
            )
    outputs = jnp.stack(states, axis=0)[:, None]
    input_grad = jnp.stack(grads, axis=0)[:, None]
    return outputs, input_grad, saved


def swap(array, pairs):
    return lax.ppermute(array, "seq", [(a, b) for a, b in pairs] + [(b, a) for a, b in pairs])


ACROSS = ((0, 3), (1, 2))
PARTNERS = ((0, 1), (2, 3))


def paired_plan(inputs, cotangent, marks, block_params):
    tokens = inputs.shape[2]
    mine = lax.axis_index("seq")
    late = mine >= 2
    outer = is_outer()
    attn_g, ffn_g, routers, qkv_w, out_w, gate_w, up_w, down_w, cols, shift = block_params

    def take(array):
        own = jnp.where(late, array[1, 0], array[0, 0])
        other = swap(jnp.where(late, array[0, 0], array[1, 0]).astype(BF), ACROSS).astype(F32)
        return jnp.concatenate(
            [jnp.where(late, other, own), jnp.where(late, own, other)], axis=0
        )

    def give(array):
        low, high = array[:tokens], array[tokens:]
        own = jnp.where(late, high, low)
        other = swap(jnp.where(late, low, high).astype(BF), ACROSS).astype(F32)
        return jnp.stack([jnp.where(late, other, own), jnp.where(late, own, other)], axis=0)[:, None]

    blocks = jnp.where(outer, jnp.array([0, 3, 1, 2]), jnp.array([1, 2, 0, 3]))
    info = jnp.where(late, marks[:, :, 1], marks[:, :, 0])[blocks]
    info = jnp.pad(info.transpose(1, 0, 2).reshape(2, -1), ((0, 6), (0, 0)))
    depth = info[1, : 2 * tokens]
    places = jnp.arange(tokens, dtype=jnp.int32)
    cosine, sine = rope_tables(
        jnp.concatenate([blocks[0] * tokens + places, blocks[1] * tokens + places])
    )
    state = take(inputs)
    cotangent, depth = lax.optimization_barrier((cotangent, depth))
    grad = take(cotangent)
    saved = []
    for r in range(RECUR):
        active = jnp.broadcast_to((depth > r).astype(F32)[:, None], (2 * tokens, LANE))
        normed, queries, pair = pre_part(state, attn_g, qkv_w, cosine, sine, cols)
        partner = swap(pair, PARTNERS)
        part = attend_own(queries, pair, info, r)
        attended, logs = attend_rest(queries, partner, info, part, r)
        after = post_part(
            state, attended, out_w, ffn_g, routers[r], active, gate_w, up_w, down_w, shift
        )
        saved.append(
            dict(
                after, state=state, normed=normed, queries=queries, pair=pair, partner=partner,
                attended=attended, logs=logs, active=active,
            )
        )
        state = after["state_out"]
    outputs = give(state)
    for r in reversed(range(RECUR)):
        s = saved[r]
        s.update(post_back(grad, s, ffn_g, routers[r], out_w, gate_w, up_w, down_w, shift))
        grad_partner, part, deltas = attend_rest_back(
            s["queries"], s["partner"], info, s["attended"], s["logs"], s["grad_attended"], r
        )
        grad_partner = swap(grad_partner, PARTNERS)
        grad_queries, grad_pair = attend_own_back(
            s["queries"], s["pair"], info, s["logs"], deltas, s["grad_attended"], part, r
        )
        s["packed"], grad, s["attn_gain_grad"] = pre_back(
            grad_queries, [grad_pair, grad_partner], s["partial"], s["state"], attn_g, qkv_w,
            cosine, sine, cols,
        )
    return outputs, give(grad), [saved]


def local(
    inputs, cotangent, segments, depths, query_weight, key_weight, value_weight, out_weight,
    gate_weight, up_weight, down_weight, attn_gain, ffn_gain, router_weight,
):
    micros, _, tokens, width = inputs.shape
    seq, ranks = lax.axis_size("seq"), lax.axis_size("dp")
    rows = query_weight.shape[0]
    qc, kc = query_weight.shape[1], key_weight.shape[1]
    both = ("seq", "dp")

    attn_local = jnp.concatenate([query_weight, key_weight, value_weight, out_weight], axis=1)
    span = ceil_to(max(rows, tokens), LANE)
    small = jnp.concatenate([attn_gain[None], ffn_gain[None], router_weight.T], axis=0).astype(F32)
    marks = jnp.concatenate([segments[:, 0], depths[:, 0]], axis=0).astype(F32)
    small = jnp.concatenate(
        [
            jnp.pad(small, ((0, 8 - small.shape[0]), (0, span - rows))),
            jnp.pad(marks, ((0, ceil_to(2 * micros, 8) - 2 * micros), (0, span - tokens))),
        ],
        axis=0,
    )
    parts = (attn_local, gate_weight, up_weight, down_weight, small)
    direct = micros == 2 and (seq, ranks) == (4, 8)
    if direct:
        gathered = gather_all(parts, ranks // 2)
    else:
        gathered = [lax.all_gather(part, both, axis=0, tiled=False) for part in parts]
    attn_w, gate_w, up_w, down_w = (
        full.reshape(seq, -1, full.shape[-1]) for full in gathered[:4]
    )
    small = gathered[4].reshape(seq, ranks, *small.shape)
    marks = lax.dynamic_index_in_dim(small, lax.axis_index("dp"), 1, keepdims=False)
    marks = marks[:, 8 : 8 + 2 * micros, :tokens].reshape(seq, 2, micros, tokens)
    small = small[0, :, : 2 + RECUR, :rows].transpose(1, 0, 2).reshape(2 + RECUR, width)
    attn_g, ffn_g = small[0:1], small[1:2]
    routers = [small[2 + r : 3 + r] for r in range(RECUR)]
    used = qc + 2 * kc
    total_cols = attn_w.shape[2]
    high_col = min(ceil_to(used, LANE), total_cols)
    low_col = used // LANE * LANE
    shift = used - low_col
    qkv_w, out_w = attn_w[:, :, :high_col], attn_w[:, :, low_col:]

    block_params = (
        attn_g, ffn_g, routers, qkv_w, out_w, gate_w, up_w, down_w, (qc, kc), shift
    )
    if direct:
        outputs, input_grad, saved = paired_plan(inputs, cotangent, marks, block_params)
    else:
        outputs, input_grad, saved = row_plan(inputs, cotangent, depths, marks, block_params)
    flat = [steps[r] for r in reversed(range(RECUR)) for steps in saved]

    def every(name):
        return [s[name] for s in flat]

    attn_gain_sum, ffn_gain_sum = sum(every("attn_gain_grad")), sum(every("ffn_gain_grad"))
    router_sums = [sum(steps[r]["router_grad"] for steps in saved) for r in range(RECUR)]
    small_sum = jnp.concatenate([attn_gain_sum, ffn_gain_sum, *router_sums], axis=0)
    small_sum = small_sum.reshape(2 + RECUR, ranks, rows).transpose(1, 0, 2)
    small_sum = jnp.pad(
        small_sum, ((0, 0), (0, 8 - small_sum.shape[1]), (0, ceil_to(rows, LANE) - rows))
    )
    if direct:
        small_sum = small_sum.reshape(ranks // 2, 2, 1, 1, *small_sum.shape[1:])
        small_sum = jnp.broadcast_to(small_sum, small_sum.shape[:2] + (2, 2) + small_sum.shape[4:])
        gate_grad, up_grad, attn_grad, down_grad, small_own = finish(
            every("normed"), every("packed"), every("attended"), every("grad_branch"),
            every("ffn_in"), every("grad_gate"), every("grad_up"), every("hidden"),
            every("grad_ffn"), small_sum, low_col,
        )
    else:
        down_sum = down_sums(every("hidden"), every("grad_ffn"))
        gate_sum, up_sum = pair_sums(every("ffn_in"), every("grad_gate"), every("grad_up"))
        attn_sum = attn_sums(
            every("normed"), every("packed"), every("attended"), every("grad_branch"),
            low_col, total_cols,
        )
        small_sum = jnp.broadcast_to(small_sum[None], (seq,) + small_sum.shape)
        sums = [
            part.reshape(seq, ranks, -1, part.shape[-1])
            for part in (gate_sum, up_sum, attn_sum, down_sum, small_sum)
        ]
        sums = [lax.psum_scatter(part, "seq", scatter_dimension=0) for part in sums]
        sums = [lax.psum_scatter(part, "dp", scatter_dimension=0).astype(F32) for part in sums]
        gate_grad, up_grad, attn_grad, down_grad, small_own = sums
    small_own = small_own[: 2 + RECUR, :rows]

    return (
        outputs,
        input_grad,
        attn_grad[:, :qc],
        attn_grad[:, qc : qc + kc],
        attn_grad[:, qc + kc : used],
        attn_grad[:, used:],
        gate_grad,
        up_grad,
        down_grad,
        small_own[0],
        small_own[1],
        small_own[2:].T,
    )


def solution(mesh):
    data = P(None, "dp", "seq", None)
    marks = P(None, "dp", "seq")
    weight = P("dp", "seq")
    in_specs = (data, data, marks, marks) + (weight,) * 7 + (P("dp"), P("dp"), P("dp", None))
    out_specs = (data, data) + (weight,) * 7 + (P("dp"), P("dp"), P("dp", None))
    return jax.shard_map(local, mesh=mesh, in_specs=in_specs, out_specs=out_specs, check_vma=False)
```

```python
import functools

import jax
import jax.numpy as jnp
from jax import lax
from jax.experimental import pallas as pl
from jax.experimental.pallas import tpu as pltpu
from jax.sharding import PartitionSpec as P

HEADS = 15
KV_HEADS = 5
HEAD_DIM = 64
RECUR = 3
GROUP = HEADS // KV_HEADS
KW = KV_HEADS * HEAD_DIM
QW = HEADS * HEAD_DIM
LANE = 128
MIB = 2**20
BESIDE = 16

epsilon = 1e-05
rope_base = 10000.0

NN = (((1,), (0,)), ((), ()))
NT = (((1,), (1,)), ((), ()))
BF = jnp.bfloat16
F32 = jnp.float32

vmem = pl.BlockSpec(memory_space=pltpu.VMEM)


def dot(left, right, dims=NN):
    return lax.dot_general(left, right, dims, preferred_element_type=F32)


def ceil_to(size, unit):
    return -(-size // unit) * unit


def shape(dims, dtype):
    return jax.ShapeDtypeStruct(dims, dtype)


def params(limit):
    return pltpu.CompilerParams(vmem_limit_bytes=limit * MIB)


def pin(array):
    return pltpu.with_memory_space_constraint(array, pltpu.VMEM)


def wide_limit(weight, limit):
    return limit if whole_lanes(weight) else 62


def whole_lanes(weight):
    return weight.shape[-1] % LANE == 0


def placed(weight):
    return pin(weight) if whole_lanes(weight) else weight


def side_by_side(ref, rows=slice(None)):
    return jnp.concatenate([ref[piece, rows] for piece in range(ref.shape[0])], axis=1)


def turn(block, cosine, sine):
    lanes = lax.broadcasted_iota(jnp.int32, block.shape, 1) % HEAD_DIM
    partner = jnp.where(
        lanes < HEAD_DIM // 2,
        pltpu.roll(block, LANE - HEAD_DIM // 2, 1),
        pltpu.roll(block, HEAD_DIM // 2, 1),
    )
    return block * cosine + partner * sine


def norm_back(grad_out, values_in, gain):
    inverse = lax.rsqrt(jnp.mean(values_in * values_in, axis=-1, keepdims=True) + epsilon)
    weighted = grad_out * gain
    inner = jnp.mean(weighted * values_in, axis=-1, keepdims=True)
    grad_gain = jnp.sum(grad_out * values_in * inverse, axis=0, keepdims=True)
    return weighted * inverse - values_in * (inverse * inverse * inverse * inner), grad_gain


def pre_kernel(cols, state, gain, weight, cosine, sine, normed, queries, pair, qbuf, kbuf):
    qc, kc = cols
    values_in = state[...]
    inverse = lax.rsqrt(jnp.mean(values_in * values_in, axis=-1, keepdims=True) + epsilon)
    low = (values_in * inverse * gain[...]).astype(BF)
    normed[...] = low
    used = min(ceil_to(qc + 2 * kc, LANE), weight.shape[2])
    for piece in range(weight.shape[0]):
        made = dot(low, weight[piece, :, :used])
        qbuf[:, piece * qc : (piece + 1) * qc] = made[:, :qc]
        kbuf[:, piece * kc : (piece + 1) * kc] = made[:, qc : qc + kc]
        pair[:, KW + piece * kc : KW + (piece + 1) * kc] = made[:, qc + kc : qc + 2 * kc].astype(BF)
    for buf, out, width, scale in ((qbuf, queries, QW, HEAD_DIM**-0.5), (kbuf, pair, KW, 1.0)):
        for start in range(0, width, LANE):
            stop = min(start + LANE, width)
            turned = turn(buf[:, start : start + LANE], cosine[...], sine[...]) * scale
            out[:, start:stop] = turned[:, : stop - start].astype(BF)


def pre_part(state, gain, weight, cosine, sine, cols):
    tokens, width = state.shape
    return pl.pallas_call(
        functools.partial(pre_kernel, cols),
        out_shape=(
            shape((tokens, width), BF),
            shape((tokens, QW), BF),
            shape((tokens, 2 * KW), BF),
        ),
        in_specs=[vmem] * 5,
        out_specs=(vmem,) * 3,
        scratch_shapes=[
            pltpu.VMEM((tokens, ceil_to(QW, LANE)), F32),
            pltpu.VMEM((tokens, ceil_to(KW, LANE)), F32),
        ],
        compiler_params=params(wide_limit(weight, 20)),
        name="pre",
    )(state, gain, placed(weight), cosine, sine)


def fill_bias(info, bias, recursion):
    keys, tokens = bias.shape
    columns = info[...].T
    place = lax.broadcasted_iota(jnp.int32, (keys, tokens), 0)
    query = lax.broadcasted_iota(jnp.int32, (keys, tokens), 1)
    apart = place % tokens - place // tokens * tokens - query
    same = columns[:, 0:1] == info[0:1, 0:tokens]
    live = columns[:, 1:2] > recursion
    seen = same & (((apart < 0) & live) | (apart == 0))
    bias[...] = jnp.where(seen, 0.0, -1e30)


def head_cols(head):
    return slice(head * HEAD_DIM, (head + 1) * HEAD_DIM)


def stack_heads(ref, group):
    heads = range(group * GROUP, (group + 1) * GROUP)
    return jnp.concatenate([ref[:, head_cols(head)] for head in heads], axis=0)


def attend_kernel(blocks, recursion, *refs):
    queries, pairs = refs[0], refs[1 : 1 + blocks]
    info, attended, logs, bias = refs[1 + blocks :]
    tokens = queries.shape[0]
    keys = blocks * tokens
    fill_bias(info, bias, recursion)
    logs[...] = jnp.zeros(logs.shape, F32)
    for group in range(KV_HEADS):
        key = jnp.concatenate([ref[:, head_cols(group)] for ref in pairs], axis=0)
        value = jnp.concatenate([ref[:, head_cols(KV_HEADS + group)] for ref in pairs], axis=0)
        value_t = jnp.concatenate([value.T, jnp.ones((16, keys), BF)], axis=0)
        query = stack_heads(queries, group)
        scores = dot(key, query, NT) + jnp.concatenate([bias[...]] * GROUP, axis=1)
        top = jnp.max(scores, axis=0, keepdims=True)
        weights = jnp.exp(scores - top).astype(BF)
        mixed = dot(value_t, weights)
        total = mixed[HEAD_DIM : HEAD_DIM + 1]
        mixed = mixed[:HEAD_DIM] * (1.0 / total)
        log_total = top + jnp.log(total)
        for offset in range(GROUP):
            head = group * GROUP + offset
            span = slice(offset * tokens, (offset + 1) * tokens)
            attended[:, head_cols(head)] = mixed[:, span].T.astype(BF)
            logs[head : head + 1, :] = log_total[:, span]


def attend(queries, pairs, info, recursion):
    tokens = queries.shape[0]
    blocks = len(pairs)
    return pl.pallas_call(
        functools.partial(attend_kernel, blocks, recursion),
        out_shape=(shape((tokens, QW), BF), shape((ceil_to(HEADS, 8), tokens), F32)),
        in_specs=[vmem] * (2 + blocks),
        out_specs=(vmem, vmem),
        scratch_shapes=[pltpu.VMEM((blocks * tokens, tokens), F32)],
        compiler_params=params(40),
        name="attend",
    )(queries, *pairs, info)


def attend_back_kernel(blocks, recursion, *refs):
    queries, pairs = refs[0], refs[1 : 1 + blocks]
    info, attended, logs, grad, grad_queries = refs[1 + blocks : 6 + blocks]
    grad_pairs, bias = refs[6 + blocks : 6 + 2 * blocks], refs[6 + 2 * blocks]
    tokens = queries.shape[0]
    fill_bias(info, bias, recursion)
    product = (attended[...].astype(F32) * grad[...].astype(F32)).T
    for group in range(KV_HEADS):
        key = jnp.concatenate([ref[:, head_cols(group)] for ref in pairs], axis=0)
        value = jnp.concatenate([ref[:, head_cols(KV_HEADS + group)] for ref in pairs], axis=0)
        key_t = key.T
        query = stack_heads(queries, group)
        grad_mixed = stack_heads(grad, group)
        heads = range(group * GROUP, (group + 1) * GROUP)
        delta = jnp.concatenate(
            [jnp.sum(product[head_cols(head)], axis=0, keepdims=True) for head in heads], axis=1
        )
        log_total = jnp.concatenate([logs[head : head + 1, :] for head in heads], axis=1)
        scores = dot(key, query, NT) + jnp.concatenate([bias[...]] * GROUP, axis=1)
        probs = jnp.exp(scores - log_total)
        grad_probs = dot(value, grad_mixed, NT)
        grad_scores = (probs * (grad_probs - delta)).astype(BF)
        grad_value = dot(probs.astype(BF), grad_mixed)
        grad_key = dot(grad_scores, query)
        grad_query = dot(key_t, grad_scores) * HEAD_DIM**-0.5
        for offset, head in enumerate(heads):
            span = slice(offset * tokens, (offset + 1) * tokens)
            grad_queries[:, head_cols(head)] = grad_query[:, span].T
        for block, ref in enumerate(grad_pairs):
            rows = slice(block * tokens, (block + 1) * tokens)
            ref[:, head_cols(group)] = grad_key[rows].astype(ref.dtype)
            ref[:, head_cols(KV_HEADS + group)] = grad_value[rows].astype(ref.dtype)


def attend_back(queries, pairs, info, attended, logs, grad, recursion):
    tokens = queries.shape[0]
    blocks = len(pairs)
    return pl.pallas_call(
        functools.partial(attend_back_kernel, blocks, recursion),
        out_shape=(shape((tokens, QW), F32), shape((tokens, 2 * KW), F32))
        + (shape((tokens, 2 * KW), BF),) * (blocks - 1),
        in_specs=[vmem] * (5 + blocks),
        out_specs=(vmem,) * (1 + blocks),
        scratch_shapes=[pltpu.VMEM((blocks * tokens, tokens), F32)],
        compiler_params=params(48),
        name="attend_back",
    )(queries, *pairs, info, attended, logs, grad)


def is_outer():
    place = lax.axis_index("seq")
    return (place == 0) | (place == 3)


def block_bias(info, bias, index, key_block, query_block, recursion, columns, diagonal):
    block = bias.shape[1]

    def span(which):
        return pl.ds(pl.multiple_of(which * block, block), block)

    same = columns[span(key_block), 0:1] == info[0:1, span(query_block)]
    seen = columns[span(key_block), 1:2] > recursion
    if diagonal:
        key = lax.broadcasted_iota(jnp.int32, (block, block), 0)
        query = lax.broadcasted_iota(jnp.int32, (block, block), 1)
        seen = ((key < query) & seen) | (key == query)
    bias[index] = jnp.where(same & seen, 0.0, -1e30)


def tall_heads(ref, rows, group):
    heads = range(group * GROUP, (group + 1) * GROUP)
    return jnp.concatenate([ref[rows, head_cols(head)] for head in heads], axis=0)


def thrice(bias):
    return jnp.concatenate([bias] * GROUP, axis=1)


def with_ones(value):
    return jnp.concatenate([value.T, jnp.ones((16, value.shape[0]), BF)], axis=0)


def own_kernel(recursion, queries, pair, info, part, columns, bias):
    block = queries.shape[0] // 2
    wide = GROUP * block
    columns[...] = info[...].T
    block_bias(info, bias, 0, 0, 0, recursion, columns, True)
    block_bias(info, bias, 1, 0, 1, recursion, columns, False)
    block_bias(info, bias, 2, 1, 1, recursion, columns, True)
    low, high = slice(0, block), slice(block, 2 * block)
    for group in range(KV_HEADS):
        kc, vc = head_cols(group), head_cols(KV_HEADS + group)
        query_low, query_high = tall_heads(queries, low, group), tall_heads(queries, high, group)
        first = dot(pair[low, kc], query_low, NT) + thrice(bias[0])
        second = dot(pair[low, kc], query_high, NT) + thrice(bias[1])
        third = dot(pair[high, kc], query_high, NT) + thrice(bias[2])
        value_low, value_high = with_ones(pair[low, vc]), with_ones(pair[high, vc])
        top = jnp.max(first, axis=0, keepdims=True)
        mixed = dot(value_low, jnp.exp(first - top).astype(BF))
        part[group, : HEAD_DIM + 8, :wide] = mixed[: HEAD_DIM + 8]
        part[group, HEAD_DIM + 8 :, :wide] = jnp.broadcast_to(top, (8, wide))
        top = jnp.maximum(
            jnp.max(second, axis=0, keepdims=True), jnp.max(third, axis=0, keepdims=True)
        )
        mixed = dot(value_low, jnp.exp(second - top).astype(BF))
        mixed += dot(value_high, jnp.exp(third - top).astype(BF))
        part[group, : HEAD_DIM + 8, wide:] = mixed[: HEAD_DIM + 8]
        part[group, HEAD_DIM + 8 :, wide:] = jnp.broadcast_to(top, (8, wide))


def attend_own(queries, pair, info, recursion):
    tokens = queries.shape[0]
    block = tokens // 2
    return pl.pallas_call(
        functools.partial(own_kernel, recursion),
        out_shape=shape((KV_HEADS, HEAD_DIM + 16, GROUP * tokens), F32),
        in_specs=[vmem] * 3,
        out_specs=vmem,
        scratch_shapes=[
            pltpu.VMEM(info.shape[::-1], F32),
            pltpu.VMEM((3, block, block), F32),
        ],
        compiler_params=params(16),
        name="attend_own",
    )(queries, pair, info)


def rest_rows(block):
    outer = is_outer()
    shift = pl.multiple_of(jnp.where(outer, block, 0), block)
    return outer, pl.ds(shift, block)


def rest_kernel(recursion, queries, pair, info, part, attended, logs, columns, bias):
    block = queries.shape[0] // 2
    wide = GROUP * block
    columns[...] = info[...].T
    outer, rows = rest_rows(block)
    fifth = jnp.where(outer, 1, 0)
    block_bias(info, bias, 0, 2, 1, recursion, columns, False)
    block_bias(info, bias, 1, 2 + fifth, fifth, recursion, columns, False)
    low, high = slice(0, block), slice(block, 2 * block)
    logs[...] = jnp.zeros(logs.shape, F32)
    for group in range(KV_HEADS):
        kc, vc = head_cols(group), head_cols(KV_HEADS + group)
        fourth = dot(pair[low, kc], tall_heads(queries, high, group), NT) + thrice(bias[0])
        fifth = dot(pair[rows, kc], tall_heads(queries, rows, group), NT) + thrice(bias[1])
        own_low, own_high = part[group, :, :wide], part[group, :, wide:]
        top_low, top_high = own_low[HEAD_DIM + 8 : HEAD_DIM + 9], own_high[HEAD_DIM + 8 : HEAD_DIM + 9]
        fifth_top = jnp.max(fifth, axis=0, keepdims=True)
        new_low = jnp.where(outer, top_low, jnp.maximum(top_low, fifth_top))
        new_high = jnp.maximum(top_high, jnp.max(fourth, axis=0, keepdims=True))
        new_high = jnp.where(outer, jnp.maximum(new_high, fifth_top), new_high)
        fourth = jnp.exp(fourth - new_high).astype(BF)
        fifth = jnp.exp(fifth - jnp.where(outer, new_high, new_low)).astype(BF)
        added_high = dot(with_ones(pair[low, vc]), fourth)[: HEAD_DIM + 8]
        added = dot(with_ones(pair[rows, vc]), fifth)[: HEAD_DIM + 8]
        mixed_low = own_low[: HEAD_DIM + 8] * jnp.exp(top_low - new_low)
        mixed_low += jnp.where(outer, 0.0, added)
        mixed_high = own_high[: HEAD_DIM + 8] * jnp.exp(top_high - new_high)
        mixed_high += added_high + jnp.where(outer, added, 0.0)
        for start, mixed, top in ((0, mixed_low, new_low), (block, mixed_high, new_high)):
            total = mixed[HEAD_DIM : HEAD_DIM + 1]
            final = mixed[:HEAD_DIM] * (1.0 / total)
            log_total = top + jnp.log(total)
            for offset in range(GROUP):
                head = group * GROUP + offset
                span = slice(offset * block, (offset + 1) * block)
                attended[start : start + block, head_cols(head)] = final[:, span].T.astype(BF)
                logs[head : head + 1, start : start + block] = log_total[:, span]


def attend_rest(queries, pair, info, part, recursion):
    tokens = queries.shape[0]
    block = tokens // 2
    return pl.pallas_call(
        functools.partial(rest_kernel, recursion),
        out_shape=(shape((tokens, QW), BF), shape((ceil_to(HEADS, 8), tokens), F32)),
        in_specs=[vmem] * 4,
        out_specs=(vmem, vmem),
        scratch_shapes=[
            pltpu.VMEM(info.shape[::-1], F32),
            pltpu.VMEM((2, block, block), F32),
        ],
        compiler_params=params(16),
        name="attend_rest",
    )(queries, pair, info, part)


def flat_row(ref, cols, group):
    heads = range(group * GROUP, (group + 1) * GROUP)
    return jnp.concatenate([ref[head : head + 1, cols] for head in heads], axis=1)


def block_back(key, value, query, grad_mixed, bias, log_total, delta):
    probs = jnp.exp(dot(key, query, NT) + thrice(bias) - log_total)
    grad_scores = (probs * (dot(value, grad_mixed, NT) - delta)).astype(BF)
    grad_value = dot(probs.astype(BF), grad_mixed)
    grad_key = dot(grad_scores, query)
    return dot(key.T, grad_scores), grad_key, grad_value


def rest_back_kernel(
    recursion, queries, pair, info, attended, logs, grad, grad_pair, part, deltas, columns, bias
):
    block = queries.shape[0] // 2
    wide = GROUP * block
    columns[...] = info[...].T
    outer, rows = rest_rows(block)
    fifth = jnp.where(outer, 1, 0)
    block_bias(info, bias, 0, 2, 1, recursion, columns, False)
    block_bias(info, bias, 1, 2 + fifth, fifth, recursion, columns, False)
    low, high = slice(0, block), slice(block, 2 * block)
    product = (attended[...].astype(F32) * grad[...].astype(F32)).T
    deltas[...] = jnp.zeros(deltas.shape, F32)
    for head in range(HEADS):
        deltas[head : head + 1, :] = jnp.sum(product[head_cols(head)], axis=0, keepdims=True)
    for group in range(KV_HEADS):
        kc, vc = head_cols(group), head_cols(KV_HEADS + group)
        query_high, key_high, value_high = block_back(
            pair[low, kc], pair[low, vc], tall_heads(queries, high, group),
            tall_heads(grad, high, group), bias[0], flat_row(logs, high, group),
            flat_row(deltas, high, group),
        )
        query, key, value = block_back(
            pair[rows, kc], pair[rows, vc], tall_heads(queries, rows, group),
            tall_heads(grad, rows, group), bias[1], flat_row(logs, rows, group),
            flat_row(deltas, rows, group),
        )
        part[group, :, :wide] = jnp.where(outer, 0.0, query)
        part[group, :, wide:] = query_high + jnp.where(outer, query, 0.0)
        grad_pair[low, kc] = (key_high + jnp.where(outer, 0.0, key)).astype(BF)
        grad_pair[low, vc] = (value_high + jnp.where(outer, 0.0, value)).astype(BF)
        grad_pair[high, kc] = jnp.where(outer, key, 0.0).astype(BF)
        grad_pair[high, vc] = jnp.where(outer, value, 0.0).astype(BF)


def attend_rest_back(queries, pair, info, attended, logs, grad, recursion):
    tokens = queries.shape[0]
    block = tokens // 2
    return pl.pallas_call(
        functools.partial(rest_back_kernel, recursion),
        out_shape=(
            shape((tokens, 2 * KW), BF),
            shape((KV_HEADS, HEAD_DIM, GROUP * tokens), F32),
            shape(logs.shape, F32),
        ),
        in_specs=[vmem] * 6,
        out_specs=(vmem,) * 3,
        scratch_shapes=[
            pltpu.VMEM(info.shape[::-1], F32),
            pltpu.VMEM((2, block, block), F32),
        ],
        compiler_params=params(20),
        name="attend_rest_back",
    )(queries, pair, info, attended, logs, grad)


def own_back_kernel(
    recursion, queries, pair, info, logs, deltas, grad, part, grad_queries, grad_pair, columns, bias
):
    block = queries.shape[0] // 2
    wide = GROUP * block
    columns[...] = info[...].T
    block_bias(info, bias, 0, 0, 0, recursion, columns, True)
    block_bias(info, bias, 1, 0, 1, recursion, columns, False)
    block_bias(info, bias, 2, 1, 1, recursion, columns, True)
    low, high = slice(0, block), slice(block, 2 * block)
    for group in range(KV_HEADS):
        kc, vc = head_cols(group), head_cols(KV_HEADS + group)
        made = []
        for index, keys, side in ((0, low, low), (1, low, high), (2, high, high)):
            made.append(
                block_back(
                    pair[keys, kc], pair[keys, vc], tall_heads(queries, side, group),
                    tall_heads(grad, side, group), bias[index], flat_row(logs, side, group),
                    flat_row(deltas, side, group),
                )
            )
        first, second, third = made
        grad_pair[low, kc] = first[1] + second[1]
        grad_pair[low, vc] = first[2] + second[2]
        grad_pair[high, kc] = third[1]
        grad_pair[high, vc] = third[2]
        query_low = (part[group, :, :wide] + first[0]) * HEAD_DIM**-0.5
        query_high = (part[group, :, wide:] + second[0] + third[0]) * HEAD_DIM**-0.5
        for start, made_query in ((0, query_low), (block, query_high)):
            for offset in range(GROUP):
                head = group * GROUP + offset
                span = slice(offset * block, (offset + 1) * block)
                grad_queries[start : start + block, head_cols(head)] = made_query[:, span].T


def attend_own_back(queries, pair, info, logs, deltas, grad, part, recursion):
    tokens = queries.shape[0]
    block = tokens // 2
    return pl.pallas_call(
        functools.partial(own_back_kernel, recursion),
        out_shape=(shape((tokens, QW), F32), shape((tokens, 2 * KW), F32)),
        in_specs=[vmem] * 7,
        out_specs=(vmem,) * 2,
        scratch_shapes=[
            pltpu.VMEM(info.shape[::-1], F32),
            pltpu.VMEM((3, block, block), F32),
        ],
        compiler_params=params(20),
        name="attend_own_back",
    )(queries, pair, info, logs, deltas, grad, part)


def post_kernel(
    used, cols, state, attended, attn_w, gain, router, active, gate_w, up_w, down_w,
    state_out, normed_out, gate_out, up_out, hidden_out, midway_out, update_out, routed,
    normed, midway, update, branch, total, stage, sems,
):
    pieces, _, part = gate_w.shape
    wide = down_w.shape[2]
    low_col = used // LANE * LANE

    def ship(index, source, target):
        return pltpu.make_async_copy(source, target, sems.at[index])

    def ship_piece(piece):
        spot = lax.rem(piece, 2)
        return [
            ship(3 + 3 * spot + index, stage.at[spot, index], out.at[piece])
            for index, out in enumerate((gate_out, up_out, hidden_out))
        ]

    for piece in range(pieces):
        made = dot(attended[...], attn_w[piece, :, low_col:])
        branch[:, piece * cols : (piece + 1) * cols] = made[:, used - low_col :]
    between = state[...] + branch[...]
    midway[...] = between
    ship(0, midway, midway_out).start()
    inverse = lax.rsqrt(jnp.mean(between * between, axis=-1, keepdims=True) + epsilon)
    normed[...] = (between * inverse * gain[...]).astype(BF)
    ship(1, normed, normed_out).start()
    chance = 1.0 / (1.0 + jnp.exp(-jnp.sum(state[...] * router[...], axis=-1, keepdims=True)))
    routed[...] = jnp.broadcast_to(chance, routed.shape)
    total[...] = jnp.zeros(total.shape, F32)

    def step(piece, carry):
        spot = lax.rem(piece, 2)

        @pl.when(piece >= 2)
        def _():
            for copy in ship_piece(piece - 2):
                copy.wait()

        rows = pl.ds(pl.multiple_of(piece * part, part), part)
        half = normed.shape[0] // 2
        for span in (slice(0, half), slice(half, 2 * half)):
            pre = dot(normed[span], jnp.concatenate([gate_w[piece], up_w[piece]], axis=1))
            gate, up = pre[:, :part], pre[:, part:]
            hidden = (gate / (1.0 + jnp.exp(-gate)) * up).astype(BF)
            for index, made in enumerate((gate.astype(BF), up.astype(BF), hidden)):
                stage[spot, index, span] = made
            total[span] += dot(hidden, side_by_side(down_w, rows))
        for copy in ship_piece(piece):
            copy.start()
        return carry

    lax.fori_loop(0, pieces, step, 0)
    for piece in range(pieces):
        span = slice(piece * cols, (piece + 1) * cols)
        branch[:, span] = branch[:, span] + total[:, piece * wide : piece * wide + cols]
    changed = branch[...]
    update[...] = changed.astype(BF)
    ship(2, update, update_out).start()
    state_out[...] = state[...] + (active[:, 0:1] * routed[:, 0:1]) * changed
    for index, (source, target) in enumerate(
        ((midway, midway_out), (normed, normed_out), (update, update_out))
    ):
        ship(index, source, target).wait()
    for piece in range(max(0, pieces - 2), pieces):
        for copy in ship_piece(piece):
            copy.wait()


anywhere = pl.BlockSpec(memory_space=pl.ANY)


def post_part(state, attended, attn_w, gain, router, active, gate_w, up_w, down_w, used):
    tokens, width = state.shape
    pieces, _, part = gate_w.shape
    made = pl.pallas_call(
        functools.partial(post_kernel, used, width // pieces),
        out_shape=(
            shape((tokens, width), F32),
            shape((tokens, width), BF),
            shape((pieces, tokens, part), BF),
            shape((pieces, tokens, part), BF),
            shape((pieces, tokens, part), BF),
            shape((tokens, width), F32),
            shape((tokens, width), BF),
            shape((tokens, LANE), F32),
        ),
        in_specs=[vmem] * 9,
        out_specs=(vmem,) + (anywhere,) * 6 + (vmem,),
        scratch_shapes=[
            pltpu.VMEM((tokens, width), BF),
            pltpu.VMEM((tokens, width), F32),
            pltpu.VMEM((tokens, width), BF),
            pltpu.VMEM((tokens, width), F32),
            pltpu.VMEM((tokens, pieces * down_w.shape[2]), F32),
            pltpu.VMEM((2, 3, tokens, part), BF),
            pltpu.SemaphoreType.DMA((9,)),
        ],
        compiler_params=params(wide_limit(gate_w, 30)),
        name="post",
    )(state, attended, placed(attn_w), gain, router, active, placed(gate_w), placed(up_w),
      placed(down_w))
    names = ("state_out", "ffn_in", "gate", "up", "hidden", "midway", "update", "routed")
    return dict(zip(names, made))


def post_back_kernel(
    used, cols, grad_state, update, routed, active, state, midway, gain, router, attn_w,
    gate_w, up_w, down_w, gate_pre, up_pre,
    grad_attended, partial, gain_grad, router_grad, ffn_out, gate_out, up_out, branch_out,
    scaled, total, grad_ffn, grad_branch, fetched, stage, load, sems,
):
    pieces, _, part = gate_w.shape
    low_col = used // LANE * LANE

    def ship(index, source, target):
        return pltpu.make_async_copy(source, target, sems.at[index])

    def ship_piece(piece):
        spot = lax.rem(piece, 2)
        return [
            ship(2 + 2 * spot + index, stage.at[spot, index], out.at[piece])
            for index, out in enumerate((gate_out, up_out))
        ]

    def fetch(piece):
        spot = lax.rem(piece, 2)
        return [
            pltpu.make_async_copy(ref.at[piece], fetched.at[spot, index], load.at[spot, index])
            for index, ref in enumerate((gate_pre, up_pre))
        ]

    for copy in fetch(0):
        copy.start()
    chance = routed[:, 0:1]
    weight = active[:, 0:1] * chance
    grad = grad_state[...]
    change = grad * weight
    scaled[...] = change
    slope = jnp.sum(grad * update[...].astype(F32), axis=-1, keepdims=True) * weight * (1.0 - chance)
    router_grad[...] = jnp.sum(state[...] * slope, axis=0, keepdims=True)
    partial[...] = grad + slope * router[...]
    low = change.astype(BF)
    for piece in range(pieces):
        grad_ffn[piece] = jnp.zeros(grad_ffn.shape[1:], BF)
        grad_ffn[piece, :, :cols] = low[:, piece * cols : (piece + 1) * cols]
    ship(0, grad_ffn, ffn_out).start()
    total[...] = jnp.zeros(total.shape, F32)

    def step(piece, carry):
        spot = lax.rem(piece, 2)

        @pl.when(piece + 1 < pieces)
        def _():
            for copy in fetch(piece + 1):
                copy.start()

        @pl.when(piece >= 2)
        def _():
            for copy in ship_piece(piece - 2):
                copy.wait()

        for copy in fetch(piece):
            copy.wait()
        rows = pl.ds(pl.multiple_of(piece * part, part), part)
        grad_hidden = dot(side_by_side(grad_ffn), side_by_side(down_w, rows), NT)
        gate = fetched[spot, 0].astype(F32)
        chance = 1.0 / (1.0 + jnp.exp(-gate))
        smooth = gate * chance
        slope = chance + smooth * (1.0 - chance)
        grad_gate = (grad_hidden * fetched[spot, 1].astype(F32) * slope).astype(BF)
        grad_up = (grad_hidden * smooth).astype(BF)
        stage[spot, 0] = grad_gate
        stage[spot, 1] = grad_up
        total[...] += dot(
            jnp.concatenate([grad_gate, grad_up], axis=1),
            jnp.concatenate([gate_w[piece], up_w[piece]], axis=1),
            NT,
        )
        for copy in ship_piece(piece):
            copy.start()
        return carry

    lax.fori_loop(0, pieces, step, 0)
    grad_midway, grad_gain = norm_back(total[...], midway[...], gain[...])
    gain_grad[...] = grad_gain
    partial[...] = partial[...] + grad_midway
    low = (scaled[...] + grad_midway).astype(BF)
    shift = used - low_col
    for piece in range(pieces):
        if grad_branch.shape[2] > cols:
            grad_branch[piece] = jnp.zeros(grad_branch.shape[1:], BF)
        grad_branch[piece, :, shift : shift + cols] = low[:, piece * cols : (piece + 1) * cols]
    ship(1, grad_branch, branch_out).start()
    grad = None
    for piece in range(pieces):
        made = dot(grad_branch[piece], attn_w[piece, :, low_col:], NT)
        grad = made if grad is None else grad + made
    grad_attended[...] = grad.astype(BF)
    ship(0, grad_ffn, ffn_out).wait()
    ship(1, grad_branch, branch_out).wait()
    for piece in range(max(0, pieces - 2), pieces):
        for copy in ship_piece(piece):
            copy.wait()


def post_back(grad_state, s, gain, router, attn_w, gate_w, up_w, down_w, used):
    state = s["state"]
    tokens, width = state.shape
    pieces, _, part = gate_w.shape
    branch_dims = (pieces, tokens, attn_w.shape[2] - used // LANE * LANE)
    ffn_dims = (pieces, tokens, down_w.shape[2])
    made = pl.pallas_call(
        functools.partial(post_back_kernel, used, width // pieces),
        out_shape=(
            shape((tokens, QW), BF),
            shape((tokens, width), F32),
            shape((1, width), F32),
            shape((1, width), F32),
            shape(ffn_dims, BF),
            shape((pieces, tokens, part), BF),
            shape((pieces, tokens, part), BF),
            shape(branch_dims, BF),
        ),
        in_specs=[vmem] * 12 + [anywhere] * 2,
        out_specs=(vmem,) * 4 + (anywhere,) * 4,
        scratch_shapes=[
            pltpu.VMEM((tokens, width), F32),
            pltpu.VMEM((tokens, width), F32),
            pltpu.VMEM(ffn_dims, BF),
            pltpu.VMEM(branch_dims, BF),
            pltpu.VMEM((2, 2, tokens, part), BF),
            pltpu.VMEM((2, 2, tokens, part), BF),
            pltpu.SemaphoreType.DMA((2, 2)),
            pltpu.SemaphoreType.DMA((6,)),
        ],
        compiler_params=params(wide_limit(gate_w, 34)),
        name="post_back",
    )(grad_state, s["update"], s["routed"], s["active"], state, s["midway"], gain, router,
      placed(attn_w), placed(gate_w), placed(up_w), placed(down_w), s["gate"], s["up"])
    names = (
        "grad_attended", "partial", "ffn_gain_grad", "router_grad", "grad_ffn", "grad_gate", "grad_up",
        "grad_branch",
    )
    return dict(zip(names, made))


def pre_back_kernel(cols, blocks, *refs):
    qc, kc = cols
    grad_queries, own, others = refs[0], refs[1], refs[2 : 1 + blocks]
    partial, state, gain, weight, cosine, sine = refs[1 + blocks : 7 + blocks]
    packed, grad_state, gain_grad, qbuf, kbuf = refs[7 + blocks :]
    summed = own[...]
    for ref in others:
        summed = summed + ref[...].astype(F32)
    kbuf[:, :KW] = summed[:, :KW]
    qbuf[:, :QW] = grad_queries[...]
    for buf in (qbuf, kbuf):
        for start in range(0, buf.shape[1], LANE):
            span = slice(start, start + LANE)
            buf[:, span] = turn(buf[:, span], cosine[...], -sine[...])
    low_q = qbuf[...].astype(BF)
    low_k = kbuf[...].astype(BF)
    low_v = summed[:, KW:].astype(BF)
    total = None
    used = packed.shape[2]
    for piece in range(weight.shape[0]):
        packed[piece] = jnp.zeros(packed.shape[1:], BF)
        packed[piece, :, :qc] = low_q[:, piece * qc : (piece + 1) * qc]
        packed[piece, :, qc : qc + kc] = low_k[:, piece * kc : (piece + 1) * kc]
        packed[piece, :, qc + kc : qc + 2 * kc] = low_v[:, piece * kc : (piece + 1) * kc]
        made = dot(packed[piece], weight[piece, :, :used], NT)
        total = made if total is None else total + made
    grad_in, grad_gain = norm_back(total, state[...], gain[...])
    gain_grad[...] = grad_gain
    grad_state[...] = partial[...] + grad_in


def pre_back(grad_queries, grad_pairs, partial, state, gain, weight, cosine, sine, cols):
    tokens, width = state.shape
    used = min(ceil_to(cols[0] + 2 * cols[1], LANE), weight.shape[2])
    return pl.pallas_call(
        functools.partial(pre_back_kernel, cols, len(grad_pairs)),
        out_shape=(
            shape((weight.shape[0], tokens, used), BF),
            shape((tokens, width), F32),
            shape((1, width), F32),
        ),
        in_specs=[vmem] * (7 + len(grad_pairs)),
        out_specs=(vmem,) * 3,
        scratch_shapes=[
            pltpu.VMEM((tokens, ceil_to(QW, LANE)), F32),
            pltpu.VMEM((tokens, ceil_to(KW, LANE)), F32),
        ],
        compiler_params=params(wide_limit(weight, 24)),
        name="pre_back",
    )(grad_queries, *grad_pairs, partial, state, gain, placed(weight), cosine, sine)


def attn_sums_kernel(count, low_col, *refs):
    normed, packed = refs[:count], refs[count : 2 * count]
    attended, branch = refs[2 * count : 3 * count], refs[3 * count : 4 * count]
    out, left, right = refs[4 * count :]

    @pl.when(pl.program_id(0) == 0)
    def _():
        left[...] = jnp.concatenate([ref[...].T for ref in normed], axis=1)
        right[...] = jnp.concatenate([ref[...].T for ref in attended], axis=1)

    first = dot(left[...], jnp.concatenate([ref[0] for ref in packed], axis=0))
    second = dot(right[...], jnp.concatenate([ref[0] for ref in branch], axis=0))
    high_col = first.shape[1]
    if low_col:
        out[0, :, :low_col] = first[:, :low_col].astype(BF)
    out[0, :, low_col:high_col] = (first[:, low_col:] + second[:, : high_col - low_col]).astype(BF)
    if high_col < out.shape[2]:
        out[0, :, high_col:] = second[:, high_col - low_col :].astype(BF)


def attn_sums(normed, packed, attended, branch, low_col, total_cols):
    count = len(normed)
    tokens, width = normed[0].shape
    pieces = packed[0].shape[0]
    row = pl.BlockSpec((tokens, width), lambda s: (0, 0))
    part = pl.BlockSpec((1, tokens, packed[0].shape[2]), lambda s: (s, 0, 0))
    thin = pl.BlockSpec((1, tokens, branch[0].shape[2]), lambda s: (s, 0, 0))
    return pl.pallas_call(
        functools.partial(attn_sums_kernel, count, low_col),
        grid=(pieces,),
        out_shape=shape((pieces, width, total_cols), BF),
        in_specs=[row] * count + [part] * count + [row] * count + [thin] * count,
        out_specs=pl.BlockSpec((1, width, total_cols), lambda s: (s, 0, 0)),
        scratch_shapes=[pltpu.VMEM((width, count * tokens), BF)] * 2,
        compiler_params=params(56),
        name="attn_sums",
    )(*normed, *packed, *attended, *branch)


def pair_sums_kernel(count, *refs):
    normed, first, second = refs[:count], refs[count : 2 * count], refs[2 * count : 3 * count]
    first_out, second_out, left = refs[3 * count :]

    @pl.when(pl.program_id(0) == 0)
    def _():
        left[...] = jnp.concatenate([ref[...].T for ref in normed], axis=1)

    for source, out in ((first, first_out), (second, second_out)):
        out[0] = dot(left[...], jnp.concatenate([ref[0] for ref in source], axis=0)).astype(BF)


def pair_sums(normed, first, second):
    count = len(normed)
    tokens, width = normed[0].shape
    pieces, _, part = first[0].shape
    row = pl.BlockSpec((tokens, width), lambda s: (0, 0))
    chunk = pl.BlockSpec((1, tokens, part), lambda s: (s, 0, 0))
    result = pl.BlockSpec((1, width, part), lambda s: (s, 0, 0))
    return pl.pallas_call(
        functools.partial(pair_sums_kernel, count),
        grid=(pieces,),
        out_shape=(shape((pieces, width, part), BF),) * 2,
        in_specs=[row] * count + [chunk] * (2 * count),
        out_specs=(result, result),
        scratch_shapes=[pltpu.VMEM((width, count * tokens), BF)],
        compiler_params=params(56),
        name="pair_sums",
    )(*normed, *first, *second)


def down_sums_kernel(count, *refs):
    hidden, grads, out, right = refs[:count], refs[count : 2 * count], refs[-2], refs[-1]

    @pl.when(pl.program_id(0) == 0)
    def _():
        for piece in range(out.shape[0]):
            right[piece] = jnp.concatenate([ref[piece] for ref in grads], axis=0)

    left = jnp.concatenate([ref[0].T for ref in hidden], axis=1)
    for piece in range(out.shape[0]):
        out[piece] = dot(left, right[piece]).astype(BF)


def down_sums(hidden, grads):
    count = len(hidden)
    pieces, tokens, part = hidden[0].shape
    cols = grads[0].shape[2]
    return pl.pallas_call(
        functools.partial(down_sums_kernel, count),
        grid=(pieces,),
        out_shape=shape((pieces, pieces * part, cols), BF),
        in_specs=[pl.BlockSpec((1, tokens, part), lambda f: (f, 0, 0))] * count
        + [pl.BlockSpec((pieces, tokens, cols), lambda f: (0, 0, 0))] * count,
        out_specs=pl.BlockSpec((pieces, part, cols), lambda f: (0, f, 0)),
        scratch_shapes=[pltpu.VMEM((pieces, count * tokens, cols), BF)],
        compiler_params=params(56),
        name="down_sums",
    )(*hidden, *grads)


MESH = pl.DeviceIdType.MESH


class Place:
    def __init__(self, layers):
        dp, seq = lax.axis_index("dp"), lax.axis_index("seq")
        self.layers = layers
        self.z, self.core = lax.div(dp, 2), lax.rem(dp, 2)
        self.y, self.x = lax.div(seq, 2), lax.rem(seq, 2)
        self.sibling = (self.z * 2 + 1 - self.core, seq)
        self.over_x = (dp, self.y * 2 + 1 - self.x)
        self.over_y = (dp, (1 - self.y) * 2 + self.x)
        self.up = [(lax.rem(self.z + k, layers) * 2 + self.core, seq) for k in range(layers)]
        self.down = [
            (lax.rem(self.z + layers - k, layers) * 2 + self.core, seq) for k in range(layers)
        ]
        self.peers = [self.sibling, self.over_x, self.over_y] + self.up[1:]

    def greet(self):
        barrier = pltpu.get_barrier_semaphore()
        for peer in self.peers:
            pl.semaphore_signal(barrier, inc=1, device_id=peer, device_id_type=MESH)
        pl.semaphore_wait(barrier, len(self.peers))


def remote(source, target, sems, peer):
    return pltpu.make_async_remote_copy(
        src_ref=source, dst_ref=target, send_sem=sems[0], recv_sem=sems[1],
        device_id=peer, device_id_type=MESH,
    )


def gather_kernel(count, layers, *refs):
    ins, outs = refs[:count], refs[count : 2 * count]
    send, recv, keep = refs[2 * count :]
    here = Place(layers)
    here.greet()
    y, x, z, core = here.y, here.x, here.z, here.core
    sent = []

    def slot(a, index):
        return send.at[a, index], recv.at[a, index]

    def start(a, index, source, target, peer):
        copy = remote(source, target, slot(a, index), peer)
        copy.start()
        sent.append(copy)

    def arrive(a, index, landing):
        remote(landing, landing, slot(a, index), here.sibling).wait_recv()

    def layer(k):
        return lax.rem(z + layers - k, layers)

    def sides(a):
        if a % 2 == 0:
            return here.over_x, here.over_y, (y, 1 - x), ((1 - y, x), (1 - y, 1 - x))
        return here.over_y, here.over_x, (1 - y, x), ((y, 1 - x), (1 - y, 1 - x))

    own = [pltpu.make_async_copy(ins[a], outs[a].at[y, x, z, core], keep.at[a]) for a in range(count)]
    for copy in own:
        copy.start()

    def first(k):
        for a in range(count):
            spot = outs[a].at[y, x, layer(k), core]
            source = ins[a] if k == 0 else spot
            if k:
                arrive(a, k, spot)
            start(a, layers + k, source, spot, sides(a)[0])
            start(a, 2 * layers + k, source, spot, sides(a)[1])

    def second(k):
        for a in range(count):
            side = sides(a)[2]
            spot = outs[a].at[side[0], side[1], layer(k), core]
            arrive(a, layers + k, spot)
            start(a, 3 * layers + k, spot, spot, sides(a)[1])

    def third(k):
        for a in range(count):
            for turn_of, side in enumerate(sides(a)[3]):
                arrive(a, (2 + turn_of) * layers + k, outs[a].at[side[0], side[1], layer(k), core])
            if k == 0:
                own[a].wait()
            spot = outs[a].at[:, :, layer(k), core]
            start(a, 4 * layers + k, spot, spot, here.sibling)

    def z_sends(k):
        for a in range(count):
            start(a, k, ins[a], outs[a].at[y, x, z, core], here.up[k])

    for a in range(count):
        for k in range(1, layers):
            start(a, k, ins[a], outs[a].at[y, x, z, core], here.up[k])
    for k in range(layers + 2):
        if k < layers:
            first(k)
        if 1 <= k <= layers:
            second(k - 1)
        if k >= 2:
            third(k - 2)
    for k in range(layers):
        for a in range(count):
            arrive(a, 4 * layers + k, outs[a].at[:, :, layer(k), 1 - core])
    for copy in sent:
        copy.wait_send()


def gather_all(parts, layers):
    count = len(parts)
    return pl.pallas_call(
        functools.partial(gather_kernel, count, layers),
        out_shape=tuple(pltpu.VMEM((2, 2, layers, 2) + part.shape, part.dtype) for part in parts),
        in_specs=[anywhere] * count,
        out_specs=(anywhere,) * count,
        scratch_shapes=[
            pltpu.SemaphoreType.DMA((count, 5 * layers)),
            pltpu.SemaphoreType.DMA((count, 5 * layers)),
            pltpu.SemaphoreType.DMA((count,)),
        ],
        compiler_params=pltpu.CompilerParams(
            collective_id=0, has_side_effects=True, vmem_limit_bytes=4 * MIB
        ),
        name="gather_all",
    )(*parts)


def unpack_kernel(rows, down_rows, micros, down, gains, info, active):
    spot = down.shape[2] - LANE
    first = LANE - BESIDE
    late = second_micro()
    outer = is_outer()
    here = pl.ds(pl.multiple_of(lax.axis_index("dp") * down_rows, BESIDE), active.shape[1] // 2)
    block = active.shape[1] // 2
    for rank in range(down.shape[1] // down_rows):
        tile = down[0, rank * down_rows : rank * down_rows + LANE, spot:].astype(F32).T
        gains[:, rank * rows : (rank + 1) * rows] = tile[first : first + gains.shape[0], :rows]
    info[...] = jnp.zeros(info.shape, F32)
    for index, (one, two) in enumerate(zip((0, 3, 1, 2), (1, 2, 0, 3))):
        tile = down[jnp.where(outer, one, two), here, spot:].astype(F32)
        turned = tile.T
        span = slice(index * block, (index + 1) * block)
        for row in range(2):
            start = first + 2 + RECUR + row * micros
            info[row : row + 1, span] = jnp.where(
                late, turned[start + 1 : start + 2], turned[start : start + 1]
            )
        if index < 2:
            depth = jnp.where(late, tile[:, start + 1 : start + 2], tile[:, start : start + 1])
            for r in range(RECUR):
                active[r, span] = jnp.broadcast_to(jnp.where(depth > r, 1.0, 0.0), (block, LANE))


def unpack(down, rows, tokens, ranks, micros):
    down_rows = down.shape[1] // ranks
    return pl.pallas_call(
        functools.partial(unpack_kernel, rows, down_rows, micros),
        out_shape=(
            shape((8, rows * ranks), F32),
            shape((8, 4 * tokens), F32),
            shape((RECUR, 2 * tokens, LANE), F32),
        ),
        in_specs=[vmem],
        out_specs=(vmem,) * 3,
        compiler_params=params(8),
        name="unpack",
    )(pin(down))


def finish_kernel(layers, count, low_col, *refs):
    refs = list(refs)

    def pop(size):
        taken = refs[:size]
        del refs[:size]
        return taken

    normed, packed, attended, branch, ffn_in, grad_gate, grad_up, hidden, grad_ffn = (
        pop(count) for _ in range(9)
    )
    (small,) = pop(1)
    outs = pop(4)
    held, core_in, first_in, second_in, done, z_in = (pop(4) for _ in range(6))
    raw, left, right, ffn_right, stage, down_stage = pop(6)
    send, recv, keep, load = refs
    here = Place(layers)
    here.greet()
    y, x, z, core = here.y, here.x, here.z, here.core
    tokens = raw.shape[0] // count
    sent = []

    def slot(a, index):
        return send.at[a, index], recv.at[a, index]

    def start(a, index, source, target, peer):
        copy = remote(source, target, slot(a, index), peer)
        copy.start()
        sent.append(copy)

    def arrive(a, index, landing):
        remote(landing, landing, slot(a, index), here.sibling).wait_recv()

    def layer(k):
        return lax.rem(z + k + 1, layers)

    def added(ref, one, two):
        return (one.astype(F32) + two.astype(F32)).astype(ref.dtype)

    def load_left(index, sources):
        return [
            pltpu.make_async_copy(ref, raw.at[pl.ds(i * tokens, tokens)], load.at[index, i])
            for i, ref in enumerate(sources)
        ]

    def load_right(index, spot, sources, piece, start_col):
        width = sources[0].shape[2]
        return [
            pltpu.make_async_copy(
                ref.at[piece],
                right.at[spot, pl.ds(i * tokens, tokens), pl.ds(start_col, width)],
                load.at[index + spot, i],
            )
            for i, ref in enumerate(sources)
        ]

    def go(copies):
        for copy in copies:
            copy.start()

    def hold(copies):
        for copy in copies:
            copy.wait()

    def turn_left(spot):
        for i in range(count):
            rows = slice(i * tokens, (i + 1) * tokens)
            left[spot, :, rows] = raw[rows].T

    def sends(a, piece, source):
        if a == 3:
            theirs = source.at[:, :, 1 - core]
            ours = source.at[:, :, core]
            spot = (piece,)
        else:
            theirs = source.at[:, 1 - core]
            ours = source.at[:, core]
            spot = (slice(None), lax.div(piece, 2), lax.rem(piece, 2))
        return (
            remote(
                theirs, core_in[a].at[spot], (send.at[a, piece], recv.at[a, piece]), here.sibling
            ),
            pltpu.make_async_copy(ours, held[a].at[spot], keep.at[a, piece]),
        )

    def products(a, fetch, multiply, stages):
        go(fetch(0, 0))

        def step(piece, carry):
            spot = lax.rem(piece, 2)
            hold(fetch(piece, spot))

            @pl.when(piece < 3)
            def _():
                go(fetch(piece + 1, 1 - spot))

            @pl.when(piece >= 2)
            def _():
                out, own = sends(a, piece - 2, stages.at[spot])
                out.wait_send()
                own.wait()

            multiply(piece, spot)
            for copy in sends(a, piece, stages.at[spot]):
                copy.start()
            return carry

        lax.fori_loop(0, 4, step, 0)
        for piece in (2, 3):
            out, own = sends(a, piece, stages.at[piece % 2])
            out.wait_send()
            own.wait()

    def store(spot, result):
        rows = stage.shape[3]
        for index in range(2 * layers):
            stage[spot, index // 2, index % 2] = result[index * rows : (index + 1) * rows].astype(BF)

    def ffn_product(which):
        def multiply(piece, spot):
            width = which[0].shape[2]
            store(spot, dot(left[0], right[spot, :, :width]))

        return multiply

    high_col = packed[0].shape[2]
    far_col = branch[0].shape[2]

    def attn_product(piece, spot):
        first = dot(left[1], right[spot, :, :high_col])
        second = dot(left[0], right[spot, :, high_col : high_col + far_col])
        cut = high_col - low_col
        store(
            spot,
            jnp.concatenate(
                [first[:, :low_col], first[:, low_col:] + second[:, :cut], second[:, cut:]], axis=1
            ),
        )

    def down_product(piece, spot):
        part = hidden[0].shape[2]
        turned = jnp.concatenate(
            [right[spot, i * tokens : (i + 1) * tokens, :part].T for i in range(count)], axis=1
        )
        rows = part // 2
        cols = ffn_right.shape[2] - small.shape[3]
        for column in range(4):
            result = dot(turned, ffn_right[column]).astype(BF)
            for index in range(2):
                place = (spot, column // 2, column % 2, index)
                down_stage[place] = result[index * rows : (index + 1) * rows]
                down_stage[place + (slice(None), slice(cols, None))] = small[piece, index]

    def first(a):
        for piece in range(4):
            spot = (piece,) if a == 3 else (slice(None), piece // 2, piece % 2)
            arrive(a, piece, core_in[a].at[spot])
        for k in range(layers):
            held[a][k] = added(held[a], held[a][k], core_in[a][k])
        for k in range(layers):
            if k % 2 == 0:
                start(a, 4 + k, held[a].at[layer(k), :, 1 - x], first_in[a].at[k], here.over_x)
            else:
                start(a, 4 + k, held[a].at[layer(k), 1 - y], first_in[a].at[k], here.over_y)

    def second(a):
        for k in range(layers):
            at = layer(k)
            arrive(a, 4 + k, first_in[a].at[k])
            for i in range(2):
                if k % 2 == 0:
                    held[a][at, i, x] = added(held[a], held[a][at, i, x], first_in[a][k, i])
                else:
                    held[a][at, y, i] = added(held[a], held[a][at, y, i], first_in[a][k, i])
            index = 4 + layers + k
            if k % 2 == 0:
                start(a, index, held[a].at[at, 1 - y, x], second_in[a].at[k], here.over_y)
            else:
                start(a, index, held[a].at[at, y, 1 - x], second_in[a].at[k], here.over_x)

    def third(a):
        for k in range(layers):
            arrive(a, 4 + layers + k, second_in[a].at[k])
            done[a][k] = added(held[a], held[a][layer(k), y, x], second_in[a][k])
            if k < layers - 1:
                index = 4 + 2 * layers + k
                start(a, index, done[a].at[k], z_in[a].at[k], here.up[k + 1])

    def fourth(a):
        total = done[a][layers - 1].astype(F32)
        for k in range(layers - 1):
            arrive(a, 4 + 2 * layers + k, z_in[a].at[k])
            total = total + z_in[a][k].astype(F32)
        outs[a][...] = total

    ffn_left = load_left(0, ffn_in)
    go(ffn_left)
    down_right = [
        pltpu.make_async_copy(
            ref.at[column],
            ffn_right.at[column, pl.ds(i * tokens, tokens)],
            load.at[6 + column, i],
        )
        for i, ref in enumerate(grad_ffn)
        for column in range(4)
    ]

    def fetch_of(index, sources):
        return lambda piece, spot: load_right(index, spot, sources, piece, 0)

    def fetch_attn(piece, spot):
        return load_right(2, spot, packed, piece, 0) + load_right(4, spot, branch, piece, high_col)

    hold(ffn_left)
    turn_left(0)
    normed_left = load_left(1, normed)
    go(normed_left)
    go(down_right)
    products(0, fetch_of(2, grad_gate), ffn_product(grad_gate), stage)
    first(0)
    hold(normed_left)
    turn_left(1)
    attended_left = load_left(0, attended)
    go(attended_left)
    products(1, fetch_of(2, grad_up), ffn_product(grad_up), stage)
    first(1)
    second(0)
    hold(attended_left)
    turn_left(0)
    products(2, fetch_attn, attn_product, stage)
    first(2)
    second(1)
    third(0)
    hold(down_right)
    products(3, fetch_of(2, hidden), down_product, down_stage)
    first(3)
    second(2)
    third(1)
    second(3)
    third(2)
    third(3)
    for a in range(4):
        fourth(a)
    for copy in sent:
        copy.wait_send()


def finish(normed, packed, attended, branch, ffn_in, grad_gate, grad_up, hidden, grad_ffn, small, low_col):
    count = len(normed)
    tokens, width = normed[0].shape
    pieces, _, part = hidden[0].shape
    cols = grad_ffn[0].shape[2]
    layers = small.shape[0]
    ranks = 2 * layers
    rows, down_rows = width // ranks, pieces * part // ranks
    wide = packed[0].shape[2] + branch[0].shape[2]
    ends = [(rows, part), (rows, part), (rows, part), (down_rows, cols)]

    def buffers(*lead):
        return [pltpu.VMEM(lead + end, BF) for end in ends]

    operands = (
        *normed, *packed, *attended, *branch, *ffn_in, *grad_gate, *grad_up, *hidden, *grad_ffn, small,
    )
    return pl.pallas_call(
        functools.partial(finish_kernel, layers, count, low_col),
        out_shape=tuple(shape(end, F32) for end in ends),
        in_specs=[anywhere] * (len(operands) - 1) + [vmem],
        out_specs=(vmem,) * 4,
        scratch_shapes=[
            *buffers(layers, 2, 2),
            *buffers(layers, 2, 2),
            *buffers(layers, 2),
            *buffers(layers),
            *buffers(layers),
            *buffers(layers - 1),
            pltpu.VMEM((count * tokens, width), BF),
            pltpu.VMEM((2, width, count * tokens), BF),
            pltpu.VMEM((2, count * tokens, max(wide, part)), BF),
            pltpu.VMEM((pieces, count * tokens, cols), BF),
            pltpu.VMEM((2, layers, 2, rows, part), BF),
            pltpu.VMEM((2, 2, 2, 2, down_rows, cols), BF),
            pltpu.SemaphoreType.DMA((4, 4 + 3 * layers)),
            pltpu.SemaphoreType.DMA((4, 4 + 3 * layers)),
            pltpu.SemaphoreType.DMA((4, 4)),
            pltpu.SemaphoreType.DMA((10, count)),
        ],
        compiler_params=pltpu.CompilerParams(
            collective_id=1, has_side_effects=True, vmem_limit_bytes=61 * MIB
        ),
        name="finish",
    )(*operands)


def rope_tables(positions):
    half = HEAD_DIM // 2
    frequency = rope_base ** (-(jnp.arange(half, dtype=F32) * 2.0 / HEAD_DIM))
    angles = positions.astype(F32)[:, None] * frequency[None, :]
    cosine, sine = jnp.cos(angles), jnp.sin(angles)
    repeat = LANE // HEAD_DIM
    return (
        jnp.concatenate([cosine, cosine] * repeat, axis=1),
        jnp.concatenate([-sine, sine] * repeat, axis=1),
    )


def pass_on(array, step, count):
    return lax.ppermute(array, "seq", [(i, i + step) for i in range(count - step)])


def pass_back(array, step, count):
    return lax.ppermute(array, "seq", [(i + step, i) for i in range(count - step)])


def row_plan(inputs, cotangent, depths, marks, block_params):
    micros, _, tokens, _ = inputs.shape
    seq, mine = lax.axis_size("seq"), lax.axis_index("seq")
    attn_g, ffn_g, routers, attn_w, gate_w, up_w, down_w, cols, used = block_params
    order = mine - jnp.arange(seq)
    marks = jnp.where((order >= 0)[:, None, None, None], marks[order % seq], -1.0)
    marks = marks.transpose(2, 1, 0, 3).reshape(micros, 2, seq * tokens)
    infos = [jnp.pad(marks[m], ((0, 6), (0, 0))) for m in range(micros)]
    cosine, sine = rope_tables(mine * tokens + jnp.arange(tokens, dtype=jnp.int32))
    states = [inputs[m, 0] for m in range(micros)]
    actives = [
        [
            jnp.broadcast_to((depths[m, 0] > r).astype(F32)[:, None], (tokens, LANE))
            for r in range(RECUR)
        ]
        for m in range(micros)
    ]
    saved = [[None] * RECUR for _ in range(micros)]
    for r in range(RECUR):
        made = []
        for m in range(micros):
            normed, queries, pair = pre_part(states[m], attn_g, attn_w, cosine, sine, cols)
            pairs = [pair] + [pass_on(pair, step, seq) for step in range(1, seq)]
            made.append((normed, queries, pairs))
        for m in range(micros):
            normed, queries, pairs = made[m]
            attended, logs = attend(queries, pairs, infos[m], r)
            after = post_part(
                states[m], attended, attn_w, ffn_g, routers[r], actives[m][r], gate_w, up_w, down_w, used
            )
            saved[m][r] = dict(
                after, state=states[m], normed=normed, queries=queries, pairs=pairs,
                attended=attended, logs=logs, active=actives[m][r],
            )
            states[m] = after["state_out"]
    grads = [cotangent[m, 0] for m in range(micros)]
    for r in reversed(range(RECUR)):
        partials = []
        for m in range(micros):
            s = saved[m][r]
            s.update(post_back(grads[m], s, ffn_g, routers[r], attn_w, gate_w, up_w, down_w, used))
            grad_queries, *grad_pairs = attend_back(
                s["queries"], s["pairs"], infos[m], s["attended"], s["logs"], s["grad_attended"], r
            )
            grad_pairs = [grad_pairs[0]] + [
                pass_back(grad_pairs[step], step, seq) for step in range(1, seq)
            ]
            partials.append((grad_queries, grad_pairs))
        for m in range(micros):
            s = saved[m][r]
            s["packed"], grads[m], s["attn_gain_grad"] = pre_back(
                *partials[m], s["partial"], s["state"], attn_g, attn_w, cosine, sine, cols
            )
    outputs = jnp.stack(states, axis=0)[:, None]
    input_grad = jnp.stack(grads, axis=0)[:, None]
    return outputs, input_grad, saved


def swap(array, pairs):
    seq, ranks = lax.axis_size("seq"), lax.axis_size("dp")
    moves = []
    for rank in range(ranks):
        for one, two in pairs[rank % 2]:
            moves += [(rank * seq + one, rank * seq + two), (rank * seq + two, rank * seq + one)]
    return lax.ppermute(array, ("dp", "seq"), moves)


ACROSS = (((0, 3), (1, 2)),) * 2
PARTNERS = (((0, 1), (2, 3)), ((0, 2), (1, 3)))


def second_micro():
    place = lax.axis_index("seq")
    return jnp.where(lax.axis_index("dp") % 2 == 0, place >= 2, place % 2 == 1)


def paired_start(inputs, cotangent):
    tokens = inputs.shape[2]
    second = second_micro()
    outer = is_outer()

    def split(array):
        own = jnp.where(second, array[1, 0], array[0, 0])
        return own, jnp.where(second, array[0, 0], array[1, 0]).astype(BF)

    places = jnp.arange(tokens, dtype=jnp.int32)
    low, high = jnp.where(outer, 0, 1), jnp.where(outer, 3, 2)
    tables = rope_tables(jnp.concatenate([low * tokens + places, high * tokens + places]))
    return split(inputs), split(cotangent), tables


def paired_plan(prepared, info, actives, block_params):
    (own_state, other_state), (own_grad, other_grad), (cosine, sine) = prepared
    tokens = own_state.shape[0]
    late = lax.axis_index("seq") >= 2
    attn_g, ffn_g, routers, attn_w, gate_w, up_w, down_w, cols, used = block_params

    def join(own, other):
        other = other.astype(F32)
        return jnp.concatenate([jnp.where(late, other, own), jnp.where(late, own, other)], axis=0)

    def give(array):
        low, high = array[:tokens], array[tokens:]
        own = jnp.where(late, high, low)
        other = swap(jnp.where(late, low, high).astype(BF), ACROSS).astype(F32)
        second = second_micro()
        return jnp.stack([jnp.where(second, other, own), jnp.where(second, own, other)], axis=0)[:, None]

    state = join(own_state, other_state)
    saved = []
    for r in range(RECUR):
        active = actives[r]
        normed, queries, pair = pre_part(state, attn_g, attn_w, cosine, sine, cols)
        partner = swap(pair, PARTNERS)
        if r == 0:
            other_grad, partner = lax.optimization_barrier((other_grad, partner))
            other_grad = swap(other_grad, ACROSS)
        part = attend_own(queries, pair, info, r)
        attended, logs = attend_rest(queries, partner, info, part, r)
        after = post_part(
            state, attended, attn_w, ffn_g, routers[r], active, gate_w, up_w, down_w, used
        )
        saved.append(
            dict(
                after, state=state, normed=normed, queries=queries, pair=pair, partner=partner,
                attended=attended, logs=logs, active=active,
            )
        )
        state = after["state_out"]
    outputs = give(state)
    grad = join(own_grad, other_grad)
    for r in reversed(range(RECUR)):
        s = saved[r]
        s.update(post_back(grad, s, ffn_g, routers[r], attn_w, gate_w, up_w, down_w, used))
        grad_partner, part, deltas = attend_rest_back(
            s["queries"], s["partner"], info, s["attended"], s["logs"], s["grad_attended"], r
        )
        grad_partner = swap(grad_partner, PARTNERS)
        grad_queries, grad_pair = attend_own_back(
            s["queries"], s["pair"], info, s["logs"], deltas, s["grad_attended"], part, r
        )
        s["packed"], grad, s["attn_gain_grad"] = pre_back(
            grad_queries, [grad_pair, grad_partner], s["partial"], s["state"], attn_g, attn_w,
            cosine, sine, cols,
        )
    return outputs, give(grad), [saved]


def local(
    inputs, cotangent, segments, depths, query_weight, key_weight, value_weight, out_weight,
    gate_weight, up_weight, down_weight, attn_gain, ffn_gain, router_weight,
):
    micros, _, tokens, width = inputs.shape
    seq, ranks = lax.axis_size("seq"), lax.axis_size("dp")
    rows = query_weight.shape[0]
    qc, kc = query_weight.shape[1], key_weight.shape[1]
    both = ("seq", "dp")

    attn_local = jnp.concatenate([query_weight, key_weight, value_weight, out_weight], axis=1)
    down_rows, down_cols = down_weight.shape
    marks = jnp.concatenate([segments[:, 0], depths[:, 0]], axis=0).T.astype(BF)
    small = jnp.concatenate([attn_gain[:, None], ffn_gain[:, None], router_weight], axis=1)
    small = jnp.concatenate(
        [
            jnp.pad(small, ((0, down_rows - rows), (0, 0))),
            jnp.pad(marks, ((0, down_rows - tokens), (0, BESIDE - 2 - RECUR - 2 * micros))),
        ],
        axis=1,
    )
    parts = (
        attn_local, gate_weight, up_weight, jnp.concatenate([down_weight, small], axis=1)
    )
    direct = micros == 2 and (seq, ranks) == (4, 8)
    if direct:
        states, grads, tables = paired_start(inputs, cotangent)
        states = (states[0], swap(states[1], ACROSS))
        parts, own, grads, tables = lax.optimization_barrier((parts, states[0], grads, tables))
        gathered = gather_all(parts, ranks // 2)
        prepared = ((own, states[1]), grads, tables)
    else:
        gathered = [lax.all_gather(part, both, axis=0, tiled=False) for part in parts]
    attn_w, gate_w, up_w, down_w = (full.reshape(seq, -1, full.shape[-1]) for full in gathered)
    if direct:
        small, info, actives = unpack(down_w, rows, tokens, ranks, micros)
    else:
        small = down_w[:, :, down_cols:].reshape(seq, ranks, down_rows, BESIDE).astype(F32)
        marks = lax.dynamic_index_in_dim(small, lax.axis_index("dp"), 1, keepdims=False)
        marks = marks[:, :tokens, 2 + RECUR : 2 + RECUR + 2 * micros].transpose(0, 2, 1)
        marks = marks.reshape(seq, 2, micros, tokens)
        small = small[0, :, :rows, : 2 + RECUR].reshape(width, 2 + RECUR).T
    attn_g, ffn_g = small[0:1], small[1:2]
    routers = [small[2 + r : 3 + r] for r in range(RECUR)]
    used = qc + 2 * kc
    total_cols = attn_w.shape[2]
    low_col = used // LANE * LANE
    block_params = (attn_g, ffn_g, routers, attn_w, gate_w, up_w, down_w, (qc, kc), used)
    if direct:
        outputs, input_grad, saved = paired_plan(prepared, info, actives, block_params)
    else:
        outputs, input_grad, saved = row_plan(inputs, cotangent, depths, marks, block_params)
    flat = [steps[r] for r in reversed(range(RECUR)) for steps in saved]

    def every(name):
        return [s[name] for s in flat]

    attn_gain_sum, ffn_gain_sum = sum(every("attn_gain_grad")), sum(every("ffn_gain_grad"))
    router_sums = [sum(steps[r]["router_grad"] for steps in saved) for r in range(RECUR)]
    small_sum = jnp.concatenate([attn_gain_sum, ffn_gain_sum, *router_sums], axis=0)
    small_sum = small_sum.T.reshape(ranks, rows, 2 + RECUR)
    if direct:
        small_sum = jnp.pad(
            small_sum, ((0, 0), (0, down_rows - rows), (0, BESIDE - 2 - RECUR))
        ).astype(BF)
        gate_grad, up_grad, attn_grad, down_grad = finish(
            every("normed"), every("packed"), every("attended"), every("grad_branch"),
            every("ffn_in"), every("grad_gate"), every("grad_up"), every("hidden"),
            every("grad_ffn"), small_sum.reshape(ranks // 2, 2, down_rows, BESIDE), low_col,
        )
        small_own = down_grad[:rows, down_cols : down_cols + 2 + RECUR].T
    else:
        down_sum = down_sums(every("hidden"), every("grad_ffn"))
        gate_sum, up_sum = pair_sums(every("ffn_in"), every("grad_gate"), every("grad_up"))
        attn_sum = attn_sums(
            every("normed"), every("packed"), every("attended"), every("grad_branch"),
            low_col, total_cols,
        )
        small_sum = jnp.broadcast_to(small_sum[None], (seq,) + small_sum.shape)
        sums = [
            part.reshape(seq, ranks, -1, part.shape[-1])
            for part in (gate_sum, up_sum, attn_sum, down_sum, small_sum)
        ]
        sums = [lax.psum_scatter(part, "seq", scatter_dimension=0) for part in sums]
        sums = [lax.psum_scatter(part, "dp", scatter_dimension=0).astype(F32) for part in sums]
        gate_grad, up_grad, attn_grad, down_grad, small_own = sums
        small_own = small_own.T
    down_grad = down_grad[:, :down_cols]

    return (
        outputs,
        input_grad,
        attn_grad[:, :qc],
        attn_grad[:, qc : qc + kc],
        attn_grad[:, qc + kc : used],
        attn_grad[:, used:],
        gate_grad,
        up_grad,
        down_grad,
        small_own[0],
        small_own[1],
        small_own[2:].T,
    )


def solution(mesh):
    data = P(None, "dp", "seq", None)
    marks = P(None, "dp", "seq")
    weight = P("dp", "seq")
    in_specs = (data, data, marks, marks) + (weight,) * 7 + (P("dp"), P("dp"), P("dp", None))
    out_specs = (data, data) + (weight,) * 7 + (P("dp"), P("dp"), P("dp", None))
    return jax.shard_map(local, mesh=mesh, in_specs=in_specs, out_specs=out_specs, check_vma=False)
```

```python
import functools

import jax
import jax.numpy as jnp
from jax import lax
from jax.experimental import pallas as pl
from jax.experimental.pallas import tpu as pltpu
from jax.sharding import PartitionSpec as P

HEADS = 15
KV_HEADS = 5
HEAD_DIM = 64
RECUR = 3
GROUP = HEADS // KV_HEADS
KW = KV_HEADS * HEAD_DIM
QW = HEADS * HEAD_DIM
LANE = 128
MIB = 2**20
BESIDE = 16

epsilon = 1e-05
rope_base = 10000.0

NN = (((1,), (0,)), ((), ()))
NT = (((1,), (1,)), ((), ()))
BF = jnp.bfloat16
F32 = jnp.float32

vmem = pl.BlockSpec(memory_space=pltpu.VMEM)


def dot(left, right, dims=NN):
    return lax.dot_general(left, right, dims, preferred_element_type=F32)


def ceil_to(size, unit):
    return -(-size // unit) * unit


def shape(dims, dtype):
    return jax.ShapeDtypeStruct(dims, dtype)


def params(limit):
    return pltpu.CompilerParams(vmem_limit_bytes=limit * MIB)


def pin(array):
    return pltpu.with_memory_space_constraint(array, pltpu.VMEM)


def wide_limit(weight, limit):
    return limit if whole_lanes(weight) else 62


def whole_lanes(weight):
    return weight.shape[-1] % LANE == 0


def placed(weight):
    return pin(weight) if whole_lanes(weight) else weight


def side_by_side(ref, rows=slice(None)):
    return jnp.concatenate([ref[piece, rows] for piece in range(ref.shape[0])], axis=1)


def turn(block, cosine, sine):
    lanes = lax.broadcasted_iota(jnp.int32, block.shape, 1) % HEAD_DIM
    partner = jnp.where(
        lanes < HEAD_DIM // 2,
        pltpu.roll(block, LANE - HEAD_DIM // 2, 1),
        pltpu.roll(block, HEAD_DIM // 2, 1),
    )
    return block * cosine + partner * sine


def norm_back(grad_out, values_in, gain):
    inverse = lax.rsqrt(jnp.mean(values_in * values_in, axis=-1, keepdims=True) + epsilon)
    weighted = grad_out * gain
    inner = jnp.mean(weighted * values_in, axis=-1, keepdims=True)
    grad_gain = jnp.sum(grad_out * values_in * inverse, axis=0, keepdims=True)
    return weighted * inverse - values_in * (inverse * inverse * inverse * inner), grad_gain


def pre_kernel(cols, state, gain, weight, cosine, sine, normed, queries, pair, qbuf, kbuf):
    qc, kc = cols
    values_in = state[...]
    inverse = lax.rsqrt(jnp.mean(values_in * values_in, axis=-1, keepdims=True) + epsilon)
    low = (values_in * inverse * gain[...]).astype(BF)
    normed[...] = low
    used = min(ceil_to(qc + 2 * kc, LANE), weight.shape[2])
    for piece in range(weight.shape[0]):
        made = dot(low, weight[piece, :, :used])
        qbuf[:, piece * qc : (piece + 1) * qc] = made[:, :qc]
        kbuf[:, piece * kc : (piece + 1) * kc] = made[:, qc : qc + kc]
        pair[:, KW + piece * kc : KW + (piece + 1) * kc] = made[:, qc + kc : qc + 2 * kc].astype(BF)
    for buf, out, width, scale in ((qbuf, queries, QW, HEAD_DIM**-0.5), (kbuf, pair, KW, 1.0)):
        for start in range(0, width, LANE):
            stop = min(start + LANE, width)
            turned = turn(buf[:, start : start + LANE], cosine[...], sine[...]) * scale
            out[:, start:stop] = turned[:, : stop - start].astype(BF)


def pre_part(state, gain, weight, cosine, sine, cols):
    tokens, width = state.shape
    return pl.pallas_call(
        functools.partial(pre_kernel, cols),
        out_shape=(
            shape((tokens, width), BF),
            shape((tokens, QW), BF),
            shape((tokens, 2 * KW), BF),
        ),
        in_specs=[vmem] * 5,
        out_specs=(vmem,) * 3,
        scratch_shapes=[
            pltpu.VMEM((tokens, ceil_to(QW, LANE)), F32),
            pltpu.VMEM((tokens, ceil_to(KW, LANE)), F32),
        ],
        compiler_params=params(wide_limit(weight, 14)),
        name="pre",
    )(state, gain, placed(weight), cosine, sine)


def fill_bias(info, bias, recursion):
    keys, tokens = bias.shape
    columns = info[...].T
    place = lax.broadcasted_iota(jnp.int32, (keys, tokens), 0)
    query = lax.broadcasted_iota(jnp.int32, (keys, tokens), 1)
    apart = place % tokens - place // tokens * tokens - query
    same = columns[:, 0:1] == info[0:1, 0:tokens]
    live = columns[:, 1:2] > recursion
    seen = same & (((apart < 0) & live) | (apart == 0))
    bias[...] = jnp.where(seen, 0.0, -1e30)


def head_cols(head):
    return slice(head * HEAD_DIM, (head + 1) * HEAD_DIM)


def stack_heads(ref, group):
    heads = range(group * GROUP, (group + 1) * GROUP)
    return jnp.concatenate([ref[:, head_cols(head)] for head in heads], axis=0)


def attend_kernel(blocks, recursion, *refs):
    queries, pairs = refs[0], refs[1 : 1 + blocks]
    info, attended, logs, bias = refs[1 + blocks :]
    tokens = queries.shape[0]
    keys = blocks * tokens
    fill_bias(info, bias, recursion)
    logs[...] = jnp.zeros(logs.shape, F32)
    for group in range(KV_HEADS):
        key = jnp.concatenate([ref[:, head_cols(group)] for ref in pairs], axis=0)
        value = jnp.concatenate([ref[:, head_cols(KV_HEADS + group)] for ref in pairs], axis=0)
        value_t = jnp.concatenate([value.T, jnp.ones((16, keys), BF)], axis=0)
        query = stack_heads(queries, group)
        scores = dot(key, query, NT) + jnp.concatenate([bias[...]] * GROUP, axis=1)
        top = jnp.max(scores, axis=0, keepdims=True)
        weights = jnp.exp(scores - top).astype(BF)
        mixed = dot(value_t, weights)
        total = mixed[HEAD_DIM : HEAD_DIM + 1]
        mixed = mixed[:HEAD_DIM] * (1.0 / total)
        log_total = top + jnp.log(total)
        for offset in range(GROUP):
            head = group * GROUP + offset
            span = slice(offset * tokens, (offset + 1) * tokens)
            attended[:, head_cols(head)] = mixed[:, span].T.astype(BF)
            logs[head : head + 1, :] = log_total[:, span]


def attend(queries, pairs, info, recursion):
    tokens = queries.shape[0]
    blocks = len(pairs)
    return pl.pallas_call(
        functools.partial(attend_kernel, blocks, recursion),
        out_shape=(shape((tokens, QW), BF), shape((ceil_to(HEADS, 8), tokens), F32)),
        in_specs=[vmem] * (2 + blocks),
        out_specs=(vmem, vmem),
        scratch_shapes=[pltpu.VMEM((blocks * tokens, tokens), F32)],
        compiler_params=params(40),
        name="attend",
    )(queries, *pairs, info)


def attend_back_kernel(blocks, recursion, *refs):
    queries, pairs = refs[0], refs[1 : 1 + blocks]
    info, attended, logs, grad, grad_queries = refs[1 + blocks : 6 + blocks]
    grad_pairs, bias = refs[6 + blocks : 6 + 2 * blocks], refs[6 + 2 * blocks]
    tokens = queries.shape[0]
    fill_bias(info, bias, recursion)
    product = (attended[...].astype(F32) * grad[...].astype(F32)).T
    for group in range(KV_HEADS):
        key = jnp.concatenate([ref[:, head_cols(group)] for ref in pairs], axis=0)
        value = jnp.concatenate([ref[:, head_cols(KV_HEADS + group)] for ref in pairs], axis=0)
        key_t = key.T
        query = stack_heads(queries, group)
        grad_mixed = stack_heads(grad, group)
        heads = range(group * GROUP, (group + 1) * GROUP)
        delta = jnp.concatenate(
            [jnp.sum(product[head_cols(head)], axis=0, keepdims=True) for head in heads], axis=1
        )
        log_total = jnp.concatenate([logs[head : head + 1, :] for head in heads], axis=1)
        scores = dot(key, query, NT) + jnp.concatenate([bias[...]] * GROUP, axis=1)
        probs = jnp.exp(scores - log_total)
        grad_probs = dot(value, grad_mixed, NT)
        grad_scores = (probs * (grad_probs - delta)).astype(BF)
        grad_value = dot(probs.astype(BF), grad_mixed)
        grad_key = dot(grad_scores, query)
        grad_query = dot(key_t, grad_scores) * HEAD_DIM**-0.5
        for offset, head in enumerate(heads):
            span = slice(offset * tokens, (offset + 1) * tokens)
            grad_queries[:, head_cols(head)] = grad_query[:, span].T
        for block, ref in enumerate(grad_pairs):
            rows = slice(block * tokens, (block + 1) * tokens)
            ref[:, head_cols(group)] = grad_key[rows].astype(ref.dtype)
            ref[:, head_cols(KV_HEADS + group)] = grad_value[rows].astype(ref.dtype)


def attend_back(queries, pairs, info, attended, logs, grad, recursion):
    tokens = queries.shape[0]
    blocks = len(pairs)
    return pl.pallas_call(
        functools.partial(attend_back_kernel, blocks, recursion),
        out_shape=(shape((tokens, QW), F32), shape((tokens, 2 * KW), F32))
        + (shape((tokens, 2 * KW), BF),) * (blocks - 1),
        in_specs=[vmem] * (5 + blocks),
        out_specs=(vmem,) * (1 + blocks),
        scratch_shapes=[pltpu.VMEM((blocks * tokens, tokens), F32)],
        compiler_params=params(48),
        name="attend_back",
    )(queries, *pairs, info, attended, logs, grad)


def is_outer():
    place = lax.axis_index("seq")
    return (place == 0) | (place == 3)


def block_bias(info, bias, index, key_block, query_block, recursion, columns, diagonal):
    block = bias.shape[1]

    def span(which):
        return pl.ds(pl.multiple_of(which * block, block), block)

    same = columns[span(key_block), 0:1] == info[0:1, span(query_block)]
    seen = columns[span(key_block), 1:2] > recursion
    if diagonal:
        key = lax.broadcasted_iota(jnp.int32, (block, block), 0)
        query = lax.broadcasted_iota(jnp.int32, (block, block), 1)
        seen = ((key < query) & seen) | (key == query)
    bias[index] = jnp.where(same & seen, 0.0, -1e30)


def tall_heads(ref, rows, group):
    heads = range(group * GROUP, (group + 1) * GROUP)
    return jnp.concatenate([ref[rows, head_cols(head)] for head in heads], axis=0)


def thrice(bias):
    return jnp.concatenate([bias] * GROUP, axis=1)


def with_ones(value):
    return jnp.concatenate([value.T, jnp.ones((16, value.shape[0]), BF)], axis=0)


def own_kernel(recursion, queries, pair, info, part, columns, bias):
    block = queries.shape[0] // 2
    wide = GROUP * block
    columns[...] = info[...].T
    block_bias(info, bias, 0, 0, 0, recursion, columns, True)
    block_bias(info, bias, 1, 0, 1, recursion, columns, False)
    block_bias(info, bias, 2, 1, 1, recursion, columns, True)
    low, high = slice(0, block), slice(block, 2 * block)
    for group in range(KV_HEADS):
        kc, vc = head_cols(group), head_cols(KV_HEADS + group)
        query_low, query_high = tall_heads(queries, low, group), tall_heads(queries, high, group)
        first = dot(pair[low, kc], query_low, NT) + thrice(bias[0])
        second = dot(pair[low, kc], query_high, NT) + thrice(bias[1])
        third = dot(pair[high, kc], query_high, NT) + thrice(bias[2])
        value_low, value_high = with_ones(pair[low, vc]), with_ones(pair[high, vc])
        top = jnp.max(first, axis=0, keepdims=True)
        mixed = dot(value_low, jnp.exp(first - top).astype(BF))
        part[group, : HEAD_DIM + 8, :wide] = mixed[: HEAD_DIM + 8]
        part[group, HEAD_DIM + 8 :, :wide] = jnp.broadcast_to(top, (8, wide))
        top = jnp.maximum(
            jnp.max(second, axis=0, keepdims=True), jnp.max(third, axis=0, keepdims=True)
        )
        mixed = dot(value_low, jnp.exp(second - top).astype(BF))
        mixed += dot(value_high, jnp.exp(third - top).astype(BF))
        part[group, : HEAD_DIM + 8, wide:] = mixed[: HEAD_DIM + 8]
        part[group, HEAD_DIM + 8 :, wide:] = jnp.broadcast_to(top, (8, wide))


def attend_own(queries, pair, info, recursion):
    tokens = queries.shape[0]
    block = tokens // 2
    return pl.pallas_call(
        functools.partial(own_kernel, recursion),
        out_shape=shape((KV_HEADS, HEAD_DIM + 16, GROUP * tokens), F32),
        in_specs=[vmem] * 3,
        out_specs=vmem,
        scratch_shapes=[
            pltpu.VMEM(info.shape[::-1], F32),
            pltpu.VMEM((3, block, block), F32),
        ],
        compiler_params=params(14),
        name="attend_own",
    )(queries, pair, info)


def rest_rows(block):
    outer = is_outer()
    shift = pl.multiple_of(jnp.where(outer, block, 0), block)
    return outer, pl.ds(shift, block)


def rest_kernel(recursion, queries, pair, info, part, attended, logs, columns, bias):
    block = queries.shape[0] // 2
    wide = GROUP * block
    columns[...] = info[...].T
    outer, rows = rest_rows(block)
    fifth = jnp.where(outer, 1, 0)
    block_bias(info, bias, 0, 2, 1, recursion, columns, False)
    block_bias(info, bias, 1, 2 + fifth, fifth, recursion, columns, False)
    low, high = slice(0, block), slice(block, 2 * block)
    logs[...] = jnp.zeros(logs.shape, F32)
    for group in range(KV_HEADS):
        kc, vc = head_cols(group), head_cols(KV_HEADS + group)
        fourth = dot(pair[low, kc], tall_heads(queries, high, group), NT) + thrice(bias[0])
        fifth = dot(pair[rows, kc], tall_heads(queries, rows, group), NT) + thrice(bias[1])
        own_low, own_high = part[group, :, :wide], part[group, :, wide:]
        top_low, top_high = own_low[HEAD_DIM + 8 : HEAD_DIM + 9], own_high[HEAD_DIM + 8 : HEAD_DIM + 9]
        fifth_top = jnp.max(fifth, axis=0, keepdims=True)
        new_low = jnp.where(outer, top_low, jnp.maximum(top_low, fifth_top))
        new_high = jnp.maximum(top_high, jnp.max(fourth, axis=0, keepdims=True))
        new_high = jnp.where(outer, jnp.maximum(new_high, fifth_top), new_high)
        fourth = jnp.exp(fourth - new_high).astype(BF)
        fifth = jnp.exp(fifth - jnp.where(outer, new_high, new_low)).astype(BF)
        added_high = dot(with_ones(pair[low, vc]), fourth)[: HEAD_DIM + 8]
        added = dot(with_ones(pair[rows, vc]), fifth)[: HEAD_DIM + 8]
        mixed_low = own_low[: HEAD_DIM + 8] * jnp.exp(top_low - new_low)
        mixed_low += jnp.where(outer, 0.0, added)
        mixed_high = own_high[: HEAD_DIM + 8] * jnp.exp(top_high - new_high)
        mixed_high += added_high + jnp.where(outer, added, 0.0)
        for start, mixed, top in ((0, mixed_low, new_low), (block, mixed_high, new_high)):
            total = mixed[HEAD_DIM : HEAD_DIM + 1]
            final = mixed[:HEAD_DIM] * (1.0 / total)
            log_total = top + jnp.log(total)
            for offset in range(GROUP):
                head = group * GROUP + offset
                span = slice(offset * block, (offset + 1) * block)
                attended[start : start + block, head_cols(head)] = final[:, span].T.astype(BF)
                logs[head : head + 1, start : start + block] = log_total[:, span]


def attend_rest(queries, pair, info, part, recursion):
    tokens = queries.shape[0]
    block = tokens // 2
    return pl.pallas_call(
        functools.partial(rest_kernel, recursion),
        out_shape=(shape((tokens, QW), BF), shape((ceil_to(HEADS, 8), tokens), F32)),
        in_specs=[vmem] * 4,
        out_specs=(vmem, vmem),
        scratch_shapes=[
            pltpu.VMEM(info.shape[::-1], F32),
            pltpu.VMEM((2, block, block), F32),
        ],
        compiler_params=params(14),
        name="attend_rest",
    )(queries, pair, info, part)


def flat_row(ref, cols, group):
    heads = range(group * GROUP, (group + 1) * GROUP)
    return jnp.concatenate([ref[head : head + 1, cols] for head in heads], axis=1)


def block_back(key, value, query, grad_mixed, bias, log_total, delta):
    probs = jnp.exp(dot(key, query, NT) + thrice(bias) - log_total)
    grad_scores = (probs * (dot(value, grad_mixed, NT) - delta)).astype(BF)
    grad_value = dot(probs.astype(BF), grad_mixed)
    grad_key = dot(grad_scores, query)
    return dot(key.T, grad_scores), grad_key, grad_value


def rest_back_kernel(
    recursion, queries, pair, info, attended, logs, grad, grad_pair, part, deltas, columns, bias
):
    block = queries.shape[0] // 2
    wide = GROUP * block
    columns[...] = info[...].T
    outer, rows = rest_rows(block)
    fifth = jnp.where(outer, 1, 0)
    block_bias(info, bias, 0, 2, 1, recursion, columns, False)
    block_bias(info, bias, 1, 2 + fifth, fifth, recursion, columns, False)
    low, high = slice(0, block), slice(block, 2 * block)
    product = (attended[...].astype(F32) * grad[...].astype(F32)).T
    deltas[...] = jnp.zeros(deltas.shape, F32)
    for head in range(HEADS):
        deltas[head : head + 1, :] = jnp.sum(product[head_cols(head)], axis=0, keepdims=True)
    for group in range(KV_HEADS):
        kc, vc = head_cols(group), head_cols(KV_HEADS + group)
        query_high, key_high, value_high = block_back(
            pair[low, kc], pair[low, vc], tall_heads(queries, high, group),
            tall_heads(grad, high, group), bias[0], flat_row(logs, high, group),
            flat_row(deltas, high, group),
        )
        query, key, value = block_back(
            pair[rows, kc], pair[rows, vc], tall_heads(queries, rows, group),
            tall_heads(grad, rows, group), bias[1], flat_row(logs, rows, group),
            flat_row(deltas, rows, group),
        )
        part[group, :, :wide] = jnp.where(outer, 0.0, query)
        part[group, :, wide:] = query_high + jnp.where(outer, query, 0.0)
        grad_pair[low, kc] = (key_high + jnp.where(outer, 0.0, key)).astype(BF)
        grad_pair[low, vc] = (value_high + jnp.where(outer, 0.0, value)).astype(BF)
        grad_pair[high, kc] = jnp.where(outer, key, 0.0).astype(BF)
        grad_pair[high, vc] = jnp.where(outer, value, 0.0).astype(BF)


def attend_rest_back(queries, pair, info, attended, logs, grad, recursion):
    tokens = queries.shape[0]
    block = tokens // 2
    return pl.pallas_call(
        functools.partial(rest_back_kernel, recursion),
        out_shape=(
            shape((tokens, 2 * KW), BF),
            shape((KV_HEADS, HEAD_DIM, GROUP * tokens), F32),
            shape(logs.shape, F32),
        ),
        in_specs=[vmem] * 6,
        out_specs=(vmem,) * 3,
        scratch_shapes=[
            pltpu.VMEM(info.shape[::-1], F32),
            pltpu.VMEM((2, block, block), F32),
        ],
        compiler_params=params(18),
        name="attend_rest_back",
    )(queries, pair, info, attended, logs, grad)


def own_back_kernel(
    recursion, queries, pair, info, logs, deltas, grad, part, grad_queries, grad_pair, columns, bias
):
    block = queries.shape[0] // 2
    wide = GROUP * block
    columns[...] = info[...].T
    block_bias(info, bias, 0, 0, 0, recursion, columns, True)
    block_bias(info, bias, 1, 0, 1, recursion, columns, False)
    block_bias(info, bias, 2, 1, 1, recursion, columns, True)
    low, high = slice(0, block), slice(block, 2 * block)
    for group in range(KV_HEADS):
        kc, vc = head_cols(group), head_cols(KV_HEADS + group)
        made = []
        for index, keys, side in ((0, low, low), (1, low, high), (2, high, high)):
            made.append(
                block_back(
                    pair[keys, kc], pair[keys, vc], tall_heads(queries, side, group),
                    tall_heads(grad, side, group), bias[index], flat_row(logs, side, group),
                    flat_row(deltas, side, group),
                )
            )
        first, second, third = made
        grad_pair[low, kc] = first[1] + second[1]
        grad_pair[low, vc] = first[2] + second[2]
        grad_pair[high, kc] = third[1]
        grad_pair[high, vc] = third[2]
        query_low = (part[group, :, :wide] + first[0]) * HEAD_DIM**-0.5
        query_high = (part[group, :, wide:] + second[0] + third[0]) * HEAD_DIM**-0.5
        for start, made_query in ((0, query_low), (block, query_high)):
            for offset in range(GROUP):
                head = group * GROUP + offset
                span = slice(offset * block, (offset + 1) * block)
                grad_queries[start : start + block, head_cols(head)] = made_query[:, span].T


def attend_own_back(queries, pair, info, logs, deltas, grad, part, recursion):
    tokens = queries.shape[0]
    block = tokens // 2
    return pl.pallas_call(
        functools.partial(own_back_kernel, recursion),
        out_shape=(shape((tokens, QW), F32), shape((tokens, 2 * KW), F32)),
        in_specs=[vmem] * 7,
        out_specs=(vmem,) * 2,
        scratch_shapes=[
            pltpu.VMEM(info.shape[::-1], F32),
            pltpu.VMEM((3, block, block), F32),
        ],
        compiler_params=params(18),
        name="attend_own_back",
    )(queries, pair, info, logs, deltas, grad, part)


def post_kernel(
    used, cols, state, attended, attn_w, gain, router, active, gate_w, up_w, down_w,
    state_out, normed_out, gate_out, up_out, hidden_out, midway_out, update_out, routed,
    normed, midway, update, branch, total, stage, sems,
):
    pieces, _, part = gate_w.shape
    wide = down_w.shape[2]
    low_col = used // LANE * LANE

    def ship(index, source, target):
        return pltpu.make_async_copy(source, target, sems.at[index])

    def ship_piece(piece):
        spot = lax.rem(piece, 2)
        return [
            ship(3 + 3 * spot + index, stage.at[spot, index], out.at[piece])
            for index, out in enumerate((gate_out, up_out, hidden_out))
        ]

    for piece in range(pieces):
        made = dot(attended[...], attn_w[piece, :, low_col:])
        branch[:, piece * cols : (piece + 1) * cols] = made[:, used - low_col :]
    between = state[...] + branch[...]
    midway[...] = between
    ship(0, midway, midway_out).start()
    inverse = lax.rsqrt(jnp.mean(between * between, axis=-1, keepdims=True) + epsilon)
    normed[...] = (between * inverse * gain[...]).astype(BF)
    ship(1, normed, normed_out).start()
    chance = 1.0 / (1.0 + jnp.exp(-jnp.sum(state[...] * router[...], axis=-1, keepdims=True)))
    routed[...] = jnp.broadcast_to(chance, routed.shape)
    total[...] = jnp.zeros(total.shape, F32)

    def step(piece, carry):
        spot = lax.rem(piece, 2)

        @pl.when(piece >= 2)
        def _():
            for copy in ship_piece(piece - 2):
                copy.wait()

        rows = pl.ds(pl.multiple_of(piece * part, part), part)
        half = normed.shape[0] // 2
        for span in (slice(0, half), slice(half, 2 * half)):
            pre = dot(normed[span], jnp.concatenate([gate_w[piece], up_w[piece]], axis=1))
            gate, up = pre[:, :part], pre[:, part:]
            hidden = (gate / (1.0 + jnp.exp(-gate)) * up).astype(BF)
            for index, made in enumerate((gate.astype(BF), up.astype(BF), hidden)):
                stage[spot, index, span] = made
            total[span] += dot(hidden, side_by_side(down_w, rows))
        for copy in ship_piece(piece):
            copy.start()
        return carry

    lax.fori_loop(0, pieces, step, 0)
    for piece in range(pieces):
        span = slice(piece * cols, (piece + 1) * cols)
        branch[:, span] = branch[:, span] + total[:, piece * wide : piece * wide + cols]
    changed = branch[...]
    update[...] = changed.astype(BF)
    ship(2, update, update_out).start()
    state_out[...] = state[...] + (active[:, 0:1] * routed[:, 0:1]) * changed
    for index, (source, target) in enumerate(
        ((midway, midway_out), (normed, normed_out), (update, update_out))
    ):
        ship(index, source, target).wait()
    for piece in range(max(0, pieces - 2), pieces):
        for copy in ship_piece(piece):
            copy.wait()


anywhere = pl.BlockSpec(memory_space=pl.ANY)


def post_part(state, attended, attn_w, gain, router, active, gate_w, up_w, down_w, used):
    tokens, width = state.shape
    pieces, _, part = gate_w.shape
    made = pl.pallas_call(
        functools.partial(post_kernel, used, width // pieces),
        out_shape=(
            shape((tokens, width), F32),
            shape((tokens, width), BF),
            shape((pieces, tokens, part), BF),
            shape((pieces, tokens, part), BF),
            shape((pieces, tokens, part), BF),
            shape((tokens, width), F32),
            shape((tokens, width), BF),
            shape((tokens, LANE), F32),
        ),
        in_specs=[vmem] * 9,
        out_specs=(vmem,) + (anywhere,) * 6 + (vmem,),
        scratch_shapes=[
            pltpu.VMEM((tokens, width), BF),
            pltpu.VMEM((tokens, width), F32),
            pltpu.VMEM((tokens, width), BF),
            pltpu.VMEM((tokens, width), F32),
            pltpu.VMEM((tokens, pieces * down_w.shape[2]), F32),
            pltpu.VMEM((2, 3, tokens, part), BF),
            pltpu.SemaphoreType.DMA((9,)),
        ],
        compiler_params=params(wide_limit(gate_w, 22)),
        name="post",
    )(state, attended, placed(attn_w), gain, router, active, placed(gate_w), placed(up_w),
      placed(down_w))
    names = ("state_out", "ffn_in", "gate", "up", "hidden", "midway", "update", "routed")
    return dict(zip(names, made))


def post_back_kernel(
    used, cols, grad_state, update, routed, active, state, midway, gain, router, attn_w,
    gate_w, up_w, down_w, gate_pre, up_pre,
    grad_attended, partial, gain_grad, router_grad, ffn_out, gate_out, up_out, branch_out,
    scaled, total, grad_ffn, grad_branch, fetched, stage, load, sems,
):
    pieces, _, part = gate_w.shape
    low_col = used // LANE * LANE

    def ship(index, source, target):
        return pltpu.make_async_copy(source, target, sems.at[index])

    def ship_piece(piece):
        spot = lax.rem(piece, 2)
        return [
            ship(2 + 2 * spot + index, stage.at[spot, index], out.at[piece])
            for index, out in enumerate((gate_out, up_out))
        ]

    def fetch(piece):
        spot = lax.rem(piece, 2)
        return [
            pltpu.make_async_copy(ref.at[piece], fetched.at[spot, index], load.at[spot, index])
            for index, ref in enumerate((gate_pre, up_pre))
        ]

    for copy in fetch(0):
        copy.start()
    chance = routed[:, 0:1]
    weight = active[:, 0:1] * chance
    grad = grad_state[...]
    change = grad * weight
    scaled[...] = change
    slope = jnp.sum(grad * update[...].astype(F32), axis=-1, keepdims=True) * weight * (1.0 - chance)
    router_grad[...] = jnp.sum(state[...] * slope, axis=0, keepdims=True)
    partial[...] = grad + slope * router[...]
    low = change.astype(BF)
    for piece in range(pieces):
        grad_ffn[piece] = jnp.zeros(grad_ffn.shape[1:], BF)
        grad_ffn[piece, :, :cols] = low[:, piece * cols : (piece + 1) * cols]
    ship(0, grad_ffn, ffn_out).start()
    total[...] = jnp.zeros(total.shape, F32)

    def step(piece, carry):
        spot = lax.rem(piece, 2)

        @pl.when(piece + 1 < pieces)
        def _():
            for copy in fetch(piece + 1):
                copy.start()

        @pl.when(piece >= 2)
        def _():
            for copy in ship_piece(piece - 2):
                copy.wait()

        for copy in fetch(piece):
            copy.wait()
        rows = pl.ds(pl.multiple_of(piece * part, part), part)
        grad_hidden = dot(side_by_side(grad_ffn), side_by_side(down_w, rows), NT)
        gate = fetched[spot, 0].astype(F32)
        chance = 1.0 / (1.0 + jnp.exp(-gate))
        smooth = gate * chance
        slope = chance + smooth * (1.0 - chance)
        grad_gate = (grad_hidden * fetched[spot, 1].astype(F32) * slope).astype(BF)
        grad_up = (grad_hidden * smooth).astype(BF)
        stage[spot, 0] = grad_gate
        stage[spot, 1] = grad_up
        total[...] += dot(
            jnp.concatenate([grad_gate, grad_up], axis=1),
            jnp.concatenate([gate_w[piece], up_w[piece]], axis=1),
            NT,
        )
        for copy in ship_piece(piece):
            copy.start()
        return carry

    lax.fori_loop(0, pieces, step, 0)
    grad_midway, grad_gain = norm_back(total[...], midway[...], gain[...])
    gain_grad[...] = grad_gain
    partial[...] = partial[...] + grad_midway
    low = (scaled[...] + grad_midway).astype(BF)
    shift = used - low_col
    for piece in range(pieces):
        if grad_branch.shape[2] > cols:
            grad_branch[piece] = jnp.zeros(grad_branch.shape[1:], BF)
        grad_branch[piece, :, shift : shift + cols] = low[:, piece * cols : (piece + 1) * cols]
    ship(1, grad_branch, branch_out).start()
    grad = None
    for piece in range(pieces):
        made = dot(grad_branch[piece], attn_w[piece, :, low_col:], NT)
        grad = made if grad is None else grad + made
    grad_attended[...] = grad.astype(BF)
    ship(0, grad_ffn, ffn_out).wait()
    ship(1, grad_branch, branch_out).wait()
    for piece in range(max(0, pieces - 2), pieces):
        for copy in ship_piece(piece):
            copy.wait()


def post_back(grad_state, s, gain, router, attn_w, gate_w, up_w, down_w, used):
    state = s["state"]
    tokens, width = state.shape
    pieces, _, part = gate_w.shape
    branch_dims = (pieces, tokens, attn_w.shape[2] - used // LANE * LANE)
    ffn_dims = (pieces, tokens, down_w.shape[2])
    made = pl.pallas_call(
        functools.partial(post_back_kernel, used, width // pieces),
        out_shape=(
            shape((tokens, QW), BF),
            shape((tokens, width), F32),
            shape((1, width), F32),
            shape((1, width), F32),
            shape(ffn_dims, BF),
            shape((pieces, tokens, part), BF),
            shape((pieces, tokens, part), BF),
            shape(branch_dims, BF),
        ),
        in_specs=[vmem] * 12 + [anywhere] * 2,
        out_specs=(vmem,) * 4 + (anywhere,) * 4,
        scratch_shapes=[
            pltpu.VMEM((tokens, width), F32),
            pltpu.VMEM((tokens, width), F32),
            pltpu.VMEM(ffn_dims, BF),
            pltpu.VMEM(branch_dims, BF),
            pltpu.VMEM((2, 2, tokens, part), BF),
            pltpu.VMEM((2, 2, tokens, part), BF),
            pltpu.SemaphoreType.DMA((2, 2)),
            pltpu.SemaphoreType.DMA((6,)),
        ],
        compiler_params=params(wide_limit(gate_w, 26)),
        name="post_back",
    )(grad_state, s["update"], s["routed"], s["active"], state, s["midway"], gain, router,
      placed(attn_w), placed(gate_w), placed(up_w), placed(down_w), s["gate"], s["up"])
    names = (
        "grad_attended", "partial", "ffn_gain_grad", "router_grad", "grad_ffn", "grad_gate", "grad_up",
        "grad_branch",
    )
    return dict(zip(names, made))


def pre_back_kernel(cols, blocks, *refs):
    qc, kc = cols
    grad_queries, own, others = refs[0], refs[1], refs[2 : 1 + blocks]
    partial, state, gain, weight, cosine, sine = refs[1 + blocks : 7 + blocks]
    packed, grad_state, gain_grad, qbuf, kbuf = refs[7 + blocks :]
    summed = own[...]
    for ref in others:
        summed = summed + ref[...].astype(F32)
    kbuf[:, :KW] = summed[:, :KW]
    qbuf[:, :QW] = grad_queries[...]
    for buf in (qbuf, kbuf):
        for start in range(0, buf.shape[1], LANE):
            span = slice(start, start + LANE)
            buf[:, span] = turn(buf[:, span], cosine[...], -sine[...])
    low_q = qbuf[...].astype(BF)
    low_k = kbuf[...].astype(BF)
    low_v = summed[:, KW:].astype(BF)
    total = None
    used = packed.shape[2]
    for piece in range(weight.shape[0]):
        packed[piece] = jnp.zeros(packed.shape[1:], BF)
        packed[piece, :, :qc] = low_q[:, piece * qc : (piece + 1) * qc]
        packed[piece, :, qc : qc + kc] = low_k[:, piece * kc : (piece + 1) * kc]
        packed[piece, :, qc + kc : qc + 2 * kc] = low_v[:, piece * kc : (piece + 1) * kc]
        made = dot(packed[piece], weight[piece, :, :used], NT)
        total = made if total is None else total + made
    grad_in, grad_gain = norm_back(total, state[...], gain[...])
    gain_grad[...] = grad_gain
    grad_state[...] = partial[...] + grad_in


def pre_back(grad_queries, grad_pairs, partial, state, gain, weight, cosine, sine, cols):
    tokens, width = state.shape
    used = min(ceil_to(cols[0] + 2 * cols[1], LANE), weight.shape[2])
    return pl.pallas_call(
        functools.partial(pre_back_kernel, cols, len(grad_pairs)),
        out_shape=(
            shape((weight.shape[0], tokens, used), BF),
            shape((tokens, width), F32),
            shape((1, width), F32),
        ),
        in_specs=[vmem] * (7 + len(grad_pairs)),
        out_specs=(vmem,) * 3,
        scratch_shapes=[
            pltpu.VMEM((tokens, ceil_to(QW, LANE)), F32),
            pltpu.VMEM((tokens, ceil_to(KW, LANE)), F32),
        ],
        compiler_params=params(wide_limit(weight, 16)),
        name="pre_back",
    )(grad_queries, *grad_pairs, partial, state, gain, placed(weight), cosine, sine)


def attn_sums_kernel(count, low_col, *refs):
    normed, packed = refs[:count], refs[count : 2 * count]
    attended, branch = refs[2 * count : 3 * count], refs[3 * count : 4 * count]
    out, left, right = refs[4 * count :]

    @pl.when(pl.program_id(0) == 0)
    def _():
        left[...] = jnp.concatenate([ref[...].T for ref in normed], axis=1)
        right[...] = jnp.concatenate([ref[...].T for ref in attended], axis=1)

    first = dot(left[...], jnp.concatenate([ref[0] for ref in packed], axis=0))
    second = dot(right[...], jnp.concatenate([ref[0] for ref in branch], axis=0))
    high_col = first.shape[1]
    if low_col:
        out[0, :, :low_col] = first[:, :low_col].astype(BF)
    out[0, :, low_col:high_col] = (first[:, low_col:] + second[:, : high_col - low_col]).astype(BF)
    if high_col < out.shape[2]:
        out[0, :, high_col:] = second[:, high_col - low_col :].astype(BF)


def attn_sums(normed, packed, attended, branch, low_col, total_cols):
    count = len(normed)
    tokens, width = normed[0].shape
    pieces = packed[0].shape[0]
    row = pl.BlockSpec((tokens, width), lambda s: (0, 0))
    part = pl.BlockSpec((1, tokens, packed[0].shape[2]), lambda s: (s, 0, 0))
    thin = pl.BlockSpec((1, tokens, branch[0].shape[2]), lambda s: (s, 0, 0))
    return pl.pallas_call(
        functools.partial(attn_sums_kernel, count, low_col),
        grid=(pieces,),
        out_shape=shape((pieces, width, total_cols), BF),
        in_specs=[row] * count + [part] * count + [row] * count + [thin] * count,
        out_specs=pl.BlockSpec((1, width, total_cols), lambda s: (s, 0, 0)),
        scratch_shapes=[pltpu.VMEM((width, count * tokens), BF)] * 2,
        compiler_params=params(56),
        name="attn_sums",
    )(*normed, *packed, *attended, *branch)


def pair_sums_kernel(count, *refs):
    normed, first, second = refs[:count], refs[count : 2 * count], refs[2 * count : 3 * count]
    first_out, second_out, left = refs[3 * count :]

    @pl.when(pl.program_id(0) == 0)
    def _():
        left[...] = jnp.concatenate([ref[...].T for ref in normed], axis=1)

    for source, out in ((first, first_out), (second, second_out)):
        out[0] = dot(left[...], jnp.concatenate([ref[0] for ref in source], axis=0)).astype(BF)


def pair_sums(normed, first, second):
    count = len(normed)
    tokens, width = normed[0].shape
    pieces, _, part = first[0].shape
    row = pl.BlockSpec((tokens, width), lambda s: (0, 0))
    chunk = pl.BlockSpec((1, tokens, part), lambda s: (s, 0, 0))
    result = pl.BlockSpec((1, width, part), lambda s: (s, 0, 0))
    return pl.pallas_call(
        functools.partial(pair_sums_kernel, count),
        grid=(pieces,),
        out_shape=(shape((pieces, width, part), BF),) * 2,
        in_specs=[row] * count + [chunk] * (2 * count),
        out_specs=(result, result),
        scratch_shapes=[pltpu.VMEM((width, count * tokens), BF)],
        compiler_params=params(56),
        name="pair_sums",
    )(*normed, *first, *second)


def down_sums_kernel(count, *refs):
    hidden, grads, out, right = refs[:count], refs[count : 2 * count], refs[-2], refs[-1]

    @pl.when(pl.program_id(0) == 0)
    def _():
        for piece in range(out.shape[0]):
            right[piece] = jnp.concatenate([ref[piece] for ref in grads], axis=0)

    left = jnp.concatenate([ref[0].T for ref in hidden], axis=1)
    for piece in range(out.shape[0]):
        out[piece] = dot(left, right[piece]).astype(BF)


def down_sums(hidden, grads):
    count = len(hidden)
    pieces, tokens, part = hidden[0].shape
    cols = grads[0].shape[2]
    return pl.pallas_call(
        functools.partial(down_sums_kernel, count),
        grid=(pieces,),
        out_shape=shape((pieces, pieces * part, cols), BF),
        in_specs=[pl.BlockSpec((1, tokens, part), lambda f: (f, 0, 0))] * count
        + [pl.BlockSpec((pieces, tokens, cols), lambda f: (0, 0, 0))] * count,
        out_specs=pl.BlockSpec((pieces, part, cols), lambda f: (0, f, 0)),
        scratch_shapes=[pltpu.VMEM((pieces, count * tokens, cols), BF)],
        compiler_params=params(56),
        name="down_sums",
    )(*hidden, *grads)


MESH = pl.DeviceIdType.MESH


class Place:
    def __init__(self, layers):
        dp, seq = lax.axis_index("dp"), lax.axis_index("seq")
        self.layers = layers
        self.z, self.core = lax.div(dp, 2), lax.rem(dp, 2)
        self.y, self.x = lax.div(seq, 2), lax.rem(seq, 2)
        self.sibling = (self.z * 2 + 1 - self.core, seq)
        self.over_x = (dp, self.y * 2 + 1 - self.x)
        self.over_y = (dp, (1 - self.y) * 2 + self.x)
        self.up = [(lax.rem(self.z + k, layers) * 2 + self.core, seq) for k in range(layers)]
        self.down = [
            (lax.rem(self.z + layers - k, layers) * 2 + self.core, seq) for k in range(layers)
        ]
        self.across = (dp, 3 - seq)
        self.partner = (dp, jnp.where(self.core == 0, self.over_x[1], self.over_y[1]))
        self.place_peers = [self.over_x, self.over_y, self.across]
        self.rank_peers = self.up[1:] + [
            (lax.rem(self.z + k, layers) * 2 + 1 - self.core, seq) for k in range(layers)
        ]
        self.peers = self.place_peers + self.rank_peers

    def greet(self):
        barrier = pltpu.get_barrier_semaphore()
        for peer in self.peers:
            pl.semaphore_signal(barrier, inc=1, device_id=peer, device_id_type=MESH)
        pl.semaphore_wait(barrier, len(self.peers))


def remote(source, target, sems, peer):
    return pltpu.make_async_remote_copy(
        src_ref=source, dst_ref=target, send_sem=sems[0], recv_sem=sems[1],
        device_id=peer, device_id_type=MESH,
    )


class Pieces:
    def __init__(self, ref):
        self.ref = ref
        self.shape = (4, ref.shape[2] * ref.shape[3] * ref.shape[4], ref.shape[5])

    def __getitem__(self, index):
        piece, _, lanes = index
        whole = self.ref[piece // 2, piece % 2, :, :, :, lanes]
        return whole.reshape(self.shape[1], whole.shape[-1])


def open_kernel(layers, micros, cols, *refs):
    refs = list(refs)

    def pop(size):
        taken = refs[:size]
        del refs[:size]
        return taken

    count = 4
    ins = pop(count)
    small, own_state, other_state, cosine, sine = pop(5)
    outs = pop(count)
    gains, active = pop(2 + RECUR), pop(RECUR)
    info, state, normed, queries, pair, partner, attended, logs = pop(8)
    ranks_in, places_in, state_in, part, qbuf, kbuf, columns, own_bias, rest_bias = pop(9)
    send, recv, keep, side_send, side_recv = refs
    here = Place(layers)
    here.greet()
    y, x, z, core = here.y, here.x, here.z, here.core
    rank, place = z * 2 + core, y * 2 + x
    sent = []

    def slot(a, index):
        return send.at[a, index], recv.at[a, index]

    def start(a, index, source, target, peer):
        copy = remote(source, target, slot(a, index), peer)
        copy.start()
        sent.append(copy)

    def arrive(a, index, landing):
        remote(landing, landing, slot(a, index), here.sibling).wait_recv()

    def aside(index, source, target, peer):
        copy = remote(source, target, (side_send.at[index], side_recv.at[index]), peer)
        copy.start()
        sent.append(copy)

    def arrive_aside(index, landing):
        remote(
            landing, landing, (side_send.at[index], side_recv.at[index]), here.sibling
        ).wait_recv()

    def layer(k):
        return lax.rem(z + layers - k, layers)

    def sides(a):
        if a % 2 == 0:
            return here.over_x, here.over_y, (y, 1 - x), ((1 - y, x), (1 - y, 1 - x))
        return here.over_y, here.over_x, (1 - y, x), ((y, 1 - x), (1 - y, 1 - x))

    own = [pltpu.make_async_copy(ins[a], outs[a].at[y, x, z, core], keep.at[a]) for a in range(count)]
    for copy in own:
        copy.start()

    for index, peer in enumerate(here.rank_peers):
        aside(index, small.at[pl.ds(0, 8)], ranks_in.at[rank], peer)
    first_place = len(here.rank_peers)
    for index, peer in enumerate(here.place_peers):
        aside(first_place + index, small.at[pl.ds(8, 8)], places_in.at[place], peer)
    last = first_place + len(here.place_peers)
    ranks_in[rank] = small[0:8]
    places_in[place] = small[8:16]

    def along(arrays, k):
        for a in arrays:
            start(a, k, ins[a], outs[a].at[y, x, z, core], here.up[k])

    def first(arrays, k):
        for a in arrays:
            spot = outs[a].at[y, x, layer(k), core]
            source = ins[a] if k == 0 else spot
            if k:
                arrive(a, k, spot)
            start(a, layers + k, source, spot, sides(a + k)[0])
            start(a, 2 * layers + k, source, spot, sides(a + k)[1])

    def second(arrays, k):
        for a in arrays:
            side = sides(a + k)[2]
            spot = outs[a].at[side[0], side[1], layer(k), core]
            arrive(a, layers + k, spot)
            start(a, 3 * layers + k, spot, spot, sides(a + k)[1])

    def third(arrays, k):
        for a in arrays:
            for turn_of, side in enumerate(sides(a + k)[3]):
                arrive(a, (2 + turn_of) * layers + k, outs[a].at[side[0], side[1], layer(k), core])
            if k == 0:
                own[a].wait()
            spot = outs[a].at[:, :, layer(k), core]
            start(a, 4 * layers + k, spot, spot, here.sibling)

    def complete(arrays):
        for k in range(layers):
            for a in arrays:
                arrive(a, 4 * layers + k, outs[a].at[:, :, layer(k), 1 - core])

    works = dict(f=first, s=second, t=third)

    def compute(word):
        if word == "marks":
            unpack_marks()
        elif word == "pre":
            complete((0,))
            pre_kernel(
                cols, state, gains[0], Pieces(outs[0]), cosine, sine, normed, queries,
                pair, qbuf, kbuf,
            )
            aside(last + 1, pair, partner, here.partner)
        elif word == "own":
            own_kernel(0, queries, pair, info, part, columns, own_bias)
        else:
            arrive_aside(last + 1, partner)
            rest_kernel(0, queries, partner, info, part, attended, logs, columns, rest_bias)

    def unpack_marks():
        second_pack = jnp.where(core == 0, y == 1, x == 1)
        outer = is_outer()
        rows, block = gains[0].shape[1] // (2 * layers), state.shape[0] // 2
        for index in range(len(here.rank_peers)):
            arrive_aside(index, ranks_in.at[rank])
        for index in range(len(here.place_peers)):
            arrive_aside(first_place + index, places_in.at[place])
        for index in range(2 * layers):
            for row, ref in enumerate(gains):
                ref[:, index * rows : (index + 1) * rows] = ranks_in[index][row : row + 1, :rows]
        info[...] = jnp.zeros(info.shape, F32)
        for index, (one, two) in enumerate(zip((0, 3, 1, 2), (1, 2, 0, 3))):
            marks = places_in[jnp.where(outer, one, two)][:, :block]
            for row in range(2):
                info[row : row + 1, index * block : (index + 1) * block] = jnp.where(
                    second_pack, marks[row * micros + 1 : row * micros + 2], marks[row * micros : row * micros + 1]
                )
        columns[...] = info[...].T
        for r in range(RECUR):
            active[r][...] = jnp.broadcast_to(
                jnp.where(columns[0 : 2 * block, 1:2] > r, 1.0, 0.0), (2 * block, LANE)
            )
        arrive_aside(last, state_in)
        high = y == 1
        state[pl.ds(pl.multiple_of(jnp.where(high, block, 0), block), block)] = own_state[...]
        state[pl.ds(pl.multiple_of(jnp.where(high, 0, block), block), block)] = state_in[...].astype(F32)

    for word in PLAN:
        if len(word) > 2:
            compute(word)
            continue
        arrays = (0,) if word[0].isupper() else (1, 2, 3)
        kind = word[0].lower()
        if kind == "z":
            for k in range(1, layers) if len(word) == 1 else (int(word[1]),):
                along(arrays, k)
        elif kind == "x":
            aside(last, other_state, state_in, here.across)
        else:
            works[kind](arrays, int(word[1]))
    complete((1, 2, 3))
    for copy in sent:
        copy.wait_send()


PLAN = (
    "Z", "F0", "x", "F1", "S0", "F2", "S1", "F3", "f0", "z", "S2", "T0", "marks", "S3", "T1", "f1",
    "T2", "s0", "T3", "pre", "f2", "s1", "t0", "own", "f3", "s2", "t1", "rest", "s3", "t2", "t3",
)


def open_all(parts, small, own_state, other_state, tables, micros, cols):
    count, tokens, width = len(parts), 2 * own_state.shape[0], own_state.shape[1]
    ranks = lax.axis_size("dp")
    layers, seq = ranks // 2, 4
    wide = ceil_to(KW, LANE)
    made = pl.pallas_call(
        functools.partial(open_kernel, layers, micros, cols),
        out_shape=tuple(pltpu.VMEM((2, 2, layers, 2) + part.shape, part.dtype) for part in parts)
        + (
            *[shape((1, width), F32)] * (2 + RECUR),
            *[shape((tokens, LANE), F32)] * RECUR,
            shape((8, 2 * tokens), F32),
            shape((tokens, width), F32),
            shape((tokens, width), BF),
            shape((tokens, QW), BF),
            shape((tokens, 2 * KW), BF),
            shape((tokens, 2 * KW), BF),
            shape((tokens, QW), BF),
            shape((ceil_to(HEADS, 8), tokens), F32),
        ),
        in_specs=[vmem] + [anywhere] * (count - 1) + [vmem] * 5,
        out_specs=(vmem,) + (anywhere,) * (count - 1) + (vmem,) * (10 + 2 * RECUR),
        scratch_shapes=[
            pltpu.VMEM((ranks, 8) + small.shape[1:], F32),
            pltpu.VMEM((seq, 8) + small.shape[1:], F32),
            pltpu.VMEM(other_state.shape, BF),
            pltpu.VMEM((KV_HEADS, HEAD_DIM + 16, GROUP * tokens), F32),
            pltpu.VMEM((tokens, ceil_to(QW, LANE)), F32),
            pltpu.VMEM((tokens, wide), F32),
            pltpu.VMEM((2 * tokens, 8), F32),
            pltpu.VMEM((3, tokens // 2, tokens // 2), F32),
            pltpu.VMEM((2, tokens // 2, tokens // 2), F32),
            pltpu.SemaphoreType.DMA((count, 5 * layers)),
            pltpu.SemaphoreType.DMA((count, 5 * layers)),
            pltpu.SemaphoreType.DMA((count,)),
            pltpu.SemaphoreType.DMA((ranks + seq,)),
            pltpu.SemaphoreType.DMA((ranks + seq,)),
        ],
        compiler_params=pltpu.CompilerParams(
            collective_id=0, has_side_effects=True, vmem_limit_bytes=OPEN_LIMIT * MIB
        ),
        name="open_all",
    )(*parts, small, own_state, other_state, *tables)
    gathered, gains, actives = made[:count], made[count : count + 2 + RECUR], made[count + 2 + RECUR :]
    names = ("info", "state", "normed", "queries", "pair", "partner", "attended", "logs")
    return gathered, gains, actives[:RECUR], dict(zip(names, actives[RECUR:]))


OPEN_LIMIT = 32


SECOND_AT, THIRD_AT = 2, 2


def finish_kernel(layers, count, low_col, *refs):
    refs = list(refs)

    def pop(size):
        taken = refs[:size]
        del refs[:size]
        return taken

    normed, packed, attended, branch, ffn_in, grad_gate, grad_up, hidden, grad_ffn = (
        pop(count) for _ in range(9)
    )
    (small,) = pop(1)
    outs = pop(4)
    held, core_in, first_in, second_in, z_in = (pop(4) for _ in range(5))
    raw, left, right, ffn_right, stage, down_stage = pop(6)
    send, recv, load = refs
    here = Place(layers)
    here.greet()
    y, x, z, core = here.y, here.x, here.z, here.core
    tokens = raw.shape[0] // count

    def slot(a, index):
        return send.at[a, index], recv.at[a, index]

    def arrive(a, index, landing):
        remote(landing, landing, slot(a, index), here.sibling).wait_recv()

    def layer(k):
        return lax.rem(z + k + 1, layers)

    def added(ref, one, two):
        return (one.astype(F32) + two.astype(F32)).astype(ref.dtype)

    def load_left(index, sources):
        return [
            pltpu.make_async_copy(ref, raw.at[pl.ds(i * tokens, tokens)], load.at[index, i])
            for i, ref in enumerate(sources)
        ]

    def load_right(index, spot, sources, piece, start_col):
        width = sources[0].shape[2]
        return [
            pltpu.make_async_copy(
                ref.at[piece],
                right.at[spot, pl.ds(i * tokens, tokens), pl.ds(start_col, width)],
                load.at[index + spot, i],
            )
            for i, ref in enumerate(sources)
        ]

    def go(copies):
        for copy in copies:
            copy.start()

    def hold(copies):
        for copy in copies:
            copy.wait()

    def turn_left(spot):
        for i in range(count):
            rows = slice(i * tokens, (i + 1) * tokens)
            left[spot, :, rows] = raw[rows].T

    def column_of(piece):
        return lax.rem(1 - y + lax.div(piece, 2), 2), lax.rem(1 - x + lax.rem(piece, 2), 2)

    def spot_of(a, piece):
        if a == 3:
            return (lax.rem(z + piece + 1, layers),)
        return (slice(None),) + column_of(piece)

    def number_of(a, piece):
        if a == 3:
            return lax.rem(z + piece + 1, layers)
        row, column = column_of(piece)
        return row * 2 + column

    def staged(a, spot, whose):
        lead = (spot, slice(None), slice(None)) if a == 3 else (spot, slice(None))
        return (down_stage if a == 3 else stage), lead + (whose,)

    def handed(a, piece):
        ref, place = staged(a, lax.rem(piece, 2), 1 - core)
        return remote(
            ref.at[place], core_in[a].at[spot_of(a, piece)], (send.at[a, piece], recv.at[a, piece]),
            here.sibling,
        )

    def add_cores(a, piece):
        spot = spot_of(a, piece)
        arrive(a, piece, core_in[a].at[spot])
        ref, place = staged(a, lax.rem(piece, 2), core)
        held[a][spot] = added(held[a], ref[place], core_in[a][spot])

    def products(a, fetch, multiply, hooks):
        go(fetch(number_of(a, 0), 0))

        def step(piece, carry):
            spot = lax.rem(piece, 2)
            hold(fetch(number_of(a, piece), spot))

            @pl.when(piece < 3)
            def _():
                go(fetch(number_of(a, piece + 1), 1 - spot))

            @pl.when(piece >= 2)
            def _():
                handed(a, piece - 2).wait_send()

            multiply(number_of(a, piece), spot)
            handed(a, piece).start()

            @pl.when(piece >= 1)
            def _():
                add_cores(a, piece - 1)

            for at, hook in hooks:
                pl.when(piece == at)(hook)
            return carry

        lax.fori_loop(0, 4, step, 0)
        add_cores(a, 3)
        for piece in (2, 3):
            handed(a, piece).wait_send()

    def store(spot, result):
        rows = stage.shape[3]
        for index in range(2 * layers):
            stage[spot, index // 2, index % 2] = result[index * rows : (index + 1) * rows].astype(BF)

    def ffn_product(which):
        def multiply(piece, spot):
            width = which[0].shape[2]
            store(spot, dot(left[0], right[spot, :, :width]))

        return multiply

    high_col = packed[0].shape[2]
    far_col = branch[0].shape[2]

    def attn_product(piece, spot):
        first = dot(left[1], right[spot, :, :high_col])
        second = dot(left[0], right[spot, :, high_col : high_col + far_col])
        cut = high_col - low_col
        store(
            spot,
            jnp.concatenate(
                [first[:, :low_col], first[:, low_col:] + second[:, :cut], second[:, cut:]], axis=1
            ),
        )

    def down_product(piece, spot):
        part = hidden[0].shape[2]
        turned = jnp.concatenate(
            [right[spot, i * tokens : (i + 1) * tokens, :part].T for i in range(count)], axis=1
        )
        rows = part // 2
        cols = ffn_right.shape[2] - small.shape[3]
        for column in range(4):
            result = dot(turned, ffn_right[column]).astype(BF)
            for index in range(2):
                place = (spot, column // 2, column % 2, index)
                down_stage[place] = result[index * rows : (index + 1) * rows]
                down_stage[place + (slice(None), slice(cols, None))] = small[piece, index]

    def over(a, k):
        index = 4 + k
        if k % 2 == 0:
            source, peer = held[a].at[layer(k), :, 1 - x], here.over_x
        else:
            source, peer = held[a].at[layer(k), 1 - y], here.over_y
        return remote(source, first_in[a].at[k], slot(a, index), peer)

    def first_odd(a):
        for k in range(1, layers, 2):
            over(a, k).start()

    def first_even(a):
        for k in range(0, layers, 2):
            over(a, k).start()

    order = [*range(1, layers, 2), *range(0, layers, 2)]

    def second(a):
        for k in order:
            second_layer(a, k)

    def second_layer(a, k):
        at = layer(k)
        arrive(a, 4 + k, first_in[a].at[k])
        for i in range(2):
            if k % 2 == 0:
                held[a][at, i, x] = added(held[a], held[a][at, i, x], first_in[a][k, i])
            else:
                held[a][at, y, i] = added(held[a], held[a][at, y, i], first_in[a][k, i])
        across(a, k).start()

    def across(a, k):
        if k % 2 == 0:
            source, peer = held[a].at[layer(k), 1 - y, x], here.over_y
        else:
            source, peer = held[a].at[layer(k), y, 1 - x], here.over_x
        return remote(source, second_in[a].at[k], slot(a, 4 + layers + k), peer)

    def along(a, k):
        source = held[a].at[layer(k), y, x]
        return remote(source, z_in[a].at[k], slot(a, 4 + 2 * layers + k), here.up[k + 1])

    def third(a):
        for k in order:
            third_layer(a, k)

    def third_layer(a, k):
        arrive(a, 4 + layers + k, second_in[a].at[k])
        spot = (layer(k), y, x)
        held[a][spot] = added(held[a], held[a][spot], second_in[a][k])
        if k < layers - 1:
            along(a, k).start()

    def fourth(a):
        total = held[a][z, y, x].astype(F32)
        for k in range(layers - 1):
            arrive(a, 4 + 2 * layers + k, z_in[a].at[k])
            total = total + z_in[a][k].astype(F32)
        outs[a][...] = total

    ffn_left = load_left(0, ffn_in)
    go(ffn_left)
    down_right = [
        pltpu.make_async_copy(
            ref.at[column],
            ffn_right.at[column, pl.ds(i * tokens, tokens)],
            load.at[6 + column, i],
        )
        for i, ref in enumerate(grad_ffn)
        for column in range(4)
    ]

    def fetch_of(index, sources):
        return lambda piece, spot: load_right(index, spot, sources, piece, 0)

    def fetch_attn(piece, spot):
        return load_right(2, spot, packed, piece, 0) + load_right(4, spot, branch, piece, high_col)

    hold(ffn_left)
    turn_left(0)
    normed_left = load_left(1, normed)
    go(normed_left)
    go(down_right)

    def columns_out(a):
        return [(2, lambda: first_odd(a)), (3, lambda: first_even(a))]

    products(0, fetch_of(2, grad_gate), ffn_product(grad_gate), columns_out(0))
    hold(normed_left)
    turn_left(1)
    attended_left = load_left(0, attended)
    go(attended_left)
    products(
        1, fetch_of(2, grad_up), ffn_product(grad_up), [(SECOND_AT, lambda: second(0))] + columns_out(1)
    )
    hold(attended_left)
    turn_left(0)
    products(
        2, fetch_attn, attn_product,
        [(SECOND_AT, lambda: second(1)), (THIRD_AT, lambda: third(0))] + columns_out(2),
    )
    hold(down_right)
    layers_out = [(k + 1, lambda k=k: over(3, k).start()) for k in range(layers - 1)]
    products(
        3, fetch_of(2, hidden), down_product,
        [(SECOND_AT, lambda: second(2)), (THIRD_AT, lambda: third(1))] + layers_out,
    )
    over(3, layers - 1).start()
    third(2)
    second_layer(3, 0)
    second_layer(3, 1)
    third_layer(3, 0)
    second_layer(3, 2)
    third_layer(3, 1)
    second_layer(3, 3)
    third_layer(3, 2)
    third_layer(3, 3)
    for a in range(4):
        fourth(a)
    for a in range(4):
        for k in range(layers):
            over(a, k).wait_send()
            across(a, k).wait_send()
            if k < layers - 1:
                along(a, k).wait_send()


def finish(normed, packed, attended, branch, ffn_in, grad_gate, grad_up, hidden, grad_ffn, small, low_col):
    count = len(normed)
    tokens, width = normed[0].shape
    pieces, _, part = hidden[0].shape
    cols = grad_ffn[0].shape[2]
    layers = small.shape[0]
    ranks = 2 * layers
    rows, down_rows = width // ranks, pieces * part // ranks
    wide = packed[0].shape[2] + branch[0].shape[2]
    ends = [(rows, part), (rows, part), (rows, part), (down_rows, cols)]

    def buffers(*lead):
        return [pltpu.VMEM(lead + end, BF) for end in ends]

    operands = (
        *normed, *packed, *attended, *branch, *ffn_in, *grad_gate, *grad_up, *hidden, *grad_ffn, small,
    )
    return pl.pallas_call(
        functools.partial(finish_kernel, layers, count, low_col),
        out_shape=tuple(shape(end, F32) for end in ends),
        in_specs=[anywhere] * (len(operands) - 1) + [vmem],
        out_specs=(vmem,) * 4,
        scratch_shapes=[
            *buffers(layers, 2, 2),
            *buffers(layers, 2, 2),
            *buffers(layers, 2),
            *buffers(layers),
            *buffers(layers - 1),
            pltpu.VMEM((count * tokens, width), BF),
            pltpu.VMEM((2, width, count * tokens), BF),
            pltpu.VMEM((2, count * tokens, max(wide, part)), BF),
            pltpu.VMEM((pieces, count * tokens, cols), BF),
            pltpu.VMEM((2, layers, 2, rows, part), BF),
            pltpu.VMEM((2, 2, 2, 2, down_rows, cols), BF),
            pltpu.SemaphoreType.DMA((4, 4 + 3 * layers)),
            pltpu.SemaphoreType.DMA((4, 4 + 3 * layers)),
            pltpu.SemaphoreType.DMA((10, count)),
        ],
        compiler_params=pltpu.CompilerParams(
            collective_id=1, has_side_effects=True, vmem_limit_bytes=61 * MIB
        ),
        name="finish",
    )(*operands)


def rope_tables(positions):
    half = HEAD_DIM // 2
    frequency = rope_base ** (-(jnp.arange(half, dtype=F32) * 2.0 / HEAD_DIM))
    angles = positions.astype(F32)[:, None] * frequency[None, :]
    cosine, sine = jnp.cos(angles), jnp.sin(angles)
    repeat = LANE // HEAD_DIM
    return (
        jnp.concatenate([cosine, cosine] * repeat, axis=1),
        jnp.concatenate([-sine, sine] * repeat, axis=1),
    )


def pass_on(array, step, count):
    return lax.ppermute(array, "seq", [(i, i + step) for i in range(count - step)])


def pass_back(array, step, count):
    return lax.ppermute(array, "seq", [(i + step, i) for i in range(count - step)])


def row_plan(inputs, cotangent, depths, marks, block_params):
    micros, _, tokens, _ = inputs.shape
    seq, mine = lax.axis_size("seq"), lax.axis_index("seq")
    attn_g, ffn_g, routers, attn_w, gate_w, up_w, down_w, cols, used = block_params
    order = mine - jnp.arange(seq)
    marks = jnp.where((order >= 0)[:, None, None, None], marks[order % seq], -1.0)
    marks = marks.transpose(2, 1, 0, 3).reshape(micros, 2, seq * tokens)
    infos = [jnp.pad(marks[m], ((0, 6), (0, 0))) for m in range(micros)]
    cosine, sine = rope_tables(mine * tokens + jnp.arange(tokens, dtype=jnp.int32))
    states = [inputs[m, 0] for m in range(micros)]
    actives = [
        [
            jnp.broadcast_to((depths[m, 0] > r).astype(F32)[:, None], (tokens, LANE))
            for r in range(RECUR)
        ]
        for m in range(micros)
    ]
    saved = [[None] * RECUR for _ in range(micros)]
    for r in range(RECUR):
        made = []
        for m in range(micros):
            normed, queries, pair = pre_part(states[m], attn_g, attn_w, cosine, sine, cols)
            pairs = [pair] + [pass_on(pair, step, seq) for step in range(1, seq)]
            made.append((normed, queries, pairs))
        for m in range(micros):
            normed, queries, pairs = made[m]
            attended, logs = attend(queries, pairs, infos[m], r)
            after = post_part(
                states[m], attended, attn_w, ffn_g, routers[r], actives[m][r], gate_w, up_w, down_w, used
            )
            saved[m][r] = dict(
                after, state=states[m], normed=normed, queries=queries, pairs=pairs,
                attended=attended, logs=logs, active=actives[m][r],
            )
            states[m] = after["state_out"]
    grads = [cotangent[m, 0] for m in range(micros)]
    for r in reversed(range(RECUR)):
        partials = []
        for m in range(micros):
            s = saved[m][r]
            s.update(post_back(grads[m], s, ffn_g, routers[r], attn_w, gate_w, up_w, down_w, used))
            grad_queries, *grad_pairs = attend_back(
                s["queries"], s["pairs"], infos[m], s["attended"], s["logs"], s["grad_attended"], r
            )
            grad_pairs = [grad_pairs[0]] + [
                pass_back(grad_pairs[step], step, seq) for step in range(1, seq)
            ]
            partials.append((grad_queries, grad_pairs))
        for m in range(micros):
            s = saved[m][r]
            s["packed"], grads[m], s["attn_gain_grad"] = pre_back(
                *partials[m], s["partial"], s["state"], attn_g, attn_w, cosine, sine, cols
            )
    outputs = jnp.stack(states, axis=0)[:, None]
    input_grad = jnp.stack(grads, axis=0)[:, None]
    return outputs, input_grad, saved


def swap(array, pairs):
    seq, ranks = lax.axis_size("seq"), lax.axis_size("dp")
    moves = []
    for rank in range(ranks):
        for one, two in pairs[rank % 2]:
            moves += [(rank * seq + one, rank * seq + two), (rank * seq + two, rank * seq + one)]
    return lax.ppermute(array, ("dp", "seq"), moves)


ACROSS = (((0, 3), (1, 2)),) * 2
PARTNERS = (((0, 1), (2, 3)), ((0, 2), (1, 3)))


def second_micro():
    place = lax.axis_index("seq")
    return jnp.where(lax.axis_index("dp") % 2 == 0, place >= 2, place % 2 == 1)


def paired_start(inputs, cotangent):
    tokens = inputs.shape[2]
    second = second_micro()
    outer = is_outer()

    def split(array):
        own = jnp.where(second, array[1, 0], array[0, 0])
        return own, jnp.where(second, array[0, 0], array[1, 0]).astype(BF)

    places = jnp.arange(tokens, dtype=jnp.int32)
    low, high = jnp.where(outer, 0, 1), jnp.where(outer, 3, 2)
    tables = rope_tables(jnp.concatenate([low * tokens + places, high * tokens + places]))
    return split(inputs), split(cotangent), tables


def paired_plan(opened, actives, grads, tables, block_params):
    (own_grad, other_grad), (cosine, sine) = grads, tables
    info, state = opened["info"], opened["state"]
    tokens = own_grad.shape[0]
    late = lax.axis_index("seq") >= 2
    attn_g, ffn_g, routers, attn_w, gate_w, up_w, down_w, cols, used = block_params

    def join(own, other):
        other = other.astype(F32)
        return jnp.concatenate([jnp.where(late, other, own), jnp.where(late, own, other)], axis=0)

    def give(array):
        low, high = array[:tokens], array[tokens:]
        own = jnp.where(late, high, low)
        other = swap(jnp.where(late, low, high).astype(BF), ACROSS).astype(F32)
        second = second_micro()
        return jnp.stack([jnp.where(second, other, own), jnp.where(second, own, other)], axis=0)[:, None]

    saved = []
    for r in range(RECUR):
        active = actives[r]
        if r == 0:
            normed, queries, pair, partner, attended, logs = (
                opened[name]
                for name in ("normed", "queries", "pair", "partner", "attended", "logs")
            )
        else:
            normed, queries, pair = pre_part(state, attn_g, attn_w, cosine, sine, cols)
            partner = swap(pair, PARTNERS)
            if r == 1:
                other_grad, partner = lax.optimization_barrier((other_grad, partner))
                other_grad = swap(other_grad, ACROSS)
            part = attend_own(queries, pair, info, r)
            attended, logs = attend_rest(queries, partner, info, part, r)
        after = post_part(
            state, attended, attn_w, ffn_g, routers[r], active, gate_w, up_w, down_w, used
        )
        saved.append(
            dict(
                after, state=state, normed=normed, queries=queries, pair=pair, partner=partner,
                attended=attended, logs=logs, active=active,
            )
        )
        state = after["state_out"]
    outputs = give(state)
    grad = join(own_grad, other_grad)
    for r in reversed(range(RECUR)):
        s = saved[r]
        s.update(post_back(grad, s, ffn_g, routers[r], attn_w, gate_w, up_w, down_w, used))
        grad_partner, part, deltas = attend_rest_back(
            s["queries"], s["partner"], info, s["attended"], s["logs"], s["grad_attended"], r
        )
        grad_partner = swap(grad_partner, PARTNERS)
        grad_queries, grad_pair = attend_own_back(
            s["queries"], s["pair"], info, s["logs"], deltas, s["grad_attended"], part, r
        )
        s["packed"], grad, s["attn_gain_grad"] = pre_back(
            grad_queries, [grad_pair, grad_partner], s["partial"], s["state"], attn_g, attn_w,
            cosine, sine, cols,
        )
    return outputs, give(grad), [saved]


def local(
    inputs, cotangent, segments, depths, query_weight, key_weight, value_weight, out_weight,
    gate_weight, up_weight, down_weight, attn_gain, ffn_gain, router_weight,
):
    micros, _, tokens, width = inputs.shape
    seq, ranks = lax.axis_size("seq"), lax.axis_size("dp")
    rows = query_weight.shape[0]
    qc, kc = query_weight.shape[1], key_weight.shape[1]
    both = ("seq", "dp")

    attn_local = jnp.concatenate([query_weight, key_weight, value_weight, out_weight], axis=1)
    down_cols = down_weight.shape[1]
    span = ceil_to(max(rows, tokens), LANE)
    small = jnp.concatenate([attn_gain[None], ffn_gain[None], router_weight.T], axis=0).astype(F32)
    marks = jnp.concatenate([segments[:, 0], depths[:, 0]], axis=0).astype(F32)
    small = jnp.concatenate(
        [
            jnp.pad(small, ((0, 8 - small.shape[0]), (0, span - rows))),
            jnp.pad(marks, ((0, 8 - 2 * micros), (0, span - tokens))),
        ],
        axis=0,
    )
    parts = (
        attn_local, gate_weight, up_weight, jnp.pad(down_weight, ((0, 0), (0, BESIDE)))
    )
    direct = micros == 2 and (seq, ranks) == (4, 8)
    if direct:
        states, grads, tables = paired_start(inputs, cotangent)
        parts, small, states, grads, tables = lax.optimization_barrier(
            (parts, small, states, grads, tables)
        )
        gathered, gains, actives, opened = open_all(
            parts, small, *states, tables, micros, (qc, kc)
        )
    else:
        gathered = [lax.all_gather(part, both, axis=0, tiled=False) for part in parts]
        small = lax.all_gather(small, both, axis=0, tiled=False)
        small = small.reshape(seq, ranks, *small.shape[1:])
        marks = lax.dynamic_index_in_dim(small, lax.axis_index("dp"), 1, keepdims=False)
        marks = marks[:, 8 : 8 + 2 * micros, :tokens].reshape(seq, 2, micros, tokens)
        small = small[0, :, : 2 + RECUR, :rows].transpose(1, 0, 2).reshape(2 + RECUR, width)
        gains = [small[row : row + 1] for row in range(2 + RECUR)]
    attn_w, gate_w, up_w, down_w = (full.reshape(seq, -1, full.shape[-1]) for full in gathered)
    attn_g, ffn_g, *routers = gains
    used = qc + 2 * kc
    total_cols = attn_w.shape[2]
    low_col = used // LANE * LANE
    block_params = (attn_g, ffn_g, routers, attn_w, gate_w, up_w, down_w, (qc, kc), used)
    if direct:
        outputs, input_grad, saved = paired_plan(opened, actives, grads, tables, block_params)
    else:
        outputs, input_grad, saved = row_plan(inputs, cotangent, depths, marks, block_params)
    flat = [steps[r] for r in reversed(range(RECUR)) for steps in saved]

    def every(name):
        return [s[name] for s in flat]

    attn_gain_sum, ffn_gain_sum = sum(every("attn_gain_grad")), sum(every("ffn_gain_grad"))
    router_sums = [sum(steps[r]["router_grad"] for steps in saved) for r in range(RECUR)]
    small_sum = jnp.concatenate([attn_gain_sum, ffn_gain_sum, *router_sums], axis=0)
    small_sum = small_sum.T.reshape(ranks, rows, 2 + RECUR)
    if direct:
        small_sum = jnp.pad(
            small_sum, ((0, 0), (0, down_weight.shape[0] - rows), (0, BESIDE - 2 - RECUR))
        ).astype(BF)
        gate_grad, up_grad, attn_grad, down_grad = finish(
            every("normed"), every("packed"), every("attended"), every("grad_branch"),
            every("ffn_in"), every("grad_gate"), every("grad_up"), every("hidden"),
            every("grad_ffn"), small_sum.reshape(ranks // 2, 2, -1, BESIDE), low_col,
        )
        small_own = down_grad[:rows, down_cols : down_cols + 2 + RECUR].T
    else:
        down_sum = down_sums(every("hidden"), every("grad_ffn"))
        gate_sum, up_sum = pair_sums(every("ffn_in"), every("grad_gate"), every("grad_up"))
        attn_sum = attn_sums(
            every("normed"), every("packed"), every("attended"), every("grad_branch"),
            low_col, total_cols,
        )
        small_sum = jnp.broadcast_to(small_sum[None], (seq,) + small_sum.shape)
        sums = [
            part.reshape(seq, ranks, -1, part.shape[-1])
            for part in (gate_sum, up_sum, attn_sum, down_sum, small_sum)
        ]
        sums = [lax.psum_scatter(part, "seq", scatter_dimension=0) for part in sums]
        sums = [lax.psum_scatter(part, "dp", scatter_dimension=0).astype(F32) for part in sums]
        gate_grad, up_grad, attn_grad, down_grad, small_own = sums
        small_own = small_own.T
    down_grad = down_grad[:, :down_cols]

    return (
        outputs,
        input_grad,
        attn_grad[:, :qc],
        attn_grad[:, qc : qc + kc],
        attn_grad[:, qc + kc : used],
        attn_grad[:, used:],
        gate_grad,
        up_grad,
        down_grad,
        small_own[0],
        small_own[1],
        small_own[2:].T,
    )


def solution(mesh):
    data = P(None, "dp", "seq", None)
    marks = P(None, "dp", "seq")
    weight = P("dp", "seq")
    in_specs = (data, data, marks, marks) + (weight,) * 7 + (P("dp"), P("dp"), P("dp", None))
    out_specs = (data, data) + (weight,) * 7 + (P("dp"), P("dp"), P("dp", None))
    return jax.shard_map(local, mesh=mesh, in_specs=in_specs, out_specs=out_specs, check_vma=False)
```

```python
import functools

import jax
import jax.numpy as jnp
from jax import lax
from jax.experimental import pallas as pl
from jax.experimental.pallas import tpu as pltpu
from jax.sharding import PartitionSpec as P

HEADS = 15
KV_HEADS = 5
HEAD_DIM = 64
RECUR = 3
GROUP = HEADS // KV_HEADS
KW = KV_HEADS * HEAD_DIM
QW = HEADS * HEAD_DIM
LANE = 128
MIB = 2**20
BESIDE = 16

epsilon = 1e-05
rope_base = 10000.0

NN = (((1,), (0,)), ((), ()))
NT = (((1,), (1,)), ((), ()))
BF = jnp.bfloat16
F32 = jnp.float32

vmem = pl.BlockSpec(memory_space=pltpu.VMEM)


def dot(left, right, dims=NN):
    return lax.dot_general(left, right, dims, preferred_element_type=F32)


def ceil_to(size, unit):
    return -(-size // unit) * unit


def shape(dims, dtype):
    return jax.ShapeDtypeStruct(dims, dtype)


def params(limit):
    return pltpu.CompilerParams(vmem_limit_bytes=limit * MIB)


def pin(array):
    return pltpu.with_memory_space_constraint(array, pltpu.VMEM)


def wide_limit(weight, limit):
    return limit if whole_lanes(weight) else 62


def whole_lanes(weight):
    return weight.shape[-1] % LANE == 0


def placed(weight):
    return pin(weight) if whole_lanes(weight) else weight


def side_by_side(ref, rows=slice(None)):
    return jnp.concatenate([ref[piece, rows] for piece in range(ref.shape[0])], axis=1)


def turn(block, cosine, sine):
    lanes = lax.broadcasted_iota(jnp.int32, block.shape, 1) % HEAD_DIM
    partner = jnp.where(
        lanes < HEAD_DIM // 2,
        pltpu.roll(block, LANE - HEAD_DIM // 2, 1),
        pltpu.roll(block, HEAD_DIM // 2, 1),
    )
    return block * cosine + partner * sine


def norm_back(grad_out, values_in, gain):
    inverse = lax.rsqrt(jnp.mean(values_in * values_in, axis=-1, keepdims=True) + epsilon)
    weighted = grad_out * gain
    inner = jnp.mean(weighted * values_in, axis=-1, keepdims=True)
    grad_gain = jnp.sum(grad_out * values_in * inverse, axis=0, keepdims=True)
    return weighted * inverse - values_in * (inverse * inverse * inverse * inner), grad_gain


def pre_kernel(cols, state, gain, weight, cosine, sine, normed, queries, pair, qbuf, kbuf):
    qc, kc = cols
    values_in = state[...]
    inverse = lax.rsqrt(jnp.mean(values_in * values_in, axis=-1, keepdims=True) + epsilon)
    low = (values_in * inverse * gain[...]).astype(BF)
    normed[...] = low
    used = min(ceil_to(qc + 2 * kc, LANE), weight.shape[2])
    for piece in range(weight.shape[0]):
        made = dot(low, weight[piece, :, :used])
        qbuf[:, piece * qc : (piece + 1) * qc] = made[:, :qc]
        kbuf[:, piece * kc : (piece + 1) * kc] = made[:, qc : qc + kc]
        pair[:, KW + piece * kc : KW + (piece + 1) * kc] = made[:, qc + kc : qc + 2 * kc].astype(BF)
    for buf, out, width, scale in ((qbuf, queries, QW, HEAD_DIM**-0.5), (kbuf, pair, KW, 1.0)):
        for start in range(0, width, LANE):
            stop = min(start + LANE, width)
            turned = turn(buf[:, start : start + LANE], cosine[...], sine[...]) * scale
            out[:, start:stop] = turned[:, : stop - start].astype(BF)


def pre_part(state, gain, weight, cosine, sine, cols):
    tokens, width = state.shape
    return pl.pallas_call(
        functools.partial(pre_kernel, cols),
        out_shape=(
            shape((tokens, width), BF),
            shape((tokens, QW), BF),
            shape((tokens, 2 * KW), BF),
        ),
        in_specs=[vmem] * 5,
        out_specs=(vmem,) * 3,
        scratch_shapes=[
            pltpu.VMEM((tokens, ceil_to(QW, LANE)), F32),
            pltpu.VMEM((tokens, ceil_to(KW, LANE)), F32),
        ],
        compiler_params=params(wide_limit(weight, 14)),
        name="pre",
    )(state, gain, placed(weight), cosine, sine)


def fill_bias(info, bias, recursion):
    keys, tokens = bias.shape
    columns = info[...].T
    place = lax.broadcasted_iota(jnp.int32, (keys, tokens), 0)
    query = lax.broadcasted_iota(jnp.int32, (keys, tokens), 1)
    apart = place % tokens - place // tokens * tokens - query
    same = columns[:, 0:1] == info[0:1, 0:tokens]
    live = columns[:, 1:2] > recursion
    seen = same & (((apart < 0) & live) | (apart == 0))
    bias[...] = jnp.where(seen, 0.0, -1e30)


def head_cols(head):
    return slice(head * HEAD_DIM, (head + 1) * HEAD_DIM)


def stack_heads(ref, group):
    heads = range(group * GROUP, (group + 1) * GROUP)
    return jnp.concatenate([ref[:, head_cols(head)] for head in heads], axis=0)


def attend_kernel(blocks, recursion, *refs):
    queries, pairs = refs[0], refs[1 : 1 + blocks]
    info, attended, logs, bias = refs[1 + blocks :]
    tokens = queries.shape[0]
    keys = blocks * tokens
    fill_bias(info, bias, recursion)
    logs[...] = jnp.zeros(logs.shape, F32)
    for group in range(KV_HEADS):
        key = jnp.concatenate([ref[:, head_cols(group)] for ref in pairs], axis=0)
        value = jnp.concatenate([ref[:, head_cols(KV_HEADS + group)] for ref in pairs], axis=0)
        value_t = jnp.concatenate([value.T, jnp.ones((16, keys), BF)], axis=0)
        query = stack_heads(queries, group)
        scores = dot(key, query, NT) + jnp.concatenate([bias[...]] * GROUP, axis=1)
        top = jnp.max(scores, axis=0, keepdims=True)
        weights = jnp.exp(scores - top).astype(BF)
        mixed = dot(value_t, weights)
        total = mixed[HEAD_DIM : HEAD_DIM + 1]
        mixed = mixed[:HEAD_DIM] * (1.0 / total)
        log_total = top + jnp.log(total)
        for offset in range(GROUP):
            head = group * GROUP + offset
            span = slice(offset * tokens, (offset + 1) * tokens)
            attended[:, head_cols(head)] = mixed[:, span].T.astype(BF)
            logs[head : head + 1, :] = log_total[:, span]


def attend(queries, pairs, info, recursion):
    tokens = queries.shape[0]
    blocks = len(pairs)
    return pl.pallas_call(
        functools.partial(attend_kernel, blocks, recursion),
        out_shape=(shape((tokens, QW), BF), shape((ceil_to(HEADS, 8), tokens), F32)),
        in_specs=[vmem] * (2 + blocks),
        out_specs=(vmem, vmem),
        scratch_shapes=[pltpu.VMEM((blocks * tokens, tokens), F32)],
        compiler_params=params(40),
        name="attend",
    )(queries, *pairs, info)


def attend_back_kernel(blocks, recursion, *refs):
    queries, pairs = refs[0], refs[1 : 1 + blocks]
    info, attended, logs, grad, grad_queries = refs[1 + blocks : 6 + blocks]
    grad_pairs, bias = refs[6 + blocks : 6 + 2 * blocks], refs[6 + 2 * blocks]
    tokens = queries.shape[0]
    fill_bias(info, bias, recursion)
    product = (attended[...].astype(F32) * grad[...].astype(F32)).T
    for group in range(KV_HEADS):
        key = jnp.concatenate([ref[:, head_cols(group)] for ref in pairs], axis=0)
        value = jnp.concatenate([ref[:, head_cols(KV_HEADS + group)] for ref in pairs], axis=0)
        key_t = key.T
        query = stack_heads(queries, group)
        grad_mixed = stack_heads(grad, group)
        heads = range(group * GROUP, (group + 1) * GROUP)
        delta = jnp.concatenate(
            [jnp.sum(product[head_cols(head)], axis=0, keepdims=True) for head in heads], axis=1
        )
        log_total = jnp.concatenate([logs[head : head + 1, :] for head in heads], axis=1)
        scores = dot(key, query, NT) + jnp.concatenate([bias[...]] * GROUP, axis=1)
        probs = jnp.exp(scores - log_total)
        grad_probs = dot(value, grad_mixed, NT)
        grad_scores = (probs * (grad_probs - delta)).astype(BF)
        grad_value = dot(probs.astype(BF), grad_mixed)
        grad_key = dot(grad_scores, query)
        grad_query = dot(key_t, grad_scores) * HEAD_DIM**-0.5
        for offset, head in enumerate(heads):
            span = slice(offset * tokens, (offset + 1) * tokens)
            grad_queries[:, head_cols(head)] = grad_query[:, span].T
        for block, ref in enumerate(grad_pairs):
            rows = slice(block * tokens, (block + 1) * tokens)
            ref[:, head_cols(group)] = grad_key[rows].astype(ref.dtype)
            ref[:, head_cols(KV_HEADS + group)] = grad_value[rows].astype(ref.dtype)


def attend_back(queries, pairs, info, attended, logs, grad, recursion):
    tokens = queries.shape[0]
    blocks = len(pairs)
    return pl.pallas_call(
        functools.partial(attend_back_kernel, blocks, recursion),
        out_shape=(shape((tokens, QW), F32), shape((tokens, 2 * KW), F32))
        + (shape((tokens, 2 * KW), BF),) * (blocks - 1),
        in_specs=[vmem] * (5 + blocks),
        out_specs=(vmem,) * (1 + blocks),
        scratch_shapes=[pltpu.VMEM((blocks * tokens, tokens), F32)],
        compiler_params=params(48),
        name="attend_back",
    )(queries, *pairs, info, attended, logs, grad)


def is_outer():
    place = lax.axis_index("seq")
    return (place == 0) | (place == 3)


def block_bias(info, bias, index, key_block, query_block, recursion, columns, diagonal):
    block = bias.shape[1]

    def span(which):
        return pl.ds(pl.multiple_of(which * block, block), block)

    same = columns[span(key_block), 0:1] == info[0:1, span(query_block)]
    seen = columns[span(key_block), 1:2] > recursion
    if diagonal:
        key = lax.broadcasted_iota(jnp.int32, (block, block), 0)
        query = lax.broadcasted_iota(jnp.int32, (block, block), 1)
        seen = ((key < query) & seen) | (key == query)
    bias[index] = jnp.where(same & seen, 0.0, -1e30)


def tall_heads(ref, rows, group):
    heads = range(group * GROUP, (group + 1) * GROUP)
    return jnp.concatenate([ref[rows, head_cols(head)] for head in heads], axis=0)


def thrice(bias):
    return jnp.concatenate([bias] * GROUP, axis=1)


def with_ones(value):
    return jnp.concatenate([value.T, jnp.ones((16, value.shape[0]), BF)], axis=0)


def own_kernel(recursion, queries, pair, info, part, columns, bias):
    block = queries.shape[0] // 2
    wide = GROUP * block
    columns[...] = info[...].T
    block_bias(info, bias, 0, 0, 0, recursion, columns, True)
    block_bias(info, bias, 1, 0, 1, recursion, columns, False)
    block_bias(info, bias, 2, 1, 1, recursion, columns, True)
    low, high = slice(0, block), slice(block, 2 * block)
    for group in range(KV_HEADS):
        kc, vc = head_cols(group), head_cols(KV_HEADS + group)
        query_low, query_high = tall_heads(queries, low, group), tall_heads(queries, high, group)
        first = dot(pair[low, kc], query_low, NT) + thrice(bias[0])
        second = dot(pair[low, kc], query_high, NT) + thrice(bias[1])
        third = dot(pair[high, kc], query_high, NT) + thrice(bias[2])
        value_low, value_high = with_ones(pair[low, vc]), with_ones(pair[high, vc])
        top = jnp.max(first, axis=0, keepdims=True)
        mixed = dot(value_low, jnp.exp(first - top).astype(BF))
        part[group, : HEAD_DIM + 8, :wide] = mixed[: HEAD_DIM + 8]
        part[group, HEAD_DIM + 8 :, :wide] = jnp.broadcast_to(top, (8, wide))
        top = jnp.maximum(
            jnp.max(second, axis=0, keepdims=True), jnp.max(third, axis=0, keepdims=True)
        )
        mixed = dot(value_low, jnp.exp(second - top).astype(BF))
        mixed += dot(value_high, jnp.exp(third - top).astype(BF))
        part[group, : HEAD_DIM + 8, wide:] = mixed[: HEAD_DIM + 8]
        part[group, HEAD_DIM + 8 :, wide:] = jnp.broadcast_to(top, (8, wide))


def attend_own(queries, pair, info, recursion):
    tokens = queries.shape[0]
    block = tokens // 2
    return pl.pallas_call(
        functools.partial(own_kernel, recursion),
        out_shape=shape((KV_HEADS, HEAD_DIM + 16, GROUP * tokens), F32),
        in_specs=[vmem] * 3,
        out_specs=vmem,
        scratch_shapes=[
            pltpu.VMEM(info.shape[::-1], F32),
            pltpu.VMEM((3, block, block), F32),
        ],
        compiler_params=params(14),
        name="attend_own",
    )(queries, pair, info)


def rest_rows(block):
    outer = is_outer()
    shift = pl.multiple_of(jnp.where(outer, block, 0), block)
    return outer, pl.ds(shift, block)


def rest_kernel(recursion, queries, pair, info, part, attended, logs, columns, bias):
    block = queries.shape[0] // 2
    wide = GROUP * block
    columns[...] = info[...].T
    outer, rows = rest_rows(block)
    fifth = jnp.where(outer, 1, 0)
    block_bias(info, bias, 0, 2, 1, recursion, columns, False)
    block_bias(info, bias, 1, 2 + fifth, fifth, recursion, columns, False)
    low, high = slice(0, block), slice(block, 2 * block)
    logs[...] = jnp.zeros(logs.shape, F32)
    for group in range(KV_HEADS):
        kc, vc = head_cols(group), head_cols(KV_HEADS + group)
        fourth = dot(pair[low, kc], tall_heads(queries, high, group), NT) + thrice(bias[0])
        fifth = dot(pair[rows, kc], tall_heads(queries, rows, group), NT) + thrice(bias[1])
        own_low, own_high = part[group, :, :wide], part[group, :, wide:]
        top_low, top_high = own_low[HEAD_DIM + 8 : HEAD_DIM + 9], own_high[HEAD_DIM + 8 : HEAD_DIM + 9]
        fifth_top = jnp.max(fifth, axis=0, keepdims=True)
        new_low = jnp.where(outer, top_low, jnp.maximum(top_low, fifth_top))
        new_high = jnp.maximum(top_high, jnp.max(fourth, axis=0, keepdims=True))
        new_high = jnp.where(outer, jnp.maximum(new_high, fifth_top), new_high)
        fourth = jnp.exp(fourth - new_high).astype(BF)
        fifth = jnp.exp(fifth - jnp.where(outer, new_high, new_low)).astype(BF)
        added_high = dot(with_ones(pair[low, vc]), fourth)[: HEAD_DIM + 8]
        added = dot(with_ones(pair[rows, vc]), fifth)[: HEAD_DIM + 8]
        mixed_low = own_low[: HEAD_DIM + 8] * jnp.exp(top_low - new_low)
        mixed_low += jnp.where(outer, 0.0, added)
        mixed_high = own_high[: HEAD_DIM + 8] * jnp.exp(top_high - new_high)
        mixed_high += added_high + jnp.where(outer, added, 0.0)
        for start, mixed, top in ((0, mixed_low, new_low), (block, mixed_high, new_high)):
            total = mixed[HEAD_DIM : HEAD_DIM + 1]
            final = mixed[:HEAD_DIM] * (1.0 / total)
            log_total = top + jnp.log(total)
            for offset in range(GROUP):
                head = group * GROUP + offset
                span = slice(offset * block, (offset + 1) * block)
                attended[start : start + block, head_cols(head)] = final[:, span].T.astype(BF)
                logs[head : head + 1, start : start + block] = log_total[:, span]


def attend_rest(queries, pair, info, part, recursion):
    tokens = queries.shape[0]
    block = tokens // 2
    return pl.pallas_call(
        functools.partial(rest_kernel, recursion),
        out_shape=(shape((tokens, QW), BF), shape((ceil_to(HEADS, 8), tokens), F32)),
        in_specs=[vmem] * 4,
        out_specs=(vmem, vmem),
        scratch_shapes=[
            pltpu.VMEM(info.shape[::-1], F32),
            pltpu.VMEM((2, block, block), F32),
        ],
        compiler_params=params(14),
        name="attend_rest",
    )(queries, pair, info, part)


def flat_row(ref, cols, group):
    heads = range(group * GROUP, (group + 1) * GROUP)
    return jnp.concatenate([ref[head : head + 1, cols] for head in heads], axis=1)


def block_back(key, value, query, grad_mixed, bias, log_total, delta):
    probs = jnp.exp(dot(key, query, NT) + thrice(bias) - log_total)
    grad_scores = (probs * (dot(value, grad_mixed, NT) - delta)).astype(BF)
    grad_value = dot(probs.astype(BF), grad_mixed)
    grad_key = dot(grad_scores, query)
    return dot(key.T, grad_scores), grad_key, grad_value


def rest_back_kernel(
    recursion, queries, pair, info, attended, logs, grad, grad_pair, part, deltas, columns, bias
):
    block = queries.shape[0] // 2
    wide = GROUP * block
    columns[...] = info[...].T
    outer, rows = rest_rows(block)
    fifth = jnp.where(outer, 1, 0)
    block_bias(info, bias, 0, 2, 1, recursion, columns, False)
    block_bias(info, bias, 1, 2 + fifth, fifth, recursion, columns, False)
    low, high = slice(0, block), slice(block, 2 * block)
    product = (attended[...].astype(F32) * grad[...].astype(F32)).T
    deltas[...] = jnp.zeros(deltas.shape, F32)
    for head in range(HEADS):
        deltas[head : head + 1, :] = jnp.sum(product[head_cols(head)], axis=0, keepdims=True)
    for group in range(KV_HEADS):
        kc, vc = head_cols(group), head_cols(KV_HEADS + group)
        query_high, key_high, value_high = block_back(
            pair[low, kc], pair[low, vc], tall_heads(queries, high, group),
            tall_heads(grad, high, group), bias[0], flat_row(logs, high, group),
            flat_row(deltas, high, group),
        )
        query, key, value = block_back(
            pair[rows, kc], pair[rows, vc], tall_heads(queries, rows, group),
            tall_heads(grad, rows, group), bias[1], flat_row(logs, rows, group),
            flat_row(deltas, rows, group),
        )
        part[group, :, :wide] = jnp.where(outer, 0.0, query)
        part[group, :, wide:] = query_high + jnp.where(outer, query, 0.0)
        grad_pair[low, kc] = (key_high + jnp.where(outer, 0.0, key)).astype(BF)
        grad_pair[low, vc] = (value_high + jnp.where(outer, 0.0, value)).astype(BF)
        grad_pair[high, kc] = jnp.where(outer, key, 0.0).astype(BF)
        grad_pair[high, vc] = jnp.where(outer, value, 0.0).astype(BF)


def attend_rest_back(queries, pair, info, attended, logs, grad, recursion):
    tokens = queries.shape[0]
    block = tokens // 2
    return pl.pallas_call(
        functools.partial(rest_back_kernel, recursion),
        out_shape=(
            shape((tokens, 2 * KW), BF),
            shape((KV_HEADS, HEAD_DIM, GROUP * tokens), F32),
            shape(logs.shape, F32),
        ),
        in_specs=[vmem] * 6,
        out_specs=(vmem,) * 3,
        scratch_shapes=[
            pltpu.VMEM(info.shape[::-1], F32),
            pltpu.VMEM((2, block, block), F32),
        ],
        compiler_params=params(18),
        name="attend_rest_back",
    )(queries, pair, info, attended, logs, grad)


def own_back_kernel(
    recursion, queries, pair, info, logs, deltas, grad, part, grad_queries, grad_pair, columns, bias
):
    block = queries.shape[0] // 2
    wide = GROUP * block
    columns[...] = info[...].T
    block_bias(info, bias, 0, 0, 0, recursion, columns, True)
    block_bias(info, bias, 1, 0, 1, recursion, columns, False)
    block_bias(info, bias, 2, 1, 1, recursion, columns, True)
    low, high = slice(0, block), slice(block, 2 * block)
    for group in range(KV_HEADS):
        kc, vc = head_cols(group), head_cols(KV_HEADS + group)
        made = []
        for index, keys, side in ((0, low, low), (1, low, high), (2, high, high)):
            made.append(
                block_back(
                    pair[keys, kc], pair[keys, vc], tall_heads(queries, side, group),
                    tall_heads(grad, side, group), bias[index], flat_row(logs, side, group),
                    flat_row(deltas, side, group),
                )
            )
        first, second, third = made
        grad_pair[low, kc] = first[1] + second[1]
        grad_pair[low, vc] = first[2] + second[2]
        grad_pair[high, kc] = third[1]
        grad_pair[high, vc] = third[2]
        query_low = (part[group, :, :wide] + first[0]) * HEAD_DIM**-0.5
        query_high = (part[group, :, wide:] + second[0] + third[0]) * HEAD_DIM**-0.5
        for start, made_query in ((0, query_low), (block, query_high)):
            for offset in range(GROUP):
                head = group * GROUP + offset
                span = slice(offset * block, (offset + 1) * block)
                grad_queries[start : start + block, head_cols(head)] = made_query[:, span].T


def attend_own_back(queries, pair, info, logs, deltas, grad, part, recursion):
    tokens = queries.shape[0]
    block = tokens // 2
    return pl.pallas_call(
        functools.partial(own_back_kernel, recursion),
        out_shape=(shape((tokens, QW), F32), shape((tokens, 2 * KW), F32)),
        in_specs=[vmem] * 7,
        out_specs=(vmem,) * 2,
        scratch_shapes=[
            pltpu.VMEM(info.shape[::-1], F32),
            pltpu.VMEM((3, block, block), F32),
        ],
        compiler_params=params(18),
        name="attend_own_back",
    )(queries, pair, info, logs, deltas, grad, part)


def post_kernel(
    used, cols, state, attended, attn_w, gain, router, active, gate_w, up_w, down_w,
    state_out, normed_out, gate_out, up_out, hidden_out, midway_out, update_out, routed,
    normed, midway, update, branch, total, stage, sems,
):
    pieces, _, part = gate_w.shape
    wide = down_w.shape[2]
    low_col = used // LANE * LANE

    def ship(index, source, target):
        return pltpu.make_async_copy(source, target, sems.at[index])

    def ship_piece(piece):
        spot = lax.rem(piece, 2)
        return [
            ship(3 + 3 * spot + index, stage.at[spot, index], out.at[piece])
            for index, out in enumerate((gate_out, up_out, hidden_out))
        ]

    for piece in range(pieces):
        made = dot(attended[...], attn_w[piece, :, low_col:])
        branch[:, piece * cols : (piece + 1) * cols] = made[:, used - low_col :]
    between = state[...] + branch[...]
    midway[...] = between
    ship(0, midway, midway_out).start()
    inverse = lax.rsqrt(jnp.mean(between * between, axis=-1, keepdims=True) + epsilon)
    normed[...] = (between * inverse * gain[...]).astype(BF)
    ship(1, normed, normed_out).start()
    chance = 1.0 / (1.0 + jnp.exp(-jnp.sum(state[...] * router[...], axis=-1, keepdims=True)))
    routed[...] = jnp.broadcast_to(chance, routed.shape)
    total[...] = jnp.zeros(total.shape, F32)

    def step(piece, carry):
        spot = lax.rem(piece, 2)

        @pl.when(piece >= 2)
        def _():
            for copy in ship_piece(piece - 2):
                copy.wait()

        rows = pl.ds(pl.multiple_of(piece * part, part), part)
        half = normed.shape[0] // 2
        for span in (slice(0, half), slice(half, 2 * half)):
            pre = dot(normed[span], jnp.concatenate([gate_w[piece], up_w[piece]], axis=1))
            gate, up = pre[:, :part], pre[:, part:]
            hidden = (gate / (1.0 + jnp.exp(-gate)) * up).astype(BF)
            for index, made in enumerate((gate.astype(BF), up.astype(BF), hidden)):
                stage[spot, index, span] = made
            total[span] += dot(hidden, side_by_side(down_w, rows))
        for copy in ship_piece(piece):
            copy.start()
        return carry

    lax.fori_loop(0, pieces, step, 0)
    for piece in range(pieces):
        span = slice(piece * cols, (piece + 1) * cols)
        branch[:, span] = branch[:, span] + total[:, piece * wide : piece * wide + cols]
    changed = branch[...]
    update[...] = changed.astype(BF)
    ship(2, update, update_out).start()
    state_out[...] = state[...] + (active[:, 0:1] * routed[:, 0:1]) * changed
    for index, (source, target) in enumerate(
        ((midway, midway_out), (normed, normed_out), (update, update_out))
    ):
        ship(index, source, target).wait()
    for piece in range(max(0, pieces - 2), pieces):
        for copy in ship_piece(piece):
            copy.wait()


anywhere = pl.BlockSpec(memory_space=pl.ANY)


def post_part(state, attended, attn_w, gain, router, active, gate_w, up_w, down_w, used):
    tokens, width = state.shape
    pieces, _, part = gate_w.shape
    made = pl.pallas_call(
        functools.partial(post_kernel, used, width // pieces),
        out_shape=(
            shape((tokens, width), F32),
            shape((tokens, width), BF),
            shape((pieces, tokens, part), BF),
            shape((pieces, tokens, part), BF),
            shape((pieces, tokens, part), BF),
            shape((tokens, width), F32),
            shape((tokens, width), BF),
            shape((tokens, LANE), F32),
        ),
        in_specs=[vmem] * 9,
        out_specs=(vmem,) + (anywhere,) * 6 + (vmem,),
        scratch_shapes=[
            pltpu.VMEM((tokens, width), BF),
            pltpu.VMEM((tokens, width), F32),
            pltpu.VMEM((tokens, width), BF),
            pltpu.VMEM((tokens, width), F32),
            pltpu.VMEM((tokens, pieces * down_w.shape[2]), F32),
            pltpu.VMEM((2, 3, tokens, part), BF),
            pltpu.SemaphoreType.DMA((9,)),
        ],
        compiler_params=params(wide_limit(gate_w, 22)),
        name="post",
    )(state, attended, placed(attn_w), gain, router, active, placed(gate_w), placed(up_w),
      placed(down_w))
    names = ("state_out", "ffn_in", "gate", "up", "hidden", "midway", "update", "routed")
    return dict(zip(names, made))


def post_back_kernel(
    used, cols, grad_state, update, routed, active, state, midway, gain, router, attn_w,
    gate_w, up_w, down_w, gate_pre, up_pre,
    grad_attended, partial, gain_grad, router_grad, ffn_out, gate_out, up_out, branch_out,
    scaled, total, grad_ffn, grad_branch, fetched, stage, load, sems,
):
    pieces, _, part = gate_w.shape
    low_col = used // LANE * LANE

    def ship(index, source, target):
        return pltpu.make_async_copy(source, target, sems.at[index])

    def ship_piece(piece):
        spot = lax.rem(piece, 2)
        return [
            ship(2 + 2 * spot + index, stage.at[spot, index], out.at[piece])
            for index, out in enumerate((gate_out, up_out))
        ]

    def fetch(piece):
        spot = lax.rem(piece, 2)
        return [
            pltpu.make_async_copy(ref.at[piece], fetched.at[spot, index], load.at[spot, index])
            for index, ref in enumerate((gate_pre, up_pre))
        ]

    for copy in fetch(0):
        copy.start()
    chance = routed[:, 0:1]
    weight = active[:, 0:1] * chance
    grad = grad_state[...]
    change = grad * weight
    scaled[...] = change
    slope = jnp.sum(grad * update[...].astype(F32), axis=-1, keepdims=True) * weight * (1.0 - chance)
    router_grad[...] = jnp.sum(state[...] * slope, axis=0, keepdims=True)
    partial[...] = grad + slope * router[...]
    low = change.astype(BF)
    for piece in range(pieces):
        grad_ffn[piece] = jnp.zeros(grad_ffn.shape[1:], BF)
        grad_ffn[piece, :, :cols] = low[:, piece * cols : (piece + 1) * cols]
    ship(0, grad_ffn, ffn_out).start()
    total[...] = jnp.zeros(total.shape, F32)

    def step(piece, carry):
        spot = lax.rem(piece, 2)

        @pl.when(piece + 1 < pieces)
        def _():
            for copy in fetch(piece + 1):
                copy.start()

        @pl.when(piece >= 2)
        def _():
            for copy in ship_piece(piece - 2):
                copy.wait()

        for copy in fetch(piece):
            copy.wait()
        rows = pl.ds(pl.multiple_of(piece * part, part), part)
        grad_hidden = dot(side_by_side(grad_ffn), side_by_side(down_w, rows), NT)
        gate = fetched[spot, 0].astype(F32)
        chance = 1.0 / (1.0 + jnp.exp(-gate))
        smooth = gate * chance
        slope = chance + smooth * (1.0 - chance)
        grad_gate = (grad_hidden * fetched[spot, 1].astype(F32) * slope).astype(BF)
        grad_up = (grad_hidden * smooth).astype(BF)
        stage[spot, 0] = grad_gate
        stage[spot, 1] = grad_up
        total[...] += dot(
            jnp.concatenate([grad_gate, grad_up], axis=1),
            jnp.concatenate([gate_w[piece], up_w[piece]], axis=1),
            NT,
        )
        for copy in ship_piece(piece):
            copy.start()
        return carry

    lax.fori_loop(0, pieces, step, 0)
    grad_midway, grad_gain = norm_back(total[...], midway[...], gain[...])
    gain_grad[...] = grad_gain
    partial[...] = partial[...] + grad_midway
    low = (scaled[...] + grad_midway).astype(BF)
    shift = used - low_col
    for piece in range(pieces):
        if grad_branch.shape[2] > cols:
            grad_branch[piece] = jnp.zeros(grad_branch.shape[1:], BF)
        grad_branch[piece, :, shift : shift + cols] = low[:, piece * cols : (piece + 1) * cols]
    ship(1, grad_branch, branch_out).start()
    grad = None
    for piece in range(pieces):
        made = dot(grad_branch[piece], attn_w[piece, :, low_col:], NT)
        grad = made if grad is None else grad + made
    grad_attended[...] = grad.astype(BF)
    ship(0, grad_ffn, ffn_out).wait()
    ship(1, grad_branch, branch_out).wait()
    for piece in range(max(0, pieces - 2), pieces):
        for copy in ship_piece(piece):
            copy.wait()


def post_back(grad_state, s, gain, router, attn_w, gate_w, up_w, down_w, used):
    state = s["state"]
    tokens, width = state.shape
    pieces, _, part = gate_w.shape
    branch_dims = (pieces, tokens, attn_w.shape[2] - used // LANE * LANE)
    ffn_dims = (pieces, tokens, down_w.shape[2])
    made = pl.pallas_call(
        functools.partial(post_back_kernel, used, width // pieces),
        out_shape=(
            shape((tokens, QW), BF),
            shape((tokens, width), F32),
            shape((1, width), F32),
            shape((1, width), F32),
            shape(ffn_dims, BF),
            shape((pieces, tokens, part), BF),
            shape((pieces, tokens, part), BF),
            shape(branch_dims, BF),
        ),
        in_specs=[vmem] * 12 + [anywhere] * 2,
        out_specs=(vmem,) * 4 + (anywhere,) * 4,
        scratch_shapes=[
            pltpu.VMEM((tokens, width), F32),
            pltpu.VMEM((tokens, width), F32),
            pltpu.VMEM(ffn_dims, BF),
            pltpu.VMEM(branch_dims, BF),
            pltpu.VMEM((2, 2, tokens, part), BF),
            pltpu.VMEM((2, 2, tokens, part), BF),
            pltpu.SemaphoreType.DMA((2, 2)),
            pltpu.SemaphoreType.DMA((6,)),
        ],
        compiler_params=params(wide_limit(gate_w, 26)),
        name="post_back",
    )(grad_state, s["update"], s["routed"], s["active"], state, s["midway"], gain, router,
      placed(attn_w), placed(gate_w), placed(up_w), placed(down_w), s["gate"], s["up"])
    names = (
        "grad_attended", "partial", "ffn_gain_grad", "router_grad", "grad_ffn", "grad_gate", "grad_up",
        "grad_branch",
    )
    return dict(zip(names, made))


def pre_back_kernel(cols, blocks, *refs):
    qc, kc = cols
    grad_queries, own, others = refs[0], refs[1], refs[2 : 1 + blocks]
    partial, state, gain, weight, cosine, sine = refs[1 + blocks : 7 + blocks]
    packed, grad_state, gain_grad, qbuf, kbuf = refs[7 + blocks :]
    summed = own[...]
    for ref in others:
        summed = summed + ref[...].astype(F32)
    kbuf[:, :KW] = summed[:, :KW]
    qbuf[:, :QW] = grad_queries[...]
    for buf in (qbuf, kbuf):
        for start in range(0, buf.shape[1], LANE):
            span = slice(start, start + LANE)
            buf[:, span] = turn(buf[:, span], cosine[...], -sine[...])
    low_q = qbuf[...].astype(BF)
    low_k = kbuf[...].astype(BF)
    low_v = summed[:, KW:].astype(BF)
    total = None
    used = packed.shape[2]
    for piece in range(weight.shape[0]):
        packed[piece] = jnp.zeros(packed.shape[1:], BF)
        packed[piece, :, :qc] = low_q[:, piece * qc : (piece + 1) * qc]
        packed[piece, :, qc : qc + kc] = low_k[:, piece * kc : (piece + 1) * kc]
        packed[piece, :, qc + kc : qc + 2 * kc] = low_v[:, piece * kc : (piece + 1) * kc]
        made = dot(packed[piece], weight[piece, :, :used], NT)
        total = made if total is None else total + made
    grad_in, grad_gain = norm_back(total, state[...], gain[...])
    gain_grad[...] = grad_gain
    grad_state[...] = partial[...] + grad_in


def pre_back(grad_queries, grad_pairs, partial, state, gain, weight, cosine, sine, cols):
    tokens, width = state.shape
    used = min(ceil_to(cols[0] + 2 * cols[1], LANE), weight.shape[2])
    return pl.pallas_call(
        functools.partial(pre_back_kernel, cols, len(grad_pairs)),
        out_shape=(
            shape((weight.shape[0], tokens, used), BF),
            shape((tokens, width), F32),
            shape((1, width), F32),
        ),
        in_specs=[vmem] * (7 + len(grad_pairs)),
        out_specs=(vmem,) * 3,
        scratch_shapes=[
            pltpu.VMEM((tokens, ceil_to(QW, LANE)), F32),
            pltpu.VMEM((tokens, ceil_to(KW, LANE)), F32),
        ],
        compiler_params=params(wide_limit(weight, 16)),
        name="pre_back",
    )(grad_queries, *grad_pairs, partial, state, gain, placed(weight), cosine, sine)


def attn_sums_kernel(count, low_col, *refs):
    normed, packed = refs[:count], refs[count : 2 * count]
    attended, branch = refs[2 * count : 3 * count], refs[3 * count : 4 * count]
    out, left, right = refs[4 * count :]

    @pl.when(pl.program_id(0) == 0)
    def _():
        left[...] = jnp.concatenate([ref[...].T for ref in normed], axis=1)
        right[...] = jnp.concatenate([ref[...].T for ref in attended], axis=1)

    first = dot(left[...], jnp.concatenate([ref[0] for ref in packed], axis=0))
    second = dot(right[...], jnp.concatenate([ref[0] for ref in branch], axis=0))
    high_col = first.shape[1]
    if low_col:
        out[0, :, :low_col] = first[:, :low_col].astype(BF)
    out[0, :, low_col:high_col] = (first[:, low_col:] + second[:, : high_col - low_col]).astype(BF)
    if high_col < out.shape[2]:
        out[0, :, high_col:] = second[:, high_col - low_col :].astype(BF)


def attn_sums(normed, packed, attended, branch, low_col, total_cols):
    count = len(normed)
    tokens, width = normed[0].shape
    pieces = packed[0].shape[0]
    row = pl.BlockSpec((tokens, width), lambda s: (0, 0))
    part = pl.BlockSpec((1, tokens, packed[0].shape[2]), lambda s: (s, 0, 0))
    thin = pl.BlockSpec((1, tokens, branch[0].shape[2]), lambda s: (s, 0, 0))
    return pl.pallas_call(
        functools.partial(attn_sums_kernel, count, low_col),
        grid=(pieces,),
        out_shape=shape((pieces, width, total_cols), BF),
        in_specs=[row] * count + [part] * count + [row] * count + [thin] * count,
        out_specs=pl.BlockSpec((1, width, total_cols), lambda s: (s, 0, 0)),
        scratch_shapes=[pltpu.VMEM((width, count * tokens), BF)] * 2,
        compiler_params=params(56),
        name="attn_sums",
    )(*normed, *packed, *attended, *branch)


def pair_sums_kernel(count, *refs):
    normed, first, second = refs[:count], refs[count : 2 * count], refs[2 * count : 3 * count]
    first_out, second_out, left = refs[3 * count :]

    @pl.when(pl.program_id(0) == 0)
    def _():
        left[...] = jnp.concatenate([ref[...].T for ref in normed], axis=1)

    for source, out in ((first, first_out), (second, second_out)):
        out[0] = dot(left[...], jnp.concatenate([ref[0] for ref in source], axis=0)).astype(BF)


def pair_sums(normed, first, second):
    count = len(normed)
    tokens, width = normed[0].shape
    pieces, _, part = first[0].shape
    row = pl.BlockSpec((tokens, width), lambda s: (0, 0))
    chunk = pl.BlockSpec((1, tokens, part), lambda s: (s, 0, 0))
    result = pl.BlockSpec((1, width, part), lambda s: (s, 0, 0))
    return pl.pallas_call(
        functools.partial(pair_sums_kernel, count),
        grid=(pieces,),
        out_shape=(shape((pieces, width, part), BF),) * 2,
        in_specs=[row] * count + [chunk] * (2 * count),
        out_specs=(result, result),
        scratch_shapes=[pltpu.VMEM((width, count * tokens), BF)],
        compiler_params=params(56),
        name="pair_sums",
    )(*normed, *first, *second)


def down_sums_kernel(count, *refs):
    hidden, grads, out, right = refs[:count], refs[count : 2 * count], refs[-2], refs[-1]

    @pl.when(pl.program_id(0) == 0)
    def _():
        for piece in range(out.shape[0]):
            right[piece] = jnp.concatenate([ref[piece] for ref in grads], axis=0)

    left = jnp.concatenate([ref[0].T for ref in hidden], axis=1)
    for piece in range(out.shape[0]):
        out[piece] = dot(left, right[piece]).astype(BF)


def down_sums(hidden, grads):
    count = len(hidden)
    pieces, tokens, part = hidden[0].shape
    cols = grads[0].shape[2]
    return pl.pallas_call(
        functools.partial(down_sums_kernel, count),
        grid=(pieces,),
        out_shape=shape((pieces, pieces * part, cols), BF),
        in_specs=[pl.BlockSpec((1, tokens, part), lambda f: (f, 0, 0))] * count
        + [pl.BlockSpec((pieces, tokens, cols), lambda f: (0, 0, 0))] * count,
        out_specs=pl.BlockSpec((pieces, part, cols), lambda f: (0, f, 0)),
        scratch_shapes=[pltpu.VMEM((pieces, count * tokens, cols), BF)],
        compiler_params=params(56),
        name="down_sums",
    )(*hidden, *grads)


MESH = pl.DeviceIdType.MESH


class Place:
    def __init__(self, layers):
        dp, seq = lax.axis_index("dp"), lax.axis_index("seq")
        self.layers = layers
        self.z, self.core = lax.div(dp, 2), lax.rem(dp, 2)
        self.y, self.x = lax.div(seq, 2), lax.rem(seq, 2)
        self.sibling = (self.z * 2 + 1 - self.core, seq)
        self.over_x = (dp, self.y * 2 + 1 - self.x)
        self.over_y = (dp, (1 - self.y) * 2 + self.x)
        self.up = [(lax.rem(self.z + k, layers) * 2 + self.core, seq) for k in range(layers)]
        self.down = [
            (lax.rem(self.z + layers - k, layers) * 2 + self.core, seq) for k in range(layers)
        ]
        self.across = (dp, 3 - seq)
        self.partner = (dp, jnp.where(self.core == 0, self.over_x[1], self.over_y[1]))
        self.place_peers = [self.over_x, self.over_y, self.across]
        self.rank_peers = self.up[1:] + [
            (lax.rem(self.z + k, layers) * 2 + 1 - self.core, seq) for k in range(layers)
        ]
        self.peers = self.place_peers + self.rank_peers

    def greet(self):
        barrier = pltpu.get_barrier_semaphore()
        for peer in self.peers:
            pl.semaphore_signal(barrier, inc=1, device_id=peer, device_id_type=MESH)
        pl.semaphore_wait(barrier, len(self.peers))


def remote(source, target, sems, peer):
    return pltpu.make_async_remote_copy(
        src_ref=source, dst_ref=target, send_sem=sems[0], recv_sem=sems[1],
        device_id=peer, device_id_type=MESH,
    )


class Pieces:
    def __init__(self, ref):
        self.ref = ref
        self.shape = (4, ref.shape[2] * ref.shape[3] * ref.shape[4], ref.shape[5])

    def __getitem__(self, index):
        piece, _, lanes = index
        whole = self.ref[piece // 2, piece % 2, :, :, :, lanes]
        return whole.reshape(self.shape[1], whole.shape[-1])


def open_kernel(layers, micros, cols, *refs):
    refs = list(refs)

    def pop(size):
        taken = refs[:size]
        del refs[:size]
        return taken

    count = 4
    ins = pop(count)
    small, own_state, other_state, cosine, sine = pop(5)
    outs = pop(count)
    gains, active = pop(2 + RECUR), pop(RECUR)
    info, state, normed, queries, pair, partner, attended, logs = pop(8)
    ranks_in, places_in, state_in, part, qbuf, kbuf, columns, own_bias, rest_bias = pop(9)
    send, recv, keep, side_send, side_recv = refs
    here = Place(layers)
    here.greet()
    y, x, z, core = here.y, here.x, here.z, here.core
    rank, place = z * 2 + core, y * 2 + x
    sent = []

    def slot(a, index):
        return send.at[a, index], recv.at[a, index]

    def start(a, index, source, target, peer):
        copy = remote(source, target, slot(a, index), peer)
        copy.start()
        sent.append(copy)

    def arrive(a, index, landing):
        remote(landing, landing, slot(a, index), here.sibling).wait_recv()

    def aside(index, source, target, peer):
        copy = remote(source, target, (side_send.at[index], side_recv.at[index]), peer)
        copy.start()
        sent.append(copy)

    def arrive_aside(index, landing):
        remote(
            landing, landing, (side_send.at[index], side_recv.at[index]), here.sibling
        ).wait_recv()

    def layer(k):
        return lax.rem(z + layers - k, layers)

    def sides(a):
        if a % 2 == 0:
            return here.over_x, here.over_y, (y, 1 - x), ((1 - y, x), (1 - y, 1 - x))
        return here.over_y, here.over_x, (1 - y, x), ((y, 1 - x), (1 - y, 1 - x))

    own = [pltpu.make_async_copy(ins[a], outs[a].at[y, x, z, core], keep.at[a]) for a in range(count)]
    for copy in own:
        copy.start()

    for index, peer in enumerate(here.rank_peers):
        aside(index, small.at[pl.ds(0, 8)], ranks_in.at[rank], peer)
    first_place = len(here.rank_peers)
    for index, peer in enumerate(here.place_peers):
        aside(first_place + index, small.at[pl.ds(8, 8)], places_in.at[place], peer)
    last = first_place + len(here.place_peers)
    ranks_in[rank] = small[0:8]
    places_in[place] = small[8:16]

    def along(arrays, k):
        for a in arrays:
            start(a, k, ins[a], outs[a].at[y, x, z, core], here.up[k])

    def first(arrays, k):
        for a in arrays:
            spot = outs[a].at[y, x, layer(k), core]
            source = ins[a] if k == 0 else spot
            if k:
                arrive(a, k, spot)
            start(a, layers + k, source, spot, sides(a + k)[0])
            start(a, 2 * layers + k, source, spot, sides(a + k)[1])

    def second(arrays, k):
        for a in arrays:
            side = sides(a + k)[2]
            spot = outs[a].at[side[0], side[1], layer(k), core]
            arrive(a, layers + k, spot)
            start(a, 3 * layers + k, spot, spot, sides(a + k)[1])

    def third(arrays, k):
        for a in arrays:
            for turn_of, side in enumerate(sides(a + k)[3]):
                arrive(a, (2 + turn_of) * layers + k, outs[a].at[side[0], side[1], layer(k), core])
            if k == 0:
                own[a].wait()
            spot = outs[a].at[:, :, layer(k), core]
            start(a, 4 * layers + k, spot, spot, here.sibling)

    def complete(arrays):
        for k in range(layers):
            for a in arrays:
                arrive(a, 4 * layers + k, outs[a].at[:, :, layer(k), 1 - core])

    works = dict(f=first, s=second, t=third)

    def compute(word):
        if word == "marks":
            unpack_marks()
        elif word == "pre":
            complete((0,))
            pre_kernel(
                cols, state, gains[0], Pieces(outs[0]), cosine, sine, normed, queries,
                pair, qbuf, kbuf,
            )
            aside(last + 1, pair, partner, here.partner)
        elif word == "own":
            own_kernel(0, queries, pair, info, part, columns, own_bias)
        else:
            arrive_aside(last + 1, partner)
            rest_kernel(0, queries, partner, info, part, attended, logs, columns, rest_bias)

    def unpack_marks():
        second_pack = jnp.where(core == 0, y == 1, x == 1)
        outer = is_outer()
        rows, block = gains[0].shape[1] // (2 * layers), state.shape[0] // 2
        for index in range(len(here.rank_peers)):
            arrive_aside(index, ranks_in.at[rank])
        for index in range(len(here.place_peers)):
            arrive_aside(first_place + index, places_in.at[place])
        for index in range(2 * layers):
            for row, ref in enumerate(gains):
                ref[:, index * rows : (index + 1) * rows] = ranks_in[index][row : row + 1, :rows]
        info[...] = jnp.zeros(info.shape, F32)
        for index, (one, two) in enumerate(zip((0, 3, 1, 2), (1, 2, 0, 3))):
            marks = places_in[jnp.where(outer, one, two)][:, :block]
            for row in range(2):
                info[row : row + 1, index * block : (index + 1) * block] = jnp.where(
                    second_pack, marks[row * micros + 1 : row * micros + 2], marks[row * micros : row * micros + 1]
                )
        columns[...] = info[...].T
        for r in range(RECUR):
            active[r][...] = jnp.broadcast_to(
                jnp.where(columns[0 : 2 * block, 1:2] > r, 1.0, 0.0), (2 * block, LANE)
            )
        arrive_aside(last, state_in)
        high = y == 1
        state[pl.ds(pl.multiple_of(jnp.where(high, block, 0), block), block)] = own_state[...]
        state[pl.ds(pl.multiple_of(jnp.where(high, 0, block), block), block)] = state_in[...].astype(F32)

    for word in PLAN:
        if len(word) > 2:
            compute(word)
            continue
        arrays = (0,) if word[0].isupper() else (1, 2, 3)
        kind = word[0].lower()
        if kind == "z":
            for k in range(1, layers) if len(word) == 1 else (int(word[1]),):
                along(arrays, k)
        elif kind == "x":
            aside(last, other_state, state_in, here.across)
        else:
            works[kind](arrays, int(word[1]))
    complete((1, 2, 3))
    for copy in sent:
        copy.wait_send()


PLAN = (
    "Z", "F0", "x", "F1", "S0", "F2", "S1", "F3", "f0", "z", "S2", "T0", "marks", "S3", "T1", "f1",
    "T2", "s0", "T3", "pre", "f2", "s1", "t0", "own", "f3", "s2", "t1", "rest", "s3", "t2", "t3",
)


def open_all(parts, small, own_state, other_state, tables, micros, cols):
    count, tokens, width = len(parts), 2 * own_state.shape[0], own_state.shape[1]
    ranks = lax.axis_size("dp")
    layers, seq = ranks // 2, 4
    wide = ceil_to(KW, LANE)
    made = pl.pallas_call(
        functools.partial(open_kernel, layers, micros, cols),
        out_shape=tuple(pltpu.VMEM((2, 2, layers, 2) + part.shape, part.dtype) for part in parts)
        + (
            *[shape((1, width), F32)] * (2 + RECUR),
            *[shape((tokens, LANE), F32)] * RECUR,
            shape((8, 2 * tokens), F32),
            shape((tokens, width), F32),
            shape((tokens, width), BF),
            shape((tokens, QW), BF),
            shape((tokens, 2 * KW), BF),
            shape((tokens, 2 * KW), BF),
            shape((tokens, QW), BF),
            shape((ceil_to(HEADS, 8), tokens), F32),
        ),
        in_specs=[vmem] + [anywhere] * (count - 1) + [vmem] * 5,
        out_specs=(vmem,) + (anywhere,) * (count - 1) + (vmem,) * (10 + 2 * RECUR),
        scratch_shapes=[
            pltpu.VMEM((ranks, 8) + small.shape[1:], F32),
            pltpu.VMEM((seq, 8) + small.shape[1:], F32),
            pltpu.VMEM(other_state.shape, BF),
            pltpu.VMEM((KV_HEADS, HEAD_DIM + 16, GROUP * tokens), F32),
            pltpu.VMEM((tokens, ceil_to(QW, LANE)), F32),
            pltpu.VMEM((tokens, wide), F32),
            pltpu.VMEM((2 * tokens, 8), F32),
            pltpu.VMEM((3, tokens // 2, tokens // 2), F32),
            pltpu.VMEM((2, tokens // 2, tokens // 2), F32),
            pltpu.SemaphoreType.DMA((count, 5 * layers)),
            pltpu.SemaphoreType.DMA((count, 5 * layers)),
            pltpu.SemaphoreType.DMA((count,)),
            pltpu.SemaphoreType.DMA((ranks + seq,)),
            pltpu.SemaphoreType.DMA((ranks + seq,)),
        ],
        compiler_params=pltpu.CompilerParams(
            collective_id=0, has_side_effects=True, vmem_limit_bytes=OPEN_LIMIT * MIB
        ),
        name="open_all",
    )(*parts, small, own_state, other_state, *tables)
    gathered, gains, actives = made[:count], made[count : count + 2 + RECUR], made[count + 2 + RECUR :]
    names = ("info", "state", "normed", "queries", "pair", "partner", "attended", "logs")
    return gathered, gains, actives[:RECUR], dict(zip(names, actives[RECUR:]))


OPEN_LIMIT = 32


SECOND_AT, THIRD_AT = 2, 2


def finish_kernel(layers, count, low_col, *refs):
    refs = list(refs)

    def pop(size):
        taken = refs[:size]
        del refs[:size]
        return taken

    normed, packed, attended, branch, ffn_in, grad_gate, grad_up, hidden, grad_ffn = (
        pop(count) for _ in range(9)
    )
    (small,) = pop(1)
    outs = pop(4)
    held, core_in, first_in, second_in, z_in = (pop(4) for _ in range(5))
    raw, left, right, ffn_right, stage, down_stage = pop(6)
    send, recv, load = refs
    here = Place(layers)
    here.greet()
    y, x, z, core = here.y, here.x, here.z, here.core
    tokens = raw.shape[0] // count

    def slot(a, index):
        return send.at[a, index], recv.at[a, index]

    def arrive(a, index, landing):
        remote(landing, landing, slot(a, index), here.sibling).wait_recv()

    def layer(k):
        return lax.rem(z + k + 1, layers)

    def added(ref, one, two):
        return (one.astype(F32) + two.astype(F32)).astype(ref.dtype)

    def load_left(index, sources):
        return [
            pltpu.make_async_copy(ref, raw.at[pl.ds(i * tokens, tokens)], load.at[index, i])
            for i, ref in enumerate(sources)
        ]

    def load_right(index, spot, sources, piece, start_col):
        width = sources[0].shape[2]
        return [
            pltpu.make_async_copy(
                ref.at[piece],
                right.at[spot, pl.ds(i * tokens, tokens), pl.ds(start_col, width)],
                load.at[index + spot, i],
            )
            for i, ref in enumerate(sources)
        ]

    def go(copies):
        for copy in copies:
            copy.start()

    def hold(copies):
        for copy in copies:
            copy.wait()

    def turn_left(spot):
        for i in range(count):
            rows = slice(i * tokens, (i + 1) * tokens)
            left[spot, :, rows] = raw[rows].T

    def column_of(piece):
        return lax.rem(1 - y + lax.div(piece, 2), 2), lax.rem(1 - x + lax.rem(piece, 2), 2)

    def spot_of(a, piece):
        if a == 3:
            return (lax.rem(z + piece + 1, layers),)
        return (slice(None),) + column_of(piece)

    def number_of(a, piece):
        if a == 3:
            return lax.rem(z + piece + 1, layers)
        row, column = column_of(piece)
        return row * 2 + column

    def staged(a, spot, whose):
        lead = (spot, slice(None), slice(None)) if a == 3 else (spot, slice(None))
        return (down_stage if a == 3 else stage), lead + (whose,)

    def handed(a, piece):
        ref, place = staged(a, lax.rem(piece, 2), 1 - core)
        return remote(
            ref.at[place], core_in[a].at[spot_of(a, piece)], (send.at[a, piece], recv.at[a, piece]),
            here.sibling,
        )

    def add_cores(a, piece):
        spot = spot_of(a, piece)
        arrive(a, piece, core_in[a].at[spot])
        ref, place = staged(a, lax.rem(piece, 2), core)
        held[a][spot] = added(held[a], ref[place], core_in[a][spot])

    def products(a, fetch, multiply, hooks):
        go(fetch(number_of(a, 0), 0))

        def step(piece, carry):
            spot = lax.rem(piece, 2)
            hold(fetch(number_of(a, piece), spot))

            @pl.when(piece < 3)
            def _():
                go(fetch(number_of(a, piece + 1), 1 - spot))

            @pl.when(piece >= 2)
            def _():
                handed(a, piece - 2).wait_send()

            multiply(number_of(a, piece), spot)
            handed(a, piece).start()

            @pl.when(piece >= 1)
            def _():
                add_cores(a, piece - 1)

            for at, hook in hooks:
                pl.when(piece == at)(hook)
            return carry

        lax.fori_loop(0, 4, step, 0)
        add_cores(a, 3)
        for piece in (2, 3):
            handed(a, piece).wait_send()

    def store(spot, result):
        rows = stage.shape[3]
        for index in range(2 * layers):
            stage[spot, index // 2, index % 2] = result[index * rows : (index + 1) * rows].astype(BF)

    def ffn_product(which):
        def multiply(piece, spot):
            width = which[0].shape[2]
            store(spot, dot(left[0], right[spot, :, :width]))

        return multiply

    high_col = packed[0].shape[2]
    far_col = branch[0].shape[2]

    def attn_product(piece, spot):
        first = dot(left[1], right[spot, :, :high_col])
        second = dot(left[0], right[spot, :, high_col : high_col + far_col])
        cut = high_col - low_col
        store(
            spot,
            jnp.concatenate(
                [first[:, :low_col], first[:, low_col:] + second[:, :cut], second[:, cut:]], axis=1
            ),
        )

    def down_product(piece, spot):
        part = hidden[0].shape[2]
        turned = jnp.concatenate(
            [right[spot, i * tokens : (i + 1) * tokens, :part].T for i in range(count)], axis=1
        )
        rows = part // 2
        cols = ffn_right.shape[2] - small.shape[3]
        for column in range(4):
            result = dot(turned, ffn_right[column]).astype(BF)
            for index in range(2):
                place = (spot, column // 2, column % 2, index)
                down_stage[place] = result[index * rows : (index + 1) * rows]
                down_stage[place + (slice(None), slice(cols, None))] = small[piece, index]

    def over(a, k):
        index = 4 + k
        if k % 2 == 0:
            source, peer = held[a].at[layer(k), :, 1 - x], here.over_x
        else:
            source, peer = held[a].at[layer(k), 1 - y], here.over_y
        return remote(source, first_in[a].at[k], slot(a, index), peer)

    def first_odd(a):
        for k in range(1, layers, 2):
            over(a, k).start()

    def first_even(a):
        for k in range(0, layers, 2):
            over(a, k).start()

    order = [*range(1, layers, 2), *range(0, layers, 2)]

    def second(a):
        for k in order:
            second_layer(a, k)

    def second_layer(a, k):
        at = layer(k)
        arrive(a, 4 + k, first_in[a].at[k])
        for i in range(2):
            if k % 2 == 0:
                held[a][at, i, x] = added(held[a], held[a][at, i, x], first_in[a][k, i])
            else:
                held[a][at, y, i] = added(held[a], held[a][at, y, i], first_in[a][k, i])
        across(a, k).start()

    def across(a, k):
        if k % 2 == 0:
            source, peer = held[a].at[layer(k), 1 - y, x], here.over_y
        else:
            source, peer = held[a].at[layer(k), y, 1 - x], here.over_x
        return remote(source, second_in[a].at[k], slot(a, 4 + layers + k), peer)

    def along(a, k):
        source = held[a].at[layer(k), y, x]
        return remote(source, z_in[a].at[k], slot(a, 4 + 2 * layers + k), here.up[k + 1])

    def third(a):
        for k in order:
            third_layer(a, k)

    def third_layer(a, k):
        arrive(a, 4 + layers + k, second_in[a].at[k])
        spot = (layer(k), y, x)
        held[a][spot] = added(held[a], held[a][spot], second_in[a][k])
        if k < layers - 1:
            along(a, k).start()

    def fourth(a):
        total = held[a][z, y, x].astype(F32)
        for k in range(layers - 1):
            arrive(a, 4 + 2 * layers + k, z_in[a].at[k])
            total = total + z_in[a][k].astype(F32)
        outs[a][...] = total

    ffn_left = load_left(0, ffn_in)
    go(ffn_left)
    down_right = [
        pltpu.make_async_copy(
            ref.at[column],
            ffn_right.at[column, pl.ds(i * tokens, tokens)],
            load.at[6 + column, i],
        )
        for i, ref in enumerate(grad_ffn)
        for column in range(4)
    ]

    def fetch_of(index, sources):
        return lambda piece, spot: load_right(index, spot, sources, piece, 0)

    def fetch_attn(piece, spot):
        return load_right(2, spot, packed, piece, 0) + load_right(4, spot, branch, piece, high_col)

    hold(ffn_left)
    turn_left(0)
    normed_left = load_left(1, normed)
    go(normed_left)
    go(down_right)

    def columns_out(a):
        return [(2, lambda: first_odd(a)), (3, lambda: first_even(a))]

    products(0, fetch_of(2, grad_gate), ffn_product(grad_gate), columns_out(0))
    hold(normed_left)
    turn_left(1)
    attended_left = load_left(0, attended)
    go(attended_left)
    products(
        1, fetch_of(2, grad_up), ffn_product(grad_up), [(SECOND_AT, lambda: second(0))] + columns_out(1)
    )
    hold(attended_left)
    turn_left(0)
    products(
        2, fetch_attn, attn_product,
        [(SECOND_AT, lambda: second(1)), (THIRD_AT, lambda: third(0))] + columns_out(2),
    )
    hold(down_right)
    layers_out = [(k + 1, lambda k=k: over(3, k).start()) for k in range(layers - 1)]
    products(
        3, fetch_of(2, hidden), down_product,
        [(SECOND_AT, lambda: second(2)), (THIRD_AT, lambda: third(1))] + layers_out,
    )
    over(3, layers - 1).start()
    third(2)
    second_layer(3, 0)
    second_layer(3, 1)
    third_layer(3, 0)
    second_layer(3, 2)
    third_layer(3, 1)
    second_layer(3, 3)
    third_layer(3, 2)
    third_layer(3, 3)
    for a in range(4):
        fourth(a)
    for a in range(4):
        for k in range(layers):
            over(a, k).wait_send()
            across(a, k).wait_send()
            if k < layers - 1:
                along(a, k).wait_send()


def finish(normed, packed, attended, branch, ffn_in, grad_gate, grad_up, hidden, grad_ffn, small, low_col):
    count = len(normed)
    tokens, width = normed[0].shape
    pieces, _, part = hidden[0].shape
    cols = grad_ffn[0].shape[2]
    layers = small.shape[0]
    ranks = 2 * layers
    rows, down_rows = width // ranks, pieces * part // ranks
    wide = packed[0].shape[2] + branch[0].shape[2]
    ends = [(rows, part), (rows, part), (rows, part), (down_rows, cols)]

    def buffers(*lead):
        return [pltpu.VMEM(lead + end, BF) for end in ends]

    operands = (
        *normed, *packed, *attended, *branch, *ffn_in, *grad_gate, *grad_up, *hidden, *grad_ffn, small,
    )
    return pl.pallas_call(
        functools.partial(finish_kernel, layers, count, low_col),
        out_shape=tuple(shape(end, F32) for end in ends),
        in_specs=[anywhere] * (len(operands) - 1) + [vmem],
        out_specs=(vmem,) * 4,
        scratch_shapes=[
            *buffers(layers, 2, 2),
            *buffers(layers, 2, 2),
            *buffers(layers, 2),
            *buffers(layers),
            *buffers(layers - 1),
            pltpu.VMEM((count * tokens, width), BF),
            pltpu.VMEM((2, width, count * tokens), BF),
            pltpu.VMEM((2, count * tokens, max(wide, part)), BF),
            pltpu.VMEM((pieces, count * tokens, cols), BF),
            pltpu.VMEM((2, layers, 2, rows, part), BF),
            pltpu.VMEM((2, 2, 2, 2, down_rows, cols), BF),
            pltpu.SemaphoreType.DMA((4, 4 + 3 * layers)),
            pltpu.SemaphoreType.DMA((4, 4 + 3 * layers)),
            pltpu.SemaphoreType.DMA((10, count)),
        ],
        compiler_params=pltpu.CompilerParams(
            collective_id=1, has_side_effects=True, vmem_limit_bytes=61 * MIB
        ),
        name="finish",
    )(*operands)


def rope_tables(positions):
    half = HEAD_DIM // 2
    frequency = rope_base ** (-(jnp.arange(half, dtype=F32) * 2.0 / HEAD_DIM))
    angles = positions.astype(F32)[:, None] * frequency[None, :]
    cosine, sine = jnp.cos(angles), jnp.sin(angles)
    repeat = LANE // HEAD_DIM
    return (
        jnp.concatenate([cosine, cosine] * repeat, axis=1),
        jnp.concatenate([-sine, sine] * repeat, axis=1),
    )


def pass_on(array, step, count):
    return lax.ppermute(array, "seq", [(i, i + step) for i in range(count - step)])


def pass_back(array, step, count):
    return lax.ppermute(array, "seq", [(i + step, i) for i in range(count - step)])


def row_plan(inputs, cotangent, depths, marks, block_params):
    micros, _, tokens, _ = inputs.shape
    seq, mine = lax.axis_size("seq"), lax.axis_index("seq")
    attn_g, ffn_g, routers, attn_w, gate_w, up_w, down_w, cols, used = block_params
    order = mine - jnp.arange(seq)
    marks = jnp.where((order >= 0)[:, None, None, None], marks[order % seq], -1.0)
    marks = marks.transpose(2, 1, 0, 3).reshape(micros, 2, seq * tokens)
    infos = [jnp.pad(marks[m], ((0, 6), (0, 0))) for m in range(micros)]
    cosine, sine = rope_tables(mine * tokens + jnp.arange(tokens, dtype=jnp.int32))
    states = [inputs[m, 0] for m in range(micros)]
    actives = [
        [
            jnp.broadcast_to((depths[m, 0] > r).astype(F32)[:, None], (tokens, LANE))
            for r in range(RECUR)
        ]
        for m in range(micros)
    ]
    saved = [[None] * RECUR for _ in range(micros)]
    for r in range(RECUR):
        made = []
        for m in range(micros):
            normed, queries, pair = pre_part(states[m], attn_g, attn_w, cosine, sine, cols)
            pairs = [pair] + [pass_on(pair, step, seq) for step in range(1, seq)]
            made.append((normed, queries, pairs))
        for m in range(micros):
            normed, queries, pairs = made[m]
            attended, logs = attend(queries, pairs, infos[m], r)
            after = post_part(
                states[m], attended, attn_w, ffn_g, routers[r], actives[m][r], gate_w, up_w, down_w, used
            )
            saved[m][r] = dict(
                after, state=states[m], normed=normed, queries=queries, pairs=pairs,
                attended=attended, logs=logs, active=actives[m][r],
            )
            states[m] = after["state_out"]
    grads = [cotangent[m, 0] for m in range(micros)]
    for r in reversed(range(RECUR)):
        partials = []
        for m in range(micros):
            s = saved[m][r]
            s.update(post_back(grads[m], s, ffn_g, routers[r], attn_w, gate_w, up_w, down_w, used))
            grad_queries, *grad_pairs = attend_back(
                s["queries"], s["pairs"], infos[m], s["attended"], s["logs"], s["grad_attended"], r
            )
            grad_pairs = [grad_pairs[0]] + [
                pass_back(grad_pairs[step], step, seq) for step in range(1, seq)
            ]
            partials.append((grad_queries, grad_pairs))
        for m in range(micros):
            s = saved[m][r]
            s["packed"], grads[m], s["attn_gain_grad"] = pre_back(
                *partials[m], s["partial"], s["state"], attn_g, attn_w, cosine, sine, cols
            )
    outputs = jnp.stack(states, axis=0)[:, None]
    input_grad = jnp.stack(grads, axis=0)[:, None]
    return outputs, input_grad, saved


def swap(array, pairs):
    seq, ranks = lax.axis_size("seq"), lax.axis_size("dp")
    moves = []
    for rank in range(ranks):
        for one, two in pairs[rank % 2]:
            moves += [(rank * seq + one, rank * seq + two), (rank * seq + two, rank * seq + one)]
    return lax.ppermute(array, ("dp", "seq"), moves)


ACROSS = (((0, 3), (1, 2)),) * 2
PARTNERS = (((0, 1), (2, 3)), ((0, 2), (1, 3)))


def second_micro():
    place = lax.axis_index("seq")
    return jnp.where(lax.axis_index("dp") % 2 == 0, place >= 2, place % 2 == 1)


def paired_start(inputs, cotangent):
    tokens = inputs.shape[2]
    second = second_micro()
    outer = is_outer()

    def split(array):
        own = jnp.where(second, array[1, 0], array[0, 0])
        return own, jnp.where(second, array[0, 0], array[1, 0]).astype(BF)

    places = jnp.arange(tokens, dtype=jnp.int32)
    low, high = jnp.where(outer, 0, 1), jnp.where(outer, 3, 2)
    tables = rope_tables(jnp.concatenate([low * tokens + places, high * tokens + places]))
    return split(inputs), split(cotangent), tables


def paired_plan(opened, actives, grads, tables, block_params):
    (own_grad, other_grad), (cosine, sine) = grads, tables
    info, state = opened["info"], opened["state"]
    tokens = own_grad.shape[0]
    late = lax.axis_index("seq") >= 2
    attn_g, ffn_g, routers, attn_w, gate_w, up_w, down_w, cols, used = block_params

    def join(own, other):
        other = other.astype(F32)
        return jnp.concatenate([jnp.where(late, other, own), jnp.where(late, own, other)], axis=0)

    def give(array):
        low, high = array[:tokens], array[tokens:]
        own = jnp.where(late, high, low)
        other = swap(jnp.where(late, low, high).astype(BF), ACROSS).astype(F32)
        second = second_micro()
        return jnp.stack([jnp.where(second, other, own), jnp.where(second, own, other)], axis=0)[:, None]

    saved = []
    for r in range(RECUR):
        active = actives[r]
        if r == 0:
            normed, queries, pair, partner, attended, logs = (
                opened[name]
                for name in ("normed", "queries", "pair", "partner", "attended", "logs")
            )
        else:
            normed, queries, pair = pre_part(state, attn_g, attn_w, cosine, sine, cols)
            partner = swap(pair, PARTNERS)
            part = attend_own(queries, pair, info, r)
            attended, logs = attend_rest(queries, partner, info, part, r)
            if r == 1:
                other_grad, attended = lax.optimization_barrier((other_grad, attended))
                other_grad = swap(other_grad, ACROSS)
        after = post_part(
            state, attended, attn_w, ffn_g, routers[r], active, gate_w, up_w, down_w, used
        )
        saved.append(
            dict(
                after, state=state, normed=normed, queries=queries, pair=pair, partner=partner,
                attended=attended, logs=logs, active=active,
            )
        )
        state = after["state_out"]
    outputs = give(state)
    grad = join(own_grad, other_grad)
    for r in reversed(range(RECUR)):
        s = saved[r]
        s.update(post_back(grad, s, ffn_g, routers[r], attn_w, gate_w, up_w, down_w, used))
        grad_partner, part, deltas = attend_rest_back(
            s["queries"], s["partner"], info, s["attended"], s["logs"], s["grad_attended"], r
        )
        grad_partner = swap(grad_partner, PARTNERS)
        grad_queries, grad_pair = attend_own_back(
            s["queries"], s["pair"], info, s["logs"], deltas, s["grad_attended"], part, r
        )
        s["packed"], grad, s["attn_gain_grad"] = pre_back(
            grad_queries, [grad_pair, grad_partner], s["partial"], s["state"], attn_g, attn_w,
            cosine, sine, cols,
        )
    return outputs, give(grad), [saved]


def local(
    inputs, cotangent, segments, depths, query_weight, key_weight, value_weight, out_weight,
    gate_weight, up_weight, down_weight, attn_gain, ffn_gain, router_weight,
):
    micros, _, tokens, width = inputs.shape
    seq, ranks = lax.axis_size("seq"), lax.axis_size("dp")
    rows = query_weight.shape[0]
    qc, kc = query_weight.shape[1], key_weight.shape[1]
    both = ("seq", "dp")

    attn_local = jnp.concatenate([query_weight, key_weight, value_weight, out_weight], axis=1)
    down_cols = down_weight.shape[1]
    span = ceil_to(max(rows, tokens), LANE)
    small = jnp.concatenate([attn_gain[None], ffn_gain[None], router_weight.T], axis=0).astype(F32)
    marks = jnp.concatenate([segments[:, 0], depths[:, 0]], axis=0).astype(F32)
    small = jnp.concatenate(
        [
            jnp.pad(small, ((0, 8 - small.shape[0]), (0, span - rows))),
            jnp.pad(marks, ((0, 8 - 2 * micros), (0, span - tokens))),
        ],
        axis=0,
    )
    parts = (
        attn_local, gate_weight, up_weight, jnp.pad(down_weight, ((0, 0), (0, BESIDE)))
    )
    direct = micros == 2 and (seq, ranks) == (4, 8)
    if direct:
        states, grads, tables = paired_start(inputs, cotangent)
        parts, small, states, grads, tables = lax.optimization_barrier(
            (parts, small, states, grads, tables)
        )
        gathered, gains, actives, opened = open_all(
            parts, small, *states, tables, micros, (qc, kc)
        )
    else:
        gathered = [lax.all_gather(part, both, axis=0, tiled=False) for part in parts]
        small = lax.all_gather(small, both, axis=0, tiled=False)
        small = small.reshape(seq, ranks, *small.shape[1:])
        marks = lax.dynamic_index_in_dim(small, lax.axis_index("dp"), 1, keepdims=False)
        marks = marks[:, 8 : 8 + 2 * micros, :tokens].reshape(seq, 2, micros, tokens)
        small = small[0, :, : 2 + RECUR, :rows].transpose(1, 0, 2).reshape(2 + RECUR, width)
        gains = [small[row : row + 1] for row in range(2 + RECUR)]
    attn_w, gate_w, up_w, down_w = (full.reshape(seq, -1, full.shape[-1]) for full in gathered)
    attn_g, ffn_g, *routers = gains
    used = qc + 2 * kc
    total_cols = attn_w.shape[2]
    low_col = used // LANE * LANE
    block_params = (attn_g, ffn_g, routers, attn_w, gate_w, up_w, down_w, (qc, kc), used)
    if direct:
        outputs, input_grad, saved = paired_plan(opened, actives, grads, tables, block_params)
    else:
        outputs, input_grad, saved = row_plan(inputs, cotangent, depths, marks, block_params)
    flat = [steps[r] for r in reversed(range(RECUR)) for steps in saved]

    def every(name):
        return [s[name] for s in flat]

    attn_gain_sum, ffn_gain_sum = sum(every("attn_gain_grad")), sum(every("ffn_gain_grad"))
    router_sums = [sum(steps[r]["router_grad"] for steps in saved) for r in range(RECUR)]
    small_sum = jnp.concatenate([attn_gain_sum, ffn_gain_sum, *router_sums], axis=0)
    small_sum = small_sum.T.reshape(ranks, rows, 2 + RECUR)
    if direct:
        small_sum = jnp.pad(
            small_sum, ((0, 0), (0, down_weight.shape[0] - rows), (0, BESIDE - 2 - RECUR))
        ).astype(BF)
        gate_grad, up_grad, attn_grad, down_grad = finish(
            every("normed"), every("packed"), every("attended"), every("grad_branch"),
            every("ffn_in"), every("grad_gate"), every("grad_up"), every("hidden"),
            every("grad_ffn"), small_sum.reshape(ranks // 2, 2, -1, BESIDE), low_col,
        )
        small_own = down_grad[:rows, down_cols : down_cols + 2 + RECUR].T
    else:
        down_sum = down_sums(every("hidden"), every("grad_ffn"))
        gate_sum, up_sum = pair_sums(every("ffn_in"), every("grad_gate"), every("grad_up"))
        attn_sum = attn_sums(
            every("normed"), every("packed"), every("attended"), every("grad_branch"),
            low_col, total_cols,
        )
        small_sum = jnp.broadcast_to(small_sum[None], (seq,) + small_sum.shape)
        sums = [
            part.reshape(seq, ranks, -1, part.shape[-1])
            for part in (gate_sum, up_sum, attn_sum, down_sum, small_sum)
        ]
        sums = [lax.psum_scatter(part, "seq", scatter_dimension=0) for part in sums]
        sums = [lax.psum_scatter(part, "dp", scatter_dimension=0).astype(F32) for part in sums]
        gate_grad, up_grad, attn_grad, down_grad, small_own = sums
        small_own = small_own.T
    down_grad = down_grad[:, :down_cols]

    return (
        outputs,
        input_grad,
        attn_grad[:, :qc],
        attn_grad[:, qc : qc + kc],
        attn_grad[:, qc + kc : used],
        attn_grad[:, used:],
        gate_grad,
        up_grad,
        down_grad,
        small_own[0],
        small_own[1],
        small_own[2:].T,
    )


def solution(mesh):
    data = P(None, "dp", "seq", None)
    marks = P(None, "dp", "seq")
    weight = P("dp", "seq")
    in_specs = (data, data, marks, marks) + (weight,) * 7 + (P("dp"), P("dp"), P("dp", None))
    out_specs = (data, data) + (weight,) * 7 + (P("dp"), P("dp"), P("dp", None))
    return jax.shard_map(local, mesh=mesh, in_specs=in_specs, out_specs=out_specs, check_vma=False)
```
